128 devices in a mesh: pp: 4 (over y), ep: 32 (over x, z, core).
Axes of the slice: x: 4, y: 4, z: 4, core: 2. Of those that a mesh axis runs over, the one named last changes fastest.
Arguments:
- tokens_a: bfloat16 [2048, 7168], P('ep'), may hold values from -51 to 51
- tokens_b: bfloat16 [2048, 7168], P('ep'), may hold values from -51 to 51
- routes_a: int32 [4, 2048, 2], P('pp', 'ep'), may hold values from 0 to 15, all different within a row; in each aligned block of 64 rows (0 to 63, 64 to 127, ..., all dimensions but the last counted through in order) at most 10 rows name the same one
- routes_b: int32 [4, 2048, 2], P('pp', 'ep'), may hold values from 0 to 15, all different within a row; in each aligned block of 64 rows (0 to 63, 64 to 127, ..., all dimensions but the last counted through in order) at most 10 rows name the same one
- affinity_a: float32 [4, 2048, 2], P('pp', 'ep'), may hold values from 0.2 to 1
- affinity_b: float32 [4, 2048, 2], P('pp', 'ep'), may hold values from 0.2 to 1
- gate_w: bfloat16 [4, 7168, 16384], P('pp', None, 'ep'), may hold values from -0.0625 to 0.0625
- up_w: bfloat16 [4, 7168, 16384], P('pp', None, 'ep'), may hold values from -0.0625 to 0.0625
- down_w: bfloat16 [4, 16384, 7168], P('pp', 'ep'), may hold values from -0.1875 to 0.1875
Outputs:
- states_a: bfloat16 [4, 2048, 7168], P('pp', 'ep')
- states_b: bfloat16 [4, 2048, 7168], P('pp', 'ep')
The draws below stay inside these ranges and needn't reach their ends.
Inputs may be any that keep to these rules, and one draw needn't show every extreme that they name: `routes_a`: in every aligned block of 64 rows of one layer no expert is named more than 10 times, and the 2 experts of a token differ. `routes_b`: as routes_a.
All inputs are finite; a program needn't handle non-finite values.
Results may differ from the reference program's by a relative error of at most 0.013.
Values may be sent and summed in bfloat16 or wider, within the bound.
No kernel may reach another device: no remote copies, remote signals or barrier semaphores. Data moves between devices by JAX's collectives and lax.ppermute only.
A program may use at most 128 MiB of HBM per device.

```python
import math
import jax
import jax.numpy as jnp
import numpy as np
from jax import lax

D = 7168
FFW = 1024
TOPK = 2
TOK_DEV = 64
EXPERTS = 16
CAP = 10
TOKENS = 2048
N_PP = 4
N_EP = 32


def scaled_field(baseline, scale_key):
    column_key, row_key = jax.random.split(scale_key)
    column_scale = jnp.exp(jax.random.uniform(column_key, (1, D), jnp.float32, -1.15, 1.15))
    row_scale = jnp.exp(jax.random.uniform(row_key, (TOKENS, 1), jnp.float32, -1.15, 1.15))
    return (jnp.clip(baseline, -5.0, 5.0) * column_scale * row_scale).astype(jnp.bfloat16)


def draw_tokens_a(key, part):
    key = jax.random.fold_in(key, 11)
    first_key, scale_key = jax.random.split(key, 2)
    baseline = jax.random.normal(first_key, (TOKENS, D), jnp.float32)
    return scaled_field(baseline, scale_key)


def draw_tokens_b(key, part):
    key = jax.random.fold_in(key, 23)
    first_key, scale_key = jax.random.split(key, 2)
    baseline = jax.random.normal(first_key, (TOKENS, D), jnp.float32)
    return scaled_field(baseline, scale_key)


def steps_of(own_key, shape, cuts, smallest, top_value):
    loudness, own = 1.0, jax.random.fold_in(own_key, 6)
    for axis_at, shards_of in cuts:
        heights = jnp.exp(jax.random.uniform(jax.random.fold_in(own, axis_at), (shards_of,), jnp.float32, smallest / len(cuts), top_value / len(cuts)))
        loudness = loudness * jnp.repeat(heights, shape[axis_at] // shards_of).reshape([-1 if axis == axis_at else 1 for axis in range(len(shape))])
    return loudness


def shared_out(own_key, own, number, rows, number_of, top, bound, slope):
    order = jax.random.permutation(own_key, number_of)
    heavy_load, common = portions_of(number_of, rows * top, bound, slope, True), portions_of(number_of, rows * top, bound, slope, False)
    places = jnp.arange(number_of)

    def named(sizes, rotation):
        used = int((sizes > 0).sum())
        fixed = max(1, used // 4)
        moved = fixed + (places - fixed + rotation * (used - fixed)) % max(1, number_of - fixed)
        return jnp.zeros((number_of,), jnp.int32).at[order[jnp.where(places < fixed, places, moved)]].set(jnp.asarray(sizes, jnp.int32))

    sizes = jnp.where(number % 4 == 0, named(heavy_load, number // 4), named(common, number - number // 4 - 1))
    mixed = jax.random.permutation(jax.random.fold_in(own, 3), number_of)
    donor, receiver = mixed[0:number_of // 2 * 2:2], mixed[1:number_of // 2 * 2:2]
    slack = jnp.minimum(sizes[donor] - 1, bound - sizes[receiver]) // 2
    slack = jnp.where((donor == order[0]) | (receiver == order[0]) | (sizes[receiver] == 0), 0, jnp.maximum(slack, 0))
    moved = jax.random.randint(jax.random.fold_in(own, 4), (number_of // 2,), 0, 1 << 20) % (slack + 1)
    sizes = sizes.at[donor].add(-moved).at[receiver].add(moved)
    members = jnp.searchsorted(jnp.cumsum(sizes), jnp.arange(rows * top), side="right").astype(jnp.int32)
    listing = members.reshape(top, rows).T
    listing = listing[jax.random.permutation(jax.random.fold_in(own, 1), rows)]
    rotation = jax.random.randint(jax.random.fold_in(own, 2), (rows, 1), 0, top)
    return jnp.take_along_axis(listing, (jnp.arange(top)[None, :] + rotation) % top, axis=1)


def portions_of(count, total, reach, skew, full):
    weights = [(1 << 20) // math.isqrt(grade ** skew) + 1 for grade in range(1, count + 1)]
    largest = reach if full else min(reach, max(-(-total // count), total * weights[0] // sum(weights)))
    least = 1 if total - largest >= count - 1 else 0
    counts, surplus = [largest] + [least] * (count - 1), total - largest - least * (count - 1)
    while surplus > 0:
        free = [i for i in range(1, count) if counts[i] < largest] or [i for i in range(1, count) if counts[i] < reach]
        mass, left = sum([weights[i] for i in free]), surplus
        for i in free:
            more = min(reach - counts[i], max(1, left * weights[i] // mass), surplus)
            counts[i] = counts[i] + more
            surplus = surplus - more
    return np.array(counts)


def scatter_about(own_key, dims, width, bound, cuts=(), kind=jnp.bfloat16):
    drawn = width * jax.random.normal(own_key, dims, jnp.float32)
    if cuts:
        drawn = drawn * steps_of(own_key, dims, cuts, -0.22, 0.18)
    return jnp.clip(drawn, -bound, bound).astype(kind)


def setup_inputs(seed: int = 0) -> dict:
    seeds = jax.random.split(jax.random.key(seed), 10)
    tokens_a = draw_tokens_a(jax.random.fold_in(seeds[9], 71), 0)
    tokens_b = draw_tokens_b(jax.random.fold_in(seeds[9], 71), 0)
    routes_a_keys = jax.random.split(jax.random.fold_in(seeds[2], 1), N_PP * TOKENS // TOK_DEV)
    routes_a_turns = jax.random.permutation(jax.random.fold_in(seeds[2], 3), N_PP * TOKENS // TOK_DEV)
    routes_a = jax.vmap(lambda own, number: shared_out(jax.random.fold_in(seeds[2], 2), own, number, TOK_DEV, EXPERTS, TOPK, CAP, 2))(routes_a_keys, routes_a_turns).reshape((N_PP, TOKENS, TOPK))
    routes_b_keys = jax.random.split(jax.random.fold_in(seeds[3], 1), N_PP * TOKENS // TOK_DEV)
    routes_b_turns = jax.random.permutation(jax.random.fold_in(seeds[3], 3), N_PP * TOKENS // TOK_DEV)
    routes_b = jax.vmap(lambda own, number: shared_out(jax.random.fold_in(seeds[3], 2), own, number, TOK_DEV, EXPERTS, TOPK, CAP, 2))(routes_b_keys, routes_b_turns).reshape((N_PP, TOKENS, TOPK))
    affinity_a = jnp.clip(jnp.exp(math.log(1.0) - 1.609438 * jax.random.uniform(seeds[4], (N_PP, TOKENS, TOPK), jnp.float32) ** steps_of(seeds[4], (N_PP, TOKENS, TOPK), ((0, 4), (1, 32)), -0.2, 0.2)), 0.2, 1.0)
    affinity_b = jnp.clip(jnp.exp(math.log(1.0) - 1.609438 * jax.random.uniform(seeds[5], (N_PP, TOKENS, TOPK), jnp.float32) ** steps_of(seeds[5], (N_PP, TOKENS, TOPK), ((0, 4), (1, 32)), -0.2, 0.2)), 0.2, 1.0)
    gate_w = scatter_about(seeds[6], (N_PP, D, EXPERTS * FFW), D ** -0.5, 0.0625, ((0, 4), (2, 32)))
    up_w = scatter_about(seeds[7], (N_PP, D, EXPERTS * FFW), D ** -0.5, 0.0625, ((0, 4), (2, 32)))
    down_w = scatter_about(seeds[8], (N_PP, EXPERTS * FFW, D), FFW ** -0.5, 0.1875, ((0, 4), (1, 32)))
    return {"tokens_a": tokens_a, "tokens_b": tokens_b, "routes_a": routes_a, "routes_b": routes_b, "affinity_a": affinity_a, "affinity_b": affinity_b, "gate_w": gate_w, "up_w": up_w, "down_w": down_w}


def normalize(activations):
    values = activations.astype(jnp.float32)
    scale = lax.rsqrt(lax.optimization_barrier(jnp.mean(values * values, axis=-1, keepdims=True)) + 1e-06)
    return (values * scale).astype(jnp.bfloat16)

def slot_index(block_routes):
    flattened = block_routes.reshape(-1)
    onehot = (flattened[:, None] == jnp.arange(EXPERTS, dtype=jnp.int32)[None, :]).astype(jnp.int32)
    before = jnp.cumsum(onehot, axis=0) - onehot
    position = lax.optimization_barrier(jnp.sum(before * onehot, axis=1))
    return (flattened * CAP + position).astype(jnp.int32)

def moe_layer(activations, gate_section, up_section, down_section, routes, affinity):
    half_width = FFW // 2
    normed = normalize(activations)
    block_rows = normed.reshape(N_EP, TOK_DEV, D)
    targets = jax.vmap(slot_index)(routes.reshape(N_EP, TOK_DEV, TOPK))

    def fill(target, rows_block):
        select = (jnp.arange(EXPERTS * CAP, dtype=jnp.int32)[:, None] == target[None, :]).astype(jnp.float32)
        repeated = jnp.repeat(rows_block, TOPK, axis=0).astype(jnp.float32)
        return jnp.dot(select, repeated, precision=lax.Precision.HIGHEST).astype(jnp.bfloat16)
    buffers = jax.vmap(fill)(targets, block_rows)
    by_expert = buffers.reshape(N_EP, EXPERTS, CAP, D).transpose(1, 0, 2, 3).reshape(EXPERTS, N_EP * CAP, D)

    def expert(inputs):
        row_matrix, expert_index = inputs
        start = (expert_index * FFW).astype(jnp.int32)
        gate_cols = lax.dynamic_slice_in_dim(gate_section, start, FFW, 1).astype(jnp.float32)
        up_cols = lax.dynamic_slice_in_dim(up_section, start, FFW, 1).astype(jnp.float32)
        down_rows = lax.dynamic_slice_in_dim(down_section, start, FFW, 0).astype(jnp.float32)
        values = row_matrix.astype(jnp.float32)
        gate_act = jnp.dot(values, gate_cols, precision=lax.Precision.HIGHEST)
        up_act = jnp.dot(values, up_cols, precision=lax.Precision.HIGHEST)
        pieces = []
        for half in range(2):
            lower = half * half_width
            hidden = (jax.nn.silu(gate_act[:, lower:lower + half_width]) * up_act[:, lower:lower + half_width]).astype(jnp.bfloat16)
            piece = jnp.dot(hidden.astype(jnp.float32), down_rows[lower:lower + half_width], precision=lax.Precision.HIGHEST)
            pieces.append(piece.astype(jnp.bfloat16))
        return jnp.stack(pieces)
    parts = lax.map(expert, (by_expert, jnp.arange(EXPERTS, dtype=jnp.int32)))
    combined = (parts[:, 0].astype(jnp.float32) + parts[:, 1].astype(jnp.float32)).astype(jnp.bfloat16).astype(jnp.float32)
    combined = combined.reshape(EXPERTS, N_EP, CAP, D).transpose(1, 0, 2, 3).reshape(N_EP, EXPERTS * CAP, D)
    picked = jax.vmap(lambda table, target: jnp.take(table, target, axis=0))(combined, targets)
    picked = picked.reshape(TOKENS, TOPK, D)
    updated = activations.astype(jnp.float32) + lax.optimization_barrier(jnp.sum(affinity[:, :, None] * picked, axis=1))
    return updated.astype(jnp.bfloat16)

def reference(tokens_a, tokens_b, routes_a, routes_b, affinity_a, affinity_b, gate_w, up_w, down_w):
    forward_states = []
    current = tokens_a
    for section_number in range(N_PP):
        current = moe_layer(current, gate_w[section_number], up_w[section_number], down_w[section_number], routes_a[section_number], affinity_a[section_number])
        forward_states.append(current)
    reverse_states = [None] * N_PP
    current = tokens_b
    for section_number in reversed(range(N_PP)):
        current = moe_layer(current, gate_w[section_number], up_w[section_number], down_w[section_number], routes_b[section_number], affinity_b[section_number])
        reverse_states[section_number] = current
    return (jnp.stack(forward_states), jnp.stack(reverse_states))
```

```python
import functools

import jax
import jax.numpy as jnp
import numpy as np
from jax import lax
from jax.experimental import pallas as pl
from jax.experimental.pallas import tpu as pltpu
from jax.sharding import PartitionSpec as P

MIB = 1 << 20
PIECES = 4
GROUP = 8


def vmem():
    return pl.BlockSpec(memory_space=pltpu.VMEM)


def params(mib):
    return pltpu.CompilerParams(vmem_limit_bytes=mib * MIB)


def row_codes(experts, capacity):
    expert, piece, slot = np.meshgrid(
        np.arange(experts), np.arange(PIECES), np.arange(capacity), indexing="ij"
    )
    return (piece * experts * capacity + expert * capacity + slot).reshape(-1).astype(np.int32)


def group_permutation(capacity):
    rows = GROUP * PIECES * capacity
    result = np.zeros((rows, rows), np.float32)
    for piece in range(PIECES):
        for chip in range(GROUP):
            for slot in range(capacity):
                to = (piece * GROUP + chip) * capacity + slot
                result[to, (chip * PIECES + piece) * capacity + slot] = 1
    return result


def dispatch_kernel(x_ref, code_ref, row_ref, out_ref, stacked):
    tokens, width = x_ref.shape
    part = width // PIECES
    values = x_ref[...].astype(jnp.float32)
    scale = lax.rsqrt(jnp.mean(values * values, axis=-1, keepdims=True) + 1e-06)
    for piece in range(PIECES):
        columns = slice(piece * part, (piece + 1) * part)
        stacked[piece * tokens : (piece + 1) * tokens, :] = (
            x_ref[:, columns].astype(jnp.float32) * scale
        ).astype(jnp.bfloat16)
    rows = row_ref[...]
    hit = (rows == code_ref[0:1, :]) | (rows == code_ref[1:2, :])
    select = jnp.where(hit, 1.0, 0.0).astype(jnp.bfloat16)
    for start in range(0, part, 256):
        columns = slice(start, start + 256)
        out_ref[:, columns] = jnp.dot(
            select, stacked[:, columns], preferred_element_type=jnp.float32
        ).astype(jnp.bfloat16)


def dispatch(x, code, rows):
    tokens, width = x.shape
    wire, part = rows.shape[0], width // PIECES
    return pl.pallas_call(
        dispatch_kernel,
        out_shape=jax.ShapeDtypeStruct((wire, part), jnp.bfloat16),
        in_specs=[vmem()] * 3,
        out_specs=vmem(),
        scratch_shapes=[pltpu.VMEM((PIECES * tokens, part), jnp.bfloat16)],
        compiler_params=params(24),
        cost_estimate=pl.CostEstimate(
            flops=2 * wire * PIECES * tokens * part, bytes_accessed=4 * MIB, transcendentals=0
        ),
        name="dispatch",
    )(x, code, rows)


def hidden_kernel(wire_ref, perm_ref, gate_ref, up_ref, out_ref, rows, gate_sum, up_sum):
    piece = pl.program_id(0)
    height = perm_ref.shape[0]
    span = wire_ref.shape[0] // (rows.shape[0] // height)
    for group in range(rows.shape[0] // height):
        rows[group * height : (group + 1) * height, :] = jnp.dot(
            perm_ref[...],
            wire_ref[group * span : (group + 1) * span, :],
            preferred_element_type=jnp.float32,
        ).astype(jnp.bfloat16)
    gate = jnp.dot(rows[...], gate_ref[...], preferred_element_type=jnp.float32)
    up = jnp.dot(rows[...], up_ref[...], preferred_element_type=jnp.float32)

    @pl.when(piece == 0)
    def _():
        gate_sum[...] = gate
        up_sum[...] = up

    @pl.when(piece > 0)
    def _():
        gate_sum[...] += gate
        up_sum[...] += up

    @pl.when(piece == PIECES - 1)
    def _():
        out_ref[...] = (jax.nn.silu(gate_sum[...]) * up_sum[...]).astype(jnp.bfloat16)


def hidden_units(wire, perm, gate_w, up_w):
    wire_rows, part = wire.shape
    rows = wire_rows // PIECES
    width, units = gate_w.shape
    height = perm.shape[0] // PIECES
    return pl.pallas_call(
        hidden_kernel,
        out_shape=jax.ShapeDtypeStruct((rows, units), jnp.bfloat16),
        grid=(PIECES,),
        in_specs=[
            pl.BlockSpec((wire_rows, part), lambda p: (0, 0)),
            pl.BlockSpec((height, perm.shape[1]), lambda p: (p, 0)),
            pl.BlockSpec((part, units), lambda p: (p, 0)),
            pl.BlockSpec((part, units), lambda p: (p, 0)),
        ],
        out_specs=pl.BlockSpec((rows, units), lambda p: (0, 0)),
        scratch_shapes=[
            pltpu.VMEM((rows, part), jnp.bfloat16),
            pltpu.VMEM((rows, units), jnp.float32),
            pltpu.VMEM((rows, units), jnp.float32),
        ],
        compiler_params=params(32),
        cost_estimate=pl.CostEstimate(
            flops=4 * rows * width * units, bytes_accessed=16 * MIB, transcendentals=rows * units
        ),
        name="hidden_units",
    )(wire, perm, gate_w, up_w)


def down_kernel(hidden_ref, down_ref, out_ref):
    out_ref[...] = jnp.dot(
        hidden_ref[...], down_ref[...], preferred_element_type=jnp.float32
    ).astype(jnp.bfloat16)


def down_rows(hidden, down_w):
    rows, units = hidden.shape
    width = down_w.shape[1]
    step = width // 4
    return pl.pallas_call(
        down_kernel,
        out_shape=jax.ShapeDtypeStruct((rows, width), jnp.bfloat16),
        grid=(width // step,),
        in_specs=[
            pl.BlockSpec((rows, units), lambda n: (0, 0)),
            pl.BlockSpec((units, step), lambda n: (0, n)),
        ],
        out_specs=pl.BlockSpec((rows, step), lambda n: (0, n)),
        compiler_params=params(24),
        cost_estimate=pl.CostEstimate(
            flops=2 * rows * width * units, bytes_accessed=10 * MIB, transcendentals=0
        ),
        name="down_rows",
    )(hidden, down_w)


def gather_kernel(own_ref, other_ref, perm_ref, out_ref, stacked):
    rows, width = own_ref.shape
    part = width // PIECES
    span = perm_ref.shape[0]
    height = span // PIECES
    for group in range(rows // height):
        lines = slice(group * height, (group + 1) * height)
        for piece in range(PIECES):
            columns = slice(piece * part, (piece + 1) * part)
            stacked[piece * height : (piece + 1) * height, :] = (
                own_ref[lines, columns].astype(jnp.float32)
                + other_ref[lines, columns].astype(jnp.float32)
            ).astype(jnp.bfloat16)
        for start in range(0, part, 256):
            columns = slice(start, start + 256)
            out_ref[group * span : (group + 1) * span, columns] = jnp.dot(
                perm_ref[...], stacked[:, columns], preferred_element_type=jnp.float32
            ).astype(jnp.bfloat16)


def add_halves(own, other, back):
    rows, width = own.shape
    part = width // PIECES
    return pl.pallas_call(
        gather_kernel,
        out_shape=jax.ShapeDtypeStruct((rows * PIECES, part), jnp.bfloat16),
        in_specs=[vmem()] * 3,
        out_specs=vmem(),
        scratch_shapes=[pltpu.VMEM((back.shape[0], part), jnp.bfloat16)],
        compiler_params=params(24),
        cost_estimate=pl.CostEstimate(
            flops=2 * rows * PIECES * back.shape[0] * part, bytes_accessed=7 * MIB, transcendentals=0
        ),
        name="add_halves",
    )(own, other, back)


def combine_kernel(x_ref, wire_ref, code_ref, weight_ref, row_ref, out_ref, factors):
    tokens, width = x_ref.shape
    part = width // PIECES
    count = PIECES * tokens
    rows = row_ref[...]
    table = jnp.where(rows == code_ref[:, 0:1], weight_ref[:, 0:1], 0.0)
    table += jnp.where(rows == code_ref[:, 1:2], weight_ref[:, 1:2], 0.0)
    high = table.astype(jnp.bfloat16)
    factors[:count, :] = high
    factors[count:, :] = (table - high.astype(jnp.float32)).astype(jnp.bfloat16)
    for start in range(0, part, 256):
        both = jnp.dot(
            factors[...], wire_ref[:, start : start + 256], preferred_element_type=jnp.float32
        )
        total = both[:count, :] + both[count:, :]
        for piece in range(PIECES):
            columns = slice(piece * part + start, piece * part + start + 256)
            out_ref[:, columns] = (
                x_ref[:, columns].astype(jnp.float32) + total[piece * tokens : (piece + 1) * tokens]
            ).astype(jnp.bfloat16)


def combine(x, wire, code, weight, rows):
    tokens, width = x.shape
    count = PIECES * tokens
    return pl.pallas_call(
        combine_kernel,
        out_shape=jax.ShapeDtypeStruct((tokens, width), jnp.bfloat16),
        in_specs=[vmem()] * 5,
        out_specs=vmem(),
        scratch_shapes=[pltpu.VMEM((2 * count, wire.shape[0]), jnp.bfloat16)],
        compiler_params=params(24),
        cost_estimate=pl.CostEstimate(
            flops=4 * count * wire.shape[0] * wire.shape[1],
            bytes_accessed=5 * MIB,
            transcendentals=0,
        ),
        name="combine",
    )(x, wire, code, weight, rows)


def slot_codes(routes, experts, capacity):
    flat = routes.reshape(-1)
    order = jnp.arange(flat.shape[0], dtype=jnp.int32)
    earlier = (flat[:, None] == flat[None, :]) & (order[None, :] < order[:, None])
    slot = flat * capacity + jnp.sum(earlier.astype(jnp.int32), axis=1)
    slot = slot.reshape(routes.shape)
    shift = jnp.arange(PIECES, dtype=jnp.int32) * (experts * capacity)
    return (shift[:, None, None] + slot[None]).reshape(-1, routes.shape[1])


def shards(tokens_a, tokens_b, routes_a, routes_b, affinity_a, affinity_b, gate_w, up_w, down_w):
    sections = lax.axis_size("pp")
    devices = lax.axis_size("ep")
    experts = devices // 2
    token_count, width = tokens_a.shape
    capacity = 2 * (token_count * routes_a.shape[2] // devices) + 2
    section = lax.axis_index("pp")
    gate, up, down = gate_w[0], up_w[0], down_w[0]

    codes = row_codes(experts, capacity)
    row_column = jnp.asarray(codes.reshape(-1, 1))
    row_line = jnp.asarray(codes.reshape(1, -1))
    order = group_permutation(capacity)
    to_rows = jnp.asarray(order, jnp.bfloat16)
    to_wire = jnp.asarray(order.T, jnp.bfloat16)

    one_core = [[2 * chip + core for chip in range(experts)] for core in range(2)]
    siblings = [(device, device ^ 1) for device in range(devices)]

    def exchange(wire):
        blocks = wire.reshape(experts, PIECES * capacity, width // PIECES)
        moved = lax.all_to_all(
            blocks, "ep", split_axis=0, concat_axis=0, tiled=True, axis_index_groups=one_core
        )
        return moved.reshape(wire.shape)

    def to_sibling(block):
        return lax.ppermute(block, "ep", siblings)

    codes_a = slot_codes(routes_a[0], experts, capacity)
    codes_b = slot_codes(routes_b[0], experts, capacity)
    weights_a = jnp.tile(affinity_a[0], (PIECES, 1))
    weights_b = jnp.tile(affinity_b[0], (PIECES, 1))

    x = jnp.where(section == 0, tokens_a, tokens_b)
    forward_state = reverse_state = None
    for moment in range(sections):
        last = sections - 1 - moment
        forward_turn = section == moment
        code = jnp.where(forward_turn, codes_a, codes_b)
        weight = jnp.where(forward_turn, weights_a, weights_b)
        own = exchange(dispatch(x, code.T, row_column))
        other = to_sibling(own)
        own_hidden = hidden_units(own, to_rows, gate, up)
        other_hidden = hidden_units(other, to_rows, gate, up)
        other_rows = to_sibling(down_rows(other_hidden, down))
        own_rows = down_rows(own_hidden, down)
        back = exchange(add_halves(own_rows, other_rows, to_wire))
        y = combine(x, back, code, weight, row_line)
        if moment == 0:
            forward_state = reverse_state = y
        else:
            forward_state = jnp.where(forward_turn, y, forward_state)
            reverse_state = jnp.where(section == last, y, reverse_state)
        if moment + 1 < sections:
            x = lax.ppermute(y, "pp", [(moment, moment + 1), (last, last - 1)])
    return (forward_state[None], reverse_state[None])


def solution(mesh):
    placed = (
        P("ep", None),
        P("ep", None),
        P("pp", "ep", None),
        P("pp", "ep", None),
        P("pp", "ep", None),
        P("pp", "ep", None),
        P("pp", None, "ep"),
        P("pp", None, "ep"),
        P("pp", "ep", None),
    )
    return jax.shard_map(
        shards,
        mesh=mesh,
        in_specs=placed,
        out_specs=(P("pp", "ep", None), P("pp", "ep", None)),
        check_vma=False,
    )
```

```python
import jax
import jax.numpy as jnp
from jax import lax
from jax.experimental import pallas as pl
from jax.experimental.pallas import tpu as pltpu
from jax.sharding import PartitionSpec as P

MIB = 1 << 20
PIECES = 4
AHEAD = 8
GROUP = 8


def vmem():
    return pl.BlockSpec(memory_space=pltpu.VMEM)


def smem():
    return pl.BlockSpec(memory_space=pltpu.SMEM)


def anywhere():
    return pl.BlockSpec(memory_space=pl.ANY)


def whole(array):
    return pl.BlockSpec(array.shape, lambda step: (0,) * len(array.shape))


def in_hbm(block):
    return pltpu.with_memory_space_constraint(block, pltpu.HBM)


def params(mib):
    return pltpu.CompilerParams(vmem_limit_bytes=mib * MIB)


def small_cost():
    return pl.CostEstimate(flops=MIB, bytes_accessed=MIB, transcendentals=0)


def spans(width, step=256):
    return [slice(start, min(start + step, width)) for start in range(0, width, step)]


def split(index, size, count):
    factor = -(-(1 << 16) // size)
    assert all((n * factor) >> 16 == n // size for n in range(size * count))
    high = (index * factor) >> 16
    return high, index - high * size


def wire_codes(shape, axis, experts, capacity):
    index = lax.broadcasted_iota(jnp.int32, shape, axis)
    expert, rest = split(index, PIECES * capacity, experts)
    piece, slot = split(rest, capacity, PIECES)
    return (piece * experts + expert) * capacity + slot


def group_order(axis, capacity):
    size = GROUP * PIECES * capacity
    shape = (1, size) if axis == 1 else (size, 1)
    index = lax.broadcasted_iota(jnp.int32, shape, axis)
    chip, rest = split(index, PIECES * capacity, GROUP)
    piece, slot = split(rest, capacity, PIECES)
    place = (piece * GROUP + chip) * capacity + slot
    other = lax.broadcasted_iota(jnp.int32, (size, size), 1 - axis)
    return jnp.where(other == place, 1.0, 0.0).astype(jnp.bfloat16)


def tie_kernel(*refs):
    del refs


def tie(first, second):
    return pl.pallas_call(
        tie_kernel,
        out_shape=tuple(pltpu.HBM(x.shape, x.dtype) for x in (first, second)),
        in_specs=[anywhere()] * 2,
        out_specs=(anywhere(),) * 2,
        input_output_aliases={0: 0, 1: 1},
        cost_estimate=pl.CostEstimate(flops=0, bytes_accessed=0, transcendentals=0),
        name="tie",
    )(in_hbm(first), in_hbm(second))


def dispatch(x, lines, moment, block, experts, capacity):
    tokens, width = x.shape
    part = width // PIECES
    wire = experts * PIECES * capacity
    count = PIECES * tokens

    def kernel(x_ref, line_ref, out_ref, stacked):
        for piece in range(PIECES):
            stacked[piece * tokens : (piece + 1) * tokens, :] = x_ref[
                :, piece * part : (piece + 1) * part
            ]
        rows = wire_codes((wire, 1), 0, experts, capacity)
        lines = line_ref[0, 0]
        hit = (rows == lines[0:1, :]) | (rows == lines[1:2, :])
        select = jnp.where(hit, 1.0, 0.0).astype(jnp.bfloat16)
        for columns in spans(part):
            out_ref[:, columns] = jnp.dot(
                select, stacked[:, columns], preferred_element_type=jnp.float32
            ).astype(jnp.bfloat16)

    return pl.pallas_call(
        kernel,
        out_shape=pltpu.HBM((wire, part), jnp.bfloat16),
        grid=(1,),
        in_specs=[
            whole(x),
            pl.BlockSpec((1, 1) + lines.shape[2:], lambda step: (moment, block, 0, 0)),
        ],
        out_specs=pl.BlockSpec((wire, part), lambda step: (0, 0)),
        scratch_shapes=[pltpu.VMEM((count, part), jnp.bfloat16)],
        compiler_params=params(24),
        cost_estimate=small_cost(),
        name="dispatch",
    )(x, in_hbm(lines))


def expert_rows(core, own, others, gate, up, down, capacity):
    wire_rows, part = own.shape
    rows_count = wire_rows // PIECES
    units = gate.shape[1]
    steps = 2 * PIECES
    half_width = PIECES * part
    height = GROUP * capacity
    span = PIECES * height
    groups = rows_count // height

    def kernel(
        core_ref, own_ref, low_ref, high_ref, gate_ref, up_ref, down_ref,
        mine_ref, theirs_0, theirs_1, theirs_2, theirs_3,
        wires, rows, gate_blocks, up_blocks, down_blocks, gate_sum, up_sum,
        wire_sems, gate_sems, up_sems, down_sems,
    ):
        core = core_ref[0]
        theirs = (theirs_0, theirs_1, theirs_2, theirs_3)
        wire_copies = [
            pltpu.make_async_copy(own_ref, wires.at[pl.ds(0, wire_rows)], wire_sems.at[0]),
            pltpu.make_async_copy(
                low_ref, wires.at[pl.ds(wire_rows, wire_rows // 2)], wire_sems.at[1]
            ),
            pltpu.make_async_copy(
                high_ref, wires.at[pl.ds(3 * wire_rows // 2, wire_rows // 2)], wire_sems.at[2]
            ),
        ]

        def loads(step):
            if step < steps:
                half = core if step < PIECES else 1 - core
                lines = pl.ds(pl.multiple_of((half * PIECES + step % PIECES) * part, part), part)
                return (
                    pltpu.make_async_copy(
                        gate_ref.at[lines], gate_blocks.at[step], gate_sems.at[step]
                    ),
                    pltpu.make_async_copy(up_ref.at[lines], up_blocks.at[step], up_sems.at[step]),
                )
            number = step - steps
            half = 1 - core if number < PIECES else core
            columns = pl.ds(pl.multiple_of((half * PIECES + number % PIECES) * part, part), part)
            return (
                pltpu.make_async_copy(
                    down_ref.at[:, columns], down_blocks.at[number], down_sems.at[number]
                ),
            )

        def start(step):
            if step < 2 * steps:
                for copy in loads(step):
                    copy.start()

        def wait(step):
            for copy in loads(step):
                copy.wait()
            start(step + AHEAD)

        for copy in wire_copies:
            copy.start()
        for step in range(AHEAD):
            start(step)
        order = group_order(1, capacity)
        squares = 0.0
        for step in range(steps):
            if step % PIECES == 0:
                base = 0 if step == 0 else wire_rows
                for copy in wire_copies[:1] if step == 0 else wire_copies[1:]:
                    copy.wait()
                for group in range(groups):
                    for columns in spans(part):
                        ordered = jnp.dot(
                            order,
                            wires[base + group * span : base + (group + 1) * span, columns],
                            preferred_element_type=jnp.float32,
                        ).astype(jnp.bfloat16)
                        for piece in range(PIECES):
                            rows[
                                group * height : (group + 1) * height,
                                piece * part + columns.start : piece * part + columns.stop,
                            ] = ordered[piece * height : (piece + 1) * height]
            wait(step)
            piece = step % PIECES
            values = rows[:, piece * part : (piece + 1) * part]
            gate = jnp.dot(values, gate_blocks[step], preferred_element_type=jnp.float32)
            up = jnp.dot(values, up_blocks[step], preferred_element_type=jnp.float32)
            if step == 0:
                gate_sum[...], up_sum[...] = gate, up
            else:
                gate_sum[...] += gate
                up_sum[...] += up
            for columns in spans(part, 128):
                few = values[:, columns].astype(jnp.float32)
                squares += few * few
        mean = jnp.sum(squares, axis=-1, keepdims=True) / (2 * half_width)
        scale = lax.rsqrt(mean + 1e-06)
        hidden = (jax.nn.silu(gate_sum[...] * scale) * (up_sum[...] * scale)).astype(jnp.bfloat16)
        for number in range(steps):
            wait(steps + number)
            piece = number % PIECES
            product = jnp.dot(
                hidden, down_blocks[number], preferred_element_type=jnp.float32
            ).astype(jnp.bfloat16)
            if number < PIECES:
                theirs[piece][...] = product
            else:
                mine_ref[:, piece * part : (piece + 1) * part] = product

    return pl.pallas_call(
        kernel,
        out_shape=(jax.ShapeDtypeStruct((rows_count, half_width), jnp.bfloat16),)
        + (jax.ShapeDtypeStruct((rows_count, part), jnp.bfloat16),) * PIECES,
        in_specs=[smem()] + [anywhere()] * 6,
        out_specs=(vmem(),) * (1 + PIECES),
        scratch_shapes=[
            pltpu.VMEM((2 * wire_rows, part), jnp.bfloat16),
            pltpu.VMEM((rows_count, half_width), jnp.bfloat16),
            pltpu.VMEM((steps, part, units), jnp.bfloat16),
            pltpu.VMEM((steps, part, units), jnp.bfloat16),
            pltpu.VMEM((steps, units, part), jnp.bfloat16),
            pltpu.VMEM((rows_count, units), jnp.float32),
            pltpu.VMEM((rows_count, units), jnp.float32),
            pltpu.SemaphoreType.DMA((3,)),
            pltpu.SemaphoreType.DMA((steps,)),
            pltpu.SemaphoreType.DMA((steps,)),
            pltpu.SemaphoreType.DMA((steps,)),
        ],
        compiler_params=params(40),
        cost_estimate=small_cost(),
        name="expert_rows",
    )(core, in_hbm(own), *others, in_hbm(gate), in_hbm(up), in_hbm(down))


def add_halves(own, others, capacity):
    rows, width = own.shape
    part = width // PIECES
    height = GROUP * capacity
    span = PIECES * height

    def kernel(own_ref, theirs_0, theirs_1, theirs_2, theirs_3, out_ref, stacked):
        order = group_order(0, capacity)
        for group in range(rows // height):
            lines = slice(group * height, (group + 1) * height)
            for piece, other_ref in enumerate((theirs_0, theirs_1, theirs_2, theirs_3)):
                stacked[piece * height : (piece + 1) * height, :] = (
                    own_ref[lines, piece * part : (piece + 1) * part].astype(jnp.float32)
                    + other_ref[lines, :].astype(jnp.float32)
                ).astype(jnp.bfloat16)
            for columns in spans(part):
                out_ref[group * span : (group + 1) * span, columns] = jnp.dot(
                    order, stacked[:, columns], preferred_element_type=jnp.float32
                ).astype(jnp.bfloat16)

    return pl.pallas_call(
        kernel,
        out_shape=pltpu.HBM((rows * PIECES, part), jnp.bfloat16),
        grid=(1,),
        in_specs=[whole(own)] + [whole(other) for other in others],
        out_specs=pl.BlockSpec((rows * PIECES, part), lambda step: (0, 0)),
        scratch_shapes=[pltpu.VMEM((span, part), jnp.bfloat16)],
        compiler_params=params(24),
        cost_estimate=small_cost(),
        name="add_halves",
    )(own, *others)


def combine(place, x, wire, columns, weights, states, moment, block, sections, experts, capacity):
    tokens, width = x.shape
    part = width // PIECES
    count = PIECES * tokens
    wire_rows = wire.shape[0]

    def kernel(place_ref, x_ref, wire_ref, column_ref, weight_ref, *rest):
        y_ref, forward_ref, reverse_ref, sent_ref, factors, sems = rest[-6:]
        section, core = place_ref[0], place_ref[1]
        rows = wire_codes((1, wire_rows), 1, experts, capacity)
        codes, shares = column_ref[0, 0], weight_ref[0, 0]
        table = jnp.where(rows == codes[:, 0:1], shares[:, 0:1], 0.0)
        table += jnp.where(rows == codes[:, 1:2], shares[:, 1:2], 0.0)
        high = table.astype(jnp.bfloat16)
        factors[:count, :] = high
        factors[count:, :] = (table - high.astype(jnp.float32)).astype(jnp.bfloat16)
        for lanes in spans(part):
            both = jnp.dot(factors[...], wire_ref[:, lanes], preferred_element_type=jnp.float32)
            total = both[:count, :] + both[count:, :]
            for piece in range(PIECES):
                target = slice(piece * part + lanes.start, piece * part + lanes.stop)
                y_ref[:, target] = (
                    x_ref[:, target].astype(jnp.float32) + total[piece * tokens : (piece + 1) * tokens]
                ).astype(jnp.bfloat16)
        for number, (state_ref, turn) in enumerate(
            ((forward_ref, moment), (reverse_ref, sections - 1 - moment))
        ):

            @pl.when((section == turn) & (core == block))
            def _():
                half = pl.ds(block * width, width)
                copy = pltpu.make_async_copy(y_ref, state_ref.at[:, half], sems.at[number])
                copy.start()
                copy.wait()

            @pl.when((section == turn) & (core != block))
            def _():
                copy = pltpu.make_async_copy(y_ref, sent_ref.at[number], sems.at[number])
                copy.start()
                copy.wait()

    result = pltpu.HBM((tokens, 2 * width), x.dtype)
    per_block = lambda array: pl.BlockSpec(
        (1, 1) + array.shape[2:], lambda step: (moment, block, 0, 0)
    )
    outs = pl.pallas_call(
        kernel,
        out_shape=(
            jax.ShapeDtypeStruct((tokens, width), x.dtype),
            result,
            result,
            pltpu.HBM((2, tokens, width), x.dtype),
        ),
        grid=(1,),
        in_specs=[smem(), whole(x), whole(wire), per_block(columns), per_block(weights)]
        + [anywhere()] * len(states),
        out_specs=(pl.BlockSpec((tokens, width), lambda step: (0, 0)),) + (anywhere(),) * 3,
        input_output_aliases={5 + n: 1 + n for n in range(len(states))},
        scratch_shapes=[
            pltpu.VMEM((2 * count, wire_rows), jnp.bfloat16),
            pltpu.SemaphoreType.DMA((2,)),
        ],
        compiler_params=params(24),
        cost_estimate=small_cost(),
        name="combine",
    )(
        place, in_hbm(x), in_hbm(wire), in_hbm(columns), in_hbm(weights),
        *[in_hbm(state) for state in states],
    )
    return outs[0], outs[1:]


def finish(place, states, arrived):
    tokens, width = arrived.shape[1:]

    def kernel(place_ref, forward_in, reverse_in, arrived_ref, forward_ref, reverse_ref, sems):
        del forward_in, reverse_in
        half = pl.ds(pl.multiple_of((1 - place_ref[1]) * width, width), width)
        copies = [
            pltpu.make_async_copy(arrived_ref.at[n], ref.at[:, half], sems.at[n])
            for n, ref in enumerate((forward_ref, reverse_ref))
        ]
        for copy in copies:
            copy.start()
        for copy in copies:
            copy.wait()

    return pl.pallas_call(
        kernel,
        out_shape=tuple(pltpu.HBM(state.shape, state.dtype) for state in states),
        in_specs=[smem()] + [anywhere()] * 3,
        out_specs=(anywhere(),) * 2,
        input_output_aliases={1: 0, 2: 1},
        scratch_shapes=[pltpu.SemaphoreType.DMA((2,))],
        name="finish",
    )(place, *[in_hbm(state) for state in states], arrived)


def slots(routes, experts, capacity):
    flat = routes.reshape(routes.shape[:-2] + (-1,))
    order = jnp.arange(flat.shape[-1], dtype=jnp.int32)
    earlier = (flat[..., :, None] == flat[..., None, :]) & (order[None, :] < order[:, None])
    slot = flat * capacity + jnp.sum(earlier.astype(jnp.int32), axis=-1)
    return slot.reshape(routes.shape)


def shards(tokens_a, tokens_b, routes_a, routes_b, affinity_a, affinity_b, gate_w, up_w, down_w):
    sections = lax.axis_size("pp")
    devices = lax.axis_size("ep")
    experts = devices // 2
    token_count, width = tokens_a.shape
    half_width = width // 2
    capacity = 2 * (token_count * routes_a.shape[2] // devices) + 2
    section = lax.axis_index("pp")
    core = (lax.axis_index("ep") % 2).astype(jnp.int32)
    low = core == 0
    place = jnp.stack([section.astype(jnp.int32), core])
    own_half = core.reshape(1)
    gate, up, down = gate_w[0], up_w[0], down_w[0]

    one_core = [[2 * chip + side for chip in range(experts)] for side in range(2)]
    siblings = [(device, device ^ 1) for device in range(devices)]

    def exchange(wire):
        blocks = wire.reshape(experts, PIECES * capacity, wire.shape[1])
        moved = lax.all_to_all(
            blocks, "ep", split_axis=0, concat_axis=0, tiled=True, axis_index_groups=one_core
        )
        return moved.reshape(wire.shape)

    def to_sibling(block):
        return lax.ppermute(block, "ep", siblings)

    def by_block(mine, theirs):
        return jnp.where(low, mine, theirs), jnp.where(low, theirs, mine)

    def by_moment(pair):
        return jnp.stack([jnp.where(section == m, pair[0], pair[1]) for m in range(sections)])

    target = slots(jnp.stack([routes_a[0], routes_b[0]]), experts, capacity)
    target = by_moment(target)
    affinity = by_moment(jnp.stack([affinity_a[0], affinity_b[0]]))
    target = jnp.stack(by_block(target, to_sibling(target)), axis=1)
    affinity = jnp.stack(by_block(affinity, to_sibling(affinity)), axis=1)
    shift = jnp.arange(PIECES, dtype=jnp.int32)[:, None, None] * (experts * capacity)
    flat = (sections, 2, PIECES * token_count, target.shape[-1])
    columns = (target[:, :, None] + shift).reshape(flat)
    weights = jnp.tile(affinity, (1, 1, PIECES, 1))
    lines = columns.swapaxes(2, 3)

    first = jnp.where(section == 0, tokens_a, tokens_b)
    lower, upper = first[:, :half_width], first[:, half_width:]
    chunks = list(
        by_block(jnp.where(low, lower, upper), to_sibling(jnp.where(low, upper, lower)))
    )

    def leave(i, moment):
        return dispatch(chunks[i], lines, moment, i, experts, capacity)

    def experts_of(wire):
        middle = wire.shape[0] // 2
        others = [to_sibling(wire[:middle]), to_sibling(wire[middle:])]
        mine, *theirs = expert_rows(own_half, wire, others, gate, up, down, capacity)
        return add_halves(mine, [to_sibling(block) for block in theirs], capacity)

    states = ()
    first_wire = exchange(leave(0, 0))
    second_leaving, first_wire = tie(leave(1, 0), first_wire)
    for moment in range(sections):
        last = sections - 1 - moment
        hop = [(moment, moment + 1), (last, last - 1)]

        def settle(i, back):
            y, after = combine(
                place, chunks[i], back, columns, weights, states, moment, i, sections, experts, capacity
            )
            if moment + 1 == sections:
                return after, None
            chunks[i] = lax.ppermute(y, "pp", hop)
            return after, leave(i, moment + 1)

        second_wire = exchange(second_leaving)
        first_rows = experts_of(first_wire)
        first_rows, second_wire = tie(first_rows, second_wire)
        first_back = exchange(first_rows)
        second_rows = experts_of(second_wire)
        second_rows, first_back = tie(second_rows, first_back)
        second_back = exchange(second_rows)
        states, first_leaving = settle(0, first_back)
        if moment + 1 < sections:
            first_leaving, second_back = tie(first_leaving, second_back)
            first_wire = exchange(first_leaving)
        states, second_leaving = settle(1, second_back)
        if moment + 1 < sections:
            second_leaving, first_wire = tie(second_leaving, first_wire)
    forward, reverse, sent = states
    forward, reverse = finish(place, (forward, reverse), to_sibling(sent))
    return (forward[None], reverse[None])


def solution(mesh):
    placed = (
        P("ep", None),
        P("ep", None),
        P("pp", "ep", None),
        P("pp", "ep", None),
        P("pp", "ep", None),
        P("pp", "ep", None),
        P("pp", None, "ep"),
        P("pp", None, "ep"),
        P("pp", "ep", None),
    )
    return jax.shard_map(
        shards,
        mesh=mesh,
        in_specs=placed,
        out_specs=(P("pp", "ep", None), P("pp", "ep", None)),
        check_vma=False,
    )
```

```python
import jax
import jax.numpy as jnp
from jax import lax
from jax.experimental import pallas as pl
from jax.experimental.pallas import tpu as pltpu
from jax.sharding import PartitionSpec as P

MIB = 1 << 20
PIECES = 4
GROUP = 8


def vmem():
    return pl.BlockSpec(memory_space=pltpu.VMEM)


def smem():
    return pl.BlockSpec(memory_space=pltpu.SMEM)


def anywhere():
    return pl.BlockSpec(memory_space=pl.ANY)


def whole(array):
    return pl.BlockSpec(array.shape, lambda step: (0,) * len(array.shape))


def in_hbm(block):
    return pltpu.with_memory_space_constraint(block, pltpu.HBM)


def params(mib):
    return pltpu.CompilerParams(vmem_limit_bytes=mib * MIB)


def small_cost():
    return pl.CostEstimate(flops=MIB, bytes_accessed=MIB, transcendentals=0)


def spans(width, step=256):
    return [slice(start, min(start + step, width)) for start in range(0, width, step)]


def split(index, size, count):
    factor = -(-(1 << 16) // size)
    assert all((n * factor) >> 16 == n // size for n in range(size * count))
    high = (index * factor) >> 16
    return high, index - high * size


def wire_codes(shape, axis, experts, capacity):
    index = lax.broadcasted_iota(jnp.int32, shape, axis)
    expert, rest = split(index, PIECES * capacity, experts)
    piece, slot = split(rest, capacity, PIECES)
    return (piece * experts + expert) * capacity + slot


def group_order(axis, capacity):
    size = GROUP * PIECES * capacity
    shape = (1, size) if axis == 1 else (size, 1)
    index = lax.broadcasted_iota(jnp.int32, shape, axis)
    chip, rest = split(index, PIECES * capacity, GROUP)
    piece, slot = split(rest, capacity, PIECES)
    place = (piece * GROUP + chip) * capacity + slot
    other = lax.broadcasted_iota(jnp.int32, (size, size), 1 - axis)
    return jnp.where(other == place, 1.0, 0.0).astype(jnp.bfloat16)


def tie_kernel(*refs):
    del refs


def tie(*blocks):
    return pl.pallas_call(
        tie_kernel,
        out_shape=tuple(pltpu.HBM(x.shape, x.dtype) for x in blocks),
        in_specs=[anywhere()] * len(blocks),
        out_specs=(anywhere(),) * len(blocks),
        input_output_aliases={n: n for n in range(len(blocks))},
        cost_estimate=pl.CostEstimate(flops=0, bytes_accessed=0, transcendentals=0),
        name="tie",
    )(*[in_hbm(x) for x in blocks])


def dispatch(x, lines, moment, block, experts, capacity):
    tokens, width = x.shape
    part = width // PIECES
    wire = experts * PIECES * capacity
    count = PIECES * tokens

    groups = 4
    lines_each = wire // groups

    def kernel(x_ref, line_ref, out_ref, stacked, ready, sems):
        for piece in range(PIECES):
            stacked[piece * tokens : (piece + 1) * tokens, :] = x_ref[
                :, piece * part : (piece + 1) * part
            ]
        lines = line_ref[0, 0]
        codes = wire_codes((wire, 1), 0, experts, capacity)
        copies = []
        for group in range(groups):
            place = slice(group * lines_each, (group + 1) * lines_each)
            rows = codes[place]
            hit = (rows == lines[0:1, :]) | (rows == lines[1:2, :])
            select = jnp.where(hit, 1.0, 0.0).astype(jnp.bfloat16)
            for columns in spans(part):
                ready[place, columns] = jnp.dot(
                    select, stacked[:, columns], preferred_element_type=jnp.float32
                ).astype(jnp.bfloat16)
            where = pl.ds(group * lines_each, lines_each)
            copies.append(
                pltpu.make_async_copy(ready.at[where], out_ref.at[where], sems.at[group])
            )
            copies[-1].start()
        for copy in copies:
            copy.wait()

    return pl.pallas_call(
        kernel,
        out_shape=pltpu.HBM((wire, part), jnp.bfloat16),
        grid=(1,),
        in_specs=[
            whole(x),
            pl.BlockSpec((1, 1) + lines.shape[2:], lambda step: (moment, block, 0, 0)),
        ],
        out_specs=anywhere(),
        scratch_shapes=[
            pltpu.VMEM((count, part), jnp.bfloat16),
            pltpu.VMEM((wire, part), jnp.bfloat16),
            pltpu.SemaphoreType.DMA((groups,)),
        ],
        compiler_params=params(24),
        cost_estimate=small_cost(),
        name="dispatch",
    )(x, in_hbm(lines))


def hidden_units(core, own, others, gate, up, capacity):
    wire_rows, part = own.shape
    rows_count = wire_rows // PIECES
    units = gate.shape[1]
    steps = 2 * PIECES
    half_width = PIECES * part
    height = GROUP * capacity
    span = PIECES * height
    groups = rows_count // height

    def kernel(
        core_ref, own_ref, low_ref, high_ref, gate_ref, up_ref, out_ref,
        wires, rows, gate_blocks, up_blocks, gate_sum, up_sum, wire_sems, gate_sems, up_sems,
    ):
        core = core_ref[0]
        wire_copies = [
            pltpu.make_async_copy(own_ref, wires.at[pl.ds(0, wire_rows)], wire_sems.at[0]),
            pltpu.make_async_copy(
                low_ref, wires.at[pl.ds(wire_rows, wire_rows // 2)], wire_sems.at[1]
            ),
            pltpu.make_async_copy(
                high_ref, wires.at[pl.ds(3 * wire_rows // 2, wire_rows // 2)], wire_sems.at[2]
            ),
        ]
        loads = []
        for step in range(steps):
            half = core if step < PIECES else 1 - core
            lines = pl.ds(pl.multiple_of((half * PIECES + step % PIECES) * part, part), part)
            loads.append(
                (
                    pltpu.make_async_copy(
                        gate_ref.at[lines], gate_blocks.at[step], gate_sems.at[step]
                    ),
                    pltpu.make_async_copy(up_ref.at[lines], up_blocks.at[step], up_sems.at[step]),
                )
            )
        for copy in wire_copies:
            copy.start()
        for pair in loads:
            for copy in pair:
                copy.start()
        order = group_order(1, capacity)
        squares = 0.0
        for step in range(steps):
            if step % PIECES == 0:
                base = 0 if step == 0 else wire_rows
                for copy in wire_copies[:1] if step == 0 else wire_copies[1:]:
                    copy.wait()
                for group in range(groups):
                    for columns in spans(part):
                        ordered = jnp.dot(
                            order,
                            wires[base + group * span : base + (group + 1) * span, columns],
                            preferred_element_type=jnp.float32,
                        ).astype(jnp.bfloat16)
                        for piece in range(PIECES):
                            rows[
                                group * height : (group + 1) * height,
                                piece * part + columns.start : piece * part + columns.stop,
                            ] = ordered[piece * height : (piece + 1) * height]
            for copy in loads[step]:
                copy.wait()
            piece = step % PIECES
            values = rows[:, piece * part : (piece + 1) * part]
            gate = jnp.dot(values, gate_blocks[step], preferred_element_type=jnp.float32)
            up = jnp.dot(values, up_blocks[step], preferred_element_type=jnp.float32)
            if step == 0:
                gate_sum[...], up_sum[...] = gate, up
            else:
                gate_sum[...] += gate
                up_sum[...] += up
            for columns in spans(part, 128):
                few = values[:, columns].astype(jnp.float32)
                squares += few * few
        mean = jnp.sum(squares, axis=-1, keepdims=True) / (2 * half_width)
        scale = lax.rsqrt(mean + 1e-06)
        out_ref[...] = (jax.nn.silu(gate_sum[...] * scale) * (up_sum[...] * scale)).astype(
            jnp.bfloat16
        )

    return pl.pallas_call(
        kernel,
        out_shape=jax.ShapeDtypeStruct((rows_count, units), jnp.bfloat16),
        in_specs=[smem()] + [anywhere()] * 5,
        out_specs=vmem(),
        scratch_shapes=[
            pltpu.VMEM((2 * wire_rows, part), jnp.bfloat16),
            pltpu.VMEM((rows_count, half_width), jnp.bfloat16),
            pltpu.VMEM((steps, part, units), jnp.bfloat16),
            pltpu.VMEM((steps, part, units), jnp.bfloat16),
            pltpu.VMEM((rows_count, units), jnp.float32),
            pltpu.VMEM((rows_count, units), jnp.float32),
            pltpu.SemaphoreType.DMA((3,)),
            pltpu.SemaphoreType.DMA((steps,)),
            pltpu.SemaphoreType.DMA((steps,)),
        ],
        compiler_params=params(40),
        cost_estimate=small_cost(),
        name="hidden_units",
    )(core, in_hbm(own), *others, in_hbm(gate), in_hbm(up))


def down_rows(core, hidden, other_hidden, down, other_down, capacity):
    rows, units = hidden.shape
    half_width = other_down.shape[1]
    part = half_width // PIECES
    height = GROUP * capacity
    span = PIECES * height
    groups = rows // height

    def kernel(
        core_ref, hidden_ref, other_ref, down_ref, other_down_ref, out_ref,
        blocks, other_blocks, stacked, ready, sems, other_sems, out_sems,
    ):
        core = core_ref[0]
        loads = []
        for piece in range(PIECES):
            place = pl.ds(pl.multiple_of((core * PIECES + piece) * part, part), part)
            loads.append(
                (
                    pltpu.make_async_copy(down_ref.at[:, place], blocks.at[piece], sems.at[piece]),
                    pltpu.make_async_copy(
                        other_down_ref.at[:, pl.ds(piece * part, part)],
                        other_blocks.at[piece],
                        other_sems.at[piece],
                    ),
                )
            )
        for pair in loads:
            for copy in pair:
                copy.start()
        order = group_order(0, capacity)
        for piece in range(PIECES):
            for copy in loads[piece]:
                copy.wait()
            total = jnp.dot(hidden_ref[...], blocks[piece], preferred_element_type=jnp.float32)
            total += jnp.dot(
                other_ref[...], other_blocks[piece], preferred_element_type=jnp.float32
            )
            total = total.astype(jnp.bfloat16)
            for group in range(groups):
                at = group * span + piece * height
                stacked[at : at + height, :] = total[group * height : (group + 1) * height]
        copies = []
        for group in range(groups):
            lines = slice(group * span, (group + 1) * span)
            for columns in spans(part):
                ready[lines, columns] = jnp.dot(
                    order, stacked[lines, columns], preferred_element_type=jnp.float32
                ).astype(jnp.bfloat16)
            where = pl.ds(group * span, span)
            copies.append(
                pltpu.make_async_copy(ready.at[where], out_ref.at[where], out_sems.at[group])
            )
            copies[-1].start()
        for copy in copies:
            copy.wait()

    return pl.pallas_call(
        kernel,
        out_shape=pltpu.HBM((rows * PIECES, part), jnp.bfloat16),
        in_specs=[smem(), vmem(), vmem()] + [anywhere()] * 2,
        out_specs=anywhere(),
        scratch_shapes=[
            pltpu.VMEM((PIECES, units, part), jnp.bfloat16),
            pltpu.VMEM((PIECES, units, part), jnp.bfloat16),
            pltpu.VMEM((rows * PIECES, part), jnp.bfloat16),
            pltpu.VMEM((rows * PIECES, part), jnp.bfloat16),
            pltpu.SemaphoreType.DMA((PIECES,)),
            pltpu.SemaphoreType.DMA((PIECES,)),
            pltpu.SemaphoreType.DMA((groups,)),
        ],
        compiler_params=params(40),
        cost_estimate=small_cost(),
        name="down_rows",
    )(core, hidden, other_hidden, in_hbm(down), in_hbm(other_down))


def combine(x, wire, columns, weights, moment, block, experts, capacity):
    tokens, width = x.shape
    part = width // PIECES
    count = PIECES * tokens
    wire_rows = wire.shape[0]

    def kernel(x_ref, wire_ref, column_ref, weight_ref, y_ref, factors):
        rows = wire_codes((1, wire_rows), 1, experts, capacity)
        codes, shares = column_ref[0, 0], weight_ref[0, 0]
        table = jnp.where(rows == codes[:, 0:1], shares[:, 0:1], 0.0)
        table += jnp.where(rows == codes[:, 1:2], shares[:, 1:2], 0.0)
        high = table.astype(jnp.bfloat16)
        factors[:count, :] = high
        factors[count:, :] = (table - high.astype(jnp.float32)).astype(jnp.bfloat16)
        for lanes in spans(part):
            both = jnp.dot(factors[...], wire_ref[:, lanes], preferred_element_type=jnp.float32)
            total = both[:count, :] + both[count:, :]
            for piece in range(PIECES):
                target = slice(piece * part + lanes.start, piece * part + lanes.stop)
                y_ref[:, target] = (
                    x_ref[:, target].astype(jnp.float32) + total[piece * tokens : (piece + 1) * tokens]
                ).astype(jnp.bfloat16)

    per_block = lambda array: pl.BlockSpec(
        (1, 1) + array.shape[2:], lambda step: (moment, block, 0, 0)
    )
    return pl.pallas_call(
        kernel,
        out_shape=jax.ShapeDtypeStruct((tokens, width), x.dtype),
        grid=(1,),
        in_specs=[whole(x), whole(wire), per_block(columns), per_block(weights)],
        out_specs=pl.BlockSpec((tokens, width), lambda step: (0, 0)),
        scratch_shapes=[pltpu.VMEM((2 * count, wire_rows), jnp.bfloat16)],
        compiler_params=params(24),
        cost_estimate=small_cost(),
        name="combine",
    )(in_hbm(x), in_hbm(wire), in_hbm(columns), in_hbm(weights))


def record(place, y, states, moment, block, sections):
    tokens, width = y.shape

    def kernel(place_ref, y_ref, *rest):
        forward_ref, reverse_ref, sent_ref, sems = rest[-4:]
        section, core = place_ref[0], place_ref[1]
        for number, (state_ref, turn) in enumerate(
            ((forward_ref, moment), (reverse_ref, sections - 1 - moment))
        ):

            @pl.when((section == turn) & (core == block))
            def _():
                half = pl.ds(block * width, width)
                copy = pltpu.make_async_copy(y_ref, state_ref.at[:, half], sems.at[number])
                copy.start()
                copy.wait()

            @pl.when((section == turn) & (core != block))
            def _():
                copy = pltpu.make_async_copy(y_ref, sent_ref.at[number], sems.at[number])
                copy.start()
                copy.wait()

    result = pltpu.HBM((tokens, 2 * width), y.dtype)
    return pl.pallas_call(
        kernel,
        out_shape=(result, result, pltpu.HBM((2, tokens, width), y.dtype)),
        in_specs=[smem()] + [anywhere()] * (1 + len(states)),
        out_specs=(anywhere(),) * 3,
        input_output_aliases={2 + n: n for n in range(len(states))},
        scratch_shapes=[pltpu.SemaphoreType.DMA((2,))],
        cost_estimate=small_cost(),
        name="record",
    )(place, y, *[in_hbm(state) for state in states])


def finish(place, states, arrived):
    tokens, width = arrived.shape[1:]

    def kernel(place_ref, forward_in, reverse_in, arrived_ref, forward_ref, reverse_ref, sems):
        del forward_in, reverse_in
        half = pl.ds(pl.multiple_of((1 - place_ref[1]) * width, width), width)
        copies = [
            pltpu.make_async_copy(arrived_ref.at[n], ref.at[:, half], sems.at[n])
            for n, ref in enumerate((forward_ref, reverse_ref))
        ]
        for copy in copies:
            copy.start()
        for copy in copies:
            copy.wait()

    return pl.pallas_call(
        kernel,
        out_shape=tuple(pltpu.HBM(state.shape, state.dtype) for state in states),
        in_specs=[smem()] + [anywhere()] * 3,
        out_specs=(anywhere(),) * 2,
        input_output_aliases={1: 0, 2: 1},
        scratch_shapes=[pltpu.SemaphoreType.DMA((2,))],
        name="finish",
    )(place, *[in_hbm(state) for state in states], arrived)


def slots(routes, experts, capacity):
    flat = routes.reshape(routes.shape[:-2] + (-1,))
    order = jnp.arange(flat.shape[-1], dtype=jnp.int32)
    earlier = (flat[..., :, None] == flat[..., None, :]) & (order[None, :] < order[:, None])
    slot = flat * capacity + jnp.sum(earlier.astype(jnp.int32), axis=-1)
    return slot.reshape(routes.shape)


def shards(tokens_a, tokens_b, routes_a, routes_b, affinity_a, affinity_b, gate_w, up_w, down_w):
    sections = lax.axis_size("pp")
    devices = lax.axis_size("ep")
    experts = devices // 2
    token_count, width = tokens_a.shape
    half_width = width // 2
    capacity = 2 * (token_count * routes_a.shape[2] // devices) + 2
    section = lax.axis_index("pp")
    core = (lax.axis_index("ep") % 2).astype(jnp.int32)
    low = core == 0
    place = jnp.stack([section.astype(jnp.int32), core])
    own_half = core.reshape(1)
    gate, up, down = gate_w[0], up_w[0], down_w[0]

    one_core = [[2 * chip + side for chip in range(experts)] for side in range(2)]
    siblings = [(device, device ^ 1) for device in range(devices)]

    def exchange(wire):
        blocks = wire.reshape(experts, PIECES * capacity, wire.shape[1])
        moved = lax.all_to_all(
            blocks, "ep", split_axis=0, concat_axis=0, tiled=True, axis_index_groups=one_core
        )
        return moved.reshape(wire.shape)

    def to_sibling(block):
        return lax.ppermute(block, "ep", siblings)

    def by_block(mine, theirs):
        return jnp.where(low, mine, theirs), jnp.where(low, theirs, mine)

    def by_moment(pair):
        return jnp.stack([jnp.where(section == m, pair[0], pair[1]) for m in range(sections)])

    target = slots(jnp.stack([routes_a[0], routes_b[0]]), experts, capacity)
    target = by_moment(target)
    affinity = by_moment(jnp.stack([affinity_a[0], affinity_b[0]]))
    target = jnp.stack(by_block(target, to_sibling(target)), axis=1)
    affinity = jnp.stack(by_block(affinity, to_sibling(affinity)), axis=1)
    shift = jnp.arange(PIECES, dtype=jnp.int32)[:, None, None] * (experts * capacity)
    flat = (sections, 2, PIECES * token_count, target.shape[-1])
    columns = (target[:, :, None] + shift).reshape(flat)
    weights = jnp.tile(affinity, (1, 1, PIECES, 1))
    lines = columns.swapaxes(2, 3)

    first = jnp.where(section == 0, tokens_a, tokens_b)
    lower, upper = first[:, :half_width], first[:, half_width:]
    chunks = list(
        by_block(jnp.where(low, lower, upper), to_sibling(jnp.where(low, upper, lower)))
    )

    def leave(i, moment):
        return dispatch(chunks[i], lines, moment, i, experts, capacity)

    def experts_of(wire):
        middle = wire.shape[0] // 2
        others = [to_sibling(wire[:middle]), to_sibling(wire[middle:])]
        hidden = hidden_units(own_half, wire, others, gate, up, capacity)
        return down_rows(own_half, hidden, to_sibling(hidden), down, other_down, capacity)

    leaving_down = jnp.where(low, down[:, half_width:], down[:, :half_width])
    other_down = jnp.concatenate([to_sibling(block) for block in jnp.split(leaving_down, 4)])

    states = ()
    first_wire = exchange(leave(0, 0))
    second_leaving, first_wire, other_down = tie(leave(1, 0), first_wire, other_down)
    for moment in range(sections):
        last = sections - 1 - moment
        hop = [(moment, moment + 1), (last, last - 1)]

        def settle(i, back):
            y = combine(chunks[i], back, columns, weights, moment, i, experts, capacity)
            after = record(place, y, states, moment, i, sections)
            if moment + 1 == sections:
                return after, None
            chunks[i] = lax.ppermute(y, "pp", hop)
            return after, leave(i, moment + 1)

        second_wire = exchange(second_leaving)
        first_rows = experts_of(first_wire)
        first_rows, second_wire = tie(first_rows, second_wire)
        first_back = exchange(first_rows)
        second_rows = experts_of(second_wire)
        second_rows, first_back = tie(second_rows, first_back)
        second_back = exchange(second_rows)
        states, first_leaving = settle(0, first_back)
        if moment + 1 < sections:
            first_leaving, second_back = tie(first_leaving, second_back)
            first_wire = exchange(first_leaving)
        states, second_leaving = settle(1, second_back)
        if moment + 1 < sections:
            second_leaving, first_wire = tie(second_leaving, first_wire)
    forward, reverse, sent = states
    forward, reverse = finish(place, (forward, reverse), to_sibling(sent))
    return (forward[None], reverse[None])


def solution(mesh):
    placed = (
        P("ep", None),
        P("ep", None),
        P("pp", "ep", None),
        P("pp", "ep", None),
        P("pp", "ep", None),
        P("pp", "ep", None),
        P("pp", None, "ep"),
        P("pp", None, "ep"),
        P("pp", "ep", None),
    )
    return jax.shard_map(
        shards,
        mesh=mesh,
        in_specs=placed,
        out_specs=(P("pp", "ep", None), P("pp", "ep", None)),
        check_vma=False,
    )
```

```python
import jax
import jax.numpy as jnp
from jax import lax
from jax.experimental import pallas as pl
from jax.experimental.pallas import tpu as pltpu
from jax.sharding import PartitionSpec as P

MIB = 1 << 20
PIECES = 4
GROUP = 8


def vmem():
    return pl.BlockSpec(memory_space=pltpu.VMEM)


def smem():
    return pl.BlockSpec(memory_space=pltpu.SMEM)


def anywhere():
    return pl.BlockSpec(memory_space=pl.ANY)


def whole(array):
    return pl.BlockSpec(array.shape, lambda step: (0,) * len(array.shape))


def in_hbm(block):
    return pltpu.with_memory_space_constraint(block, pltpu.HBM)


def in_vmem(block):
    return pltpu.with_memory_space_constraint(block, pltpu.VMEM)


def params(mib):
    return pltpu.CompilerParams(vmem_limit_bytes=mib * MIB)


def small_cost():
    return pl.CostEstimate(flops=MIB, bytes_accessed=MIB, transcendentals=0)


def spans(width, step=256):
    return [slice(start, min(start + step, width)) for start in range(0, width, step)]


def split(index, size, count):
    factor = -(-(1 << 16) // size)
    assert all((n * factor) >> 16 == n // size for n in range(size * count))
    high = (index * factor) >> 16
    return high, index - high * size


def wire_codes(shape, axis, experts, capacity):
    index = lax.broadcasted_iota(jnp.int32, shape, axis)
    expert, rest = split(index, PIECES * capacity, experts)
    piece, slot = split(rest, capacity, PIECES)
    return (piece * experts + expert) * capacity + slot


def group_order(axis, capacity):
    size = GROUP * PIECES * capacity
    shape = (1, size) if axis == 1 else (size, 1)
    index = lax.broadcasted_iota(jnp.int32, shape, axis)
    chip, rest = split(index, PIECES * capacity, GROUP)
    piece, slot = split(rest, capacity, PIECES)
    place = (piece * GROUP + chip) * capacity + slot
    other = lax.broadcasted_iota(jnp.int32, (size, size), 1 - axis)
    return jnp.where(other == place, 1.0, 0.0).astype(jnp.bfloat16)


def tie_kernel(*refs):
    del refs


def tie(*blocks):
    return pl.pallas_call(
        tie_kernel,
        out_shape=tuple(pltpu.HBM(x.shape, x.dtype) for x in blocks),
        in_specs=[anywhere()] * len(blocks),
        out_specs=(anywhere(),) * len(blocks),
        input_output_aliases={n: n for n in range(len(blocks))},
        cost_estimate=pl.CostEstimate(flops=0, bytes_accessed=0, transcendentals=0),
        name="tie",
    )(*[in_hbm(x) for x in blocks])


def dispatch(x, lines, moment, block, experts, capacity, after=()):
    tokens, width = x.shape
    part = width // PIECES
    wire = experts * PIECES * capacity
    count = PIECES * tokens

    groups = 4
    lines_each = wire // groups

    def kernel(x_ref, line_ref, *rest):
        out_ref, stacked, ready, sems = rest[-4:]
        for piece in range(PIECES):
            stacked[piece * tokens : (piece + 1) * tokens, :] = x_ref[
                :, piece * part : (piece + 1) * part
            ]
        lines = line_ref[0, 0]
        codes = wire_codes((wire, 1), 0, experts, capacity)
        copies = []
        for group in range(groups):
            place = slice(group * lines_each, (group + 1) * lines_each)
            rows = codes[place]
            hit = (rows == lines[0:1, :]) | (rows == lines[1:2, :])
            select = jnp.where(hit, 1.0, 0.0).astype(jnp.bfloat16)
            for columns in spans(part):
                ready[place, columns] = jnp.dot(
                    select, stacked[:, columns], preferred_element_type=jnp.float32
                ).astype(jnp.bfloat16)
            where = pl.ds(group * lines_each, lines_each)
            copies.append(
                pltpu.make_async_copy(ready.at[where], out_ref.at[where], sems.at[group])
            )
            copies[-1].start()
        for copy in copies:
            copy.wait()

    return pl.pallas_call(
        kernel,
        out_shape=pltpu.HBM((wire, part), jnp.bfloat16),
        grid=(1,),
        in_specs=[
            whole(x),
            pl.BlockSpec((1, 1) + lines.shape[2:], lambda step: (moment, block, 0, 0)),
        ]
        + [anywhere()] * len(after),
        out_specs=anywhere(),
        scratch_shapes=[
            pltpu.VMEM((count, part), jnp.bfloat16),
            pltpu.VMEM((wire, part), jnp.bfloat16),
            pltpu.SemaphoreType.DMA((groups,)),
        ],
        compiler_params=params(24),
        cost_estimate=small_cost(),
        name="dispatch",
    )(x, in_hbm(lines), *[in_hbm(block) for block in after])


def hidden_units(core, own, others, gate, up, capacity):
    wire_rows, part = own.shape
    rows_count = wire_rows // PIECES
    units = gate.shape[1]
    steps = 2 * PIECES
    half_width = PIECES * part
    height = GROUP * capacity
    span = PIECES * height
    groups = rows_count // height

    def kernel(
        core_ref, own_ref, low_ref, high_ref, gate_ref, up_ref, out_ref,
        wires, rows, gate_blocks, up_blocks, gate_sum, up_sum, wire_sems, gate_sems, up_sems,
    ):
        core = core_ref[0]
        wire_copies = [
            pltpu.make_async_copy(own_ref, wires.at[pl.ds(0, wire_rows)], wire_sems.at[0]),
            pltpu.make_async_copy(
                low_ref, wires.at[pl.ds(wire_rows, wire_rows // 2)], wire_sems.at[1]
            ),
            pltpu.make_async_copy(
                high_ref, wires.at[pl.ds(3 * wire_rows // 2, wire_rows // 2)], wire_sems.at[2]
            ),
        ]
        loads = []
        for step in range(steps):
            half = core if step < PIECES else 1 - core
            lines = pl.ds(pl.multiple_of((half * PIECES + step % PIECES) * part, part), part)
            loads.append(
                (
                    pltpu.make_async_copy(
                        gate_ref.at[lines], gate_blocks.at[step], gate_sems.at[step]
                    ),
                    pltpu.make_async_copy(up_ref.at[lines], up_blocks.at[step], up_sems.at[step]),
                )
            )
        for copy in wire_copies:
            copy.start()
        for pair in loads:
            for copy in pair:
                copy.start()
        order = group_order(1, capacity)
        squares = 0.0
        for step in range(steps):
            if step % PIECES == 0:
                base = 0 if step == 0 else wire_rows
                for copy in wire_copies[:1] if step == 0 else wire_copies[1:]:
                    copy.wait()
                for group in range(groups):
                    for columns in spans(part):
                        ordered = jnp.dot(
                            order,
                            wires[base + group * span : base + (group + 1) * span, columns],
                            preferred_element_type=jnp.float32,
                        ).astype(jnp.bfloat16)
                        for piece in range(PIECES):
                            rows[
                                group * height : (group + 1) * height,
                                piece * part + columns.start : piece * part + columns.stop,
                            ] = ordered[piece * height : (piece + 1) * height]
            for copy in loads[step]:
                copy.wait()
            piece = step % PIECES
            values = rows[:, piece * part : (piece + 1) * part]
            gate = jnp.dot(values, gate_blocks[step], preferred_element_type=jnp.float32)
            up = jnp.dot(values, up_blocks[step], preferred_element_type=jnp.float32)
            if step == 0:
                gate_sum[...], up_sum[...] = gate, up
            else:
                gate_sum[...] += gate
                up_sum[...] += up
            for columns in spans(part, 128):
                few = values[:, columns].astype(jnp.float32)
                squares += few * few
        mean = jnp.sum(squares, axis=-1, keepdims=True) / (2 * half_width)
        scale = lax.rsqrt(mean + 1e-06)
        out_ref[...] = (jax.nn.silu(gate_sum[...] * scale) * (up_sum[...] * scale)).astype(
            jnp.bfloat16
        )

    return pl.pallas_call(
        kernel,
        out_shape=jax.ShapeDtypeStruct((rows_count, units), jnp.bfloat16),
        in_specs=[smem()] + [anywhere()] * 5,
        out_specs=vmem(),
        scratch_shapes=[
            pltpu.VMEM((2 * wire_rows, part), jnp.bfloat16),
            pltpu.VMEM((rows_count, half_width), jnp.bfloat16),
            pltpu.VMEM((steps, part, units), jnp.bfloat16),
            pltpu.VMEM((steps, part, units), jnp.bfloat16),
            pltpu.VMEM((rows_count, units), jnp.float32),
            pltpu.VMEM((rows_count, units), jnp.float32),
            pltpu.SemaphoreType.DMA((3,)),
            pltpu.SemaphoreType.DMA((steps,)),
            pltpu.SemaphoreType.DMA((steps,)),
        ],
        compiler_params=params(40),
        cost_estimate=small_cost(),
        name="hidden_units",
    )(core, in_hbm(own), *others, in_hbm(gate), in_hbm(up))


def down_rows(core, hidden, other_hidden, down, other_down, capacity):
    rows, units = hidden.shape
    lines_each, half_width = other_down[0].shape
    blocks_count = len(other_down)
    part = half_width // PIECES
    height = GROUP * capacity
    span = PIECES * height
    groups = rows // height

    def kernel(
        core_ref, hidden_ref, other_ref, down_ref, *rest
    ):
        other_down_refs, rest = rest[:blocks_count], rest[blocks_count:]
        out_ref, blocks, other_blocks, stacked, ready, sems, other_sems, out_sems = rest
        core = core_ref[0]
        loads = []
        for piece in range(PIECES):
            place = pl.ds(pl.multiple_of((core * PIECES + piece) * part, part), part)
            loads.append(
                [pltpu.make_async_copy(down_ref.at[:, place], blocks.at[piece], sems.at[piece])]
                + [
                    pltpu.make_async_copy(
                        ref.at[:, pl.ds(piece * part, part)],
                        other_blocks.at[piece, pl.ds(number * lines_each, lines_each)],
                        other_sems.at[piece, number],
                    )
                    for number, ref in enumerate(other_down_refs)
                ]
            )
        for pair in loads:
            for copy in pair:
                copy.start()
        order = group_order(0, capacity)
        for piece in range(PIECES):
            for copy in loads[piece]:
                copy.wait()
            total = jnp.dot(hidden_ref[...], blocks[piece], preferred_element_type=jnp.float32)
            total += jnp.dot(
                other_ref[...], other_blocks[piece], preferred_element_type=jnp.float32
            )
            total = total.astype(jnp.bfloat16)
            for group in range(groups):
                at = group * span + piece * height
                stacked[at : at + height, :] = total[group * height : (group + 1) * height]
        copies = []
        for group in range(groups):
            lines = slice(group * span, (group + 1) * span)
            for columns in spans(part):
                ready[lines, columns] = jnp.dot(
                    order, stacked[lines, columns], preferred_element_type=jnp.float32
                ).astype(jnp.bfloat16)
            where = pl.ds(group * span, span)
            copies.append(
                pltpu.make_async_copy(ready.at[where], out_ref.at[where], out_sems.at[group])
            )
            copies[-1].start()
        for copy in copies:
            copy.wait()

    return pl.pallas_call(
        kernel,
        out_shape=pltpu.HBM((rows * PIECES, part), jnp.bfloat16),
        in_specs=[smem(), vmem(), vmem()] + [anywhere()] * (1 + blocks_count),
        out_specs=anywhere(),
        scratch_shapes=[
            pltpu.VMEM((PIECES, units, part), jnp.bfloat16),
            pltpu.VMEM((PIECES, units, part), jnp.bfloat16),
            pltpu.VMEM((rows * PIECES, part), jnp.bfloat16),
            pltpu.VMEM((rows * PIECES, part), jnp.bfloat16),
            pltpu.SemaphoreType.DMA((PIECES,)),
            pltpu.SemaphoreType.DMA((PIECES, blocks_count)),
            pltpu.SemaphoreType.DMA((groups,)),
        ],
        compiler_params=params(40),
        cost_estimate=small_cost(),
        name="down_rows",
    )(core, hidden, other_hidden, in_hbm(down), *[in_hbm(block) for block in other_down])


def other_half(core, down, after, count):
    units, width = down.shape
    half_width = width // 2
    height = units // count

    def kernel(core_ref, down_ref, after_ref, *rest):
        del after_ref
        outs, sems = rest[:-1], rest[-1]
        place = pl.ds(pl.multiple_of((1 - core_ref[0]) * half_width, half_width), half_width)
        copies = [
            pltpu.make_async_copy(
                down_ref.at[pl.ds(number * height, height), place], out, sems.at[number]
            )
            for number, out in enumerate(outs)
        ]
        for copy in copies:
            copy.start()
        for copy in copies:
            copy.wait()

    return pl.pallas_call(
        kernel,
        out_shape=(jax.ShapeDtypeStruct((height, half_width), down.dtype),) * count,
        in_specs=[smem()] + [anywhere()] * 2,
        out_specs=(vmem(),) * count,
        scratch_shapes=[pltpu.SemaphoreType.DMA((count,))],
        compiler_params=params(24),
        cost_estimate=small_cost(),
        name="other_half",
    )(core, in_hbm(down), in_hbm(after))


def combine(x, wire, columns, weights, moment, block, experts, capacity):
    tokens, width = x.shape
    part = width // PIECES
    count = PIECES * tokens
    wire_rows = wire.shape[0]

    def kernel(x_ref, wire_ref, column_ref, weight_ref, y_ref, factors):
        rows = wire_codes((1, wire_rows), 1, experts, capacity)
        codes, shares = column_ref[0, 0], weight_ref[0, 0]
        table = jnp.where(rows == codes[:, 0:1], shares[:, 0:1], 0.0)
        table += jnp.where(rows == codes[:, 1:2], shares[:, 1:2], 0.0)
        high = table.astype(jnp.bfloat16)
        factors[:count, :] = high
        factors[count:, :] = (table - high.astype(jnp.float32)).astype(jnp.bfloat16)
        for lanes in spans(part):
            both = jnp.dot(factors[...], wire_ref[:, lanes], preferred_element_type=jnp.float32)
            total = both[:count, :] + both[count:, :]
            for piece in range(PIECES):
                target = slice(piece * part + lanes.start, piece * part + lanes.stop)
                y_ref[:, target] = (
                    x_ref[:, target].astype(jnp.float32) + total[piece * tokens : (piece + 1) * tokens]
                ).astype(jnp.bfloat16)

    per_block = lambda array: pl.BlockSpec(
        (1, 1) + array.shape[2:], lambda step: (moment, block, 0, 0)
    )
    return pl.pallas_call(
        kernel,
        out_shape=jax.ShapeDtypeStruct((tokens, width), x.dtype),
        grid=(1,),
        in_specs=[whole(x), whole(wire), per_block(columns), per_block(weights)],
        out_specs=pl.BlockSpec((tokens, width), lambda step: (0, 0)),
        scratch_shapes=[pltpu.VMEM((2 * count, wire_rows), jnp.bfloat16)],
        compiler_params=params(24),
        cost_estimate=small_cost(),
        name="combine",
    )(in_hbm(x), in_hbm(wire), in_hbm(columns), in_hbm(weights))


def record(place, y, states, moment, block, sections):
    tokens, width = y.shape

    def kernel(place_ref, y_ref, *rest):
        forward_ref, reverse_ref, sent_ref, sems = rest[-4:]
        section, core = place_ref[0], place_ref[1]
        for number, (state_ref, turn) in enumerate(
            ((forward_ref, moment), (reverse_ref, sections - 1 - moment))
        ):

            @pl.when((section == turn) & (core == block))
            def _():
                half = pl.ds(block * width, width)
                copy = pltpu.make_async_copy(y_ref, state_ref.at[:, half], sems.at[number])
                copy.start()
                copy.wait()

            @pl.when((section == turn) & (core != block))
            def _():
                copy = pltpu.make_async_copy(y_ref, sent_ref.at[number], sems.at[number])
                copy.start()
                copy.wait()

    result = pltpu.HBM((tokens, 2 * width), y.dtype)
    return pl.pallas_call(
        kernel,
        out_shape=(result, result, pltpu.HBM((2, tokens, width), y.dtype)),
        in_specs=[smem()] + [anywhere()] * (1 + len(states)),
        out_specs=(anywhere(),) * 3,
        input_output_aliases={2 + n: n for n in range(len(states))},
        scratch_shapes=[pltpu.SemaphoreType.DMA((2,))],
        cost_estimate=small_cost(),
        name="record",
    )(place, in_vmem(y), *[in_hbm(state) for state in states])


def finish(place, states, arrived):
    tokens, width = arrived.shape[1:]

    def kernel(place_ref, forward_in, reverse_in, arrived_ref, forward_ref, reverse_ref, sems):
        del forward_in, reverse_in
        half = pl.ds(pl.multiple_of((1 - place_ref[1]) * width, width), width)
        copies = [
            pltpu.make_async_copy(arrived_ref.at[n], ref.at[:, half], sems.at[n])
            for n, ref in enumerate((forward_ref, reverse_ref))
        ]
        for copy in copies:
            copy.start()
        for copy in copies:
            copy.wait()

    return pl.pallas_call(
        kernel,
        out_shape=tuple(pltpu.HBM(state.shape, state.dtype) for state in states),
        in_specs=[smem()] + [anywhere()] * 3,
        out_specs=(anywhere(),) * 2,
        input_output_aliases={1: 0, 2: 1},
        scratch_shapes=[pltpu.SemaphoreType.DMA((2,))],
        name="finish",
    )(place, *[in_hbm(state) for state in states], in_vmem(arrived))


def slots(routes, experts, capacity):
    flat = routes.reshape(routes.shape[:-2] + (-1,))
    order = jnp.arange(flat.shape[-1], dtype=jnp.int32)
    earlier = (flat[..., :, None] == flat[..., None, :]) & (order[None, :] < order[:, None])
    slot = flat * capacity + jnp.sum(earlier.astype(jnp.int32), axis=-1)
    return slot.reshape(routes.shape)


def shards(tokens_a, tokens_b, routes_a, routes_b, affinity_a, affinity_b, gate_w, up_w, down_w):
    sections = lax.axis_size("pp")
    devices = lax.axis_size("ep")
    experts = devices // 2
    token_count, width = tokens_a.shape
    half_width = width // 2
    capacity = 2 * (token_count * routes_a.shape[2] // devices) + 2
    section = lax.axis_index("pp")
    core = (lax.axis_index("ep") % 2).astype(jnp.int32)
    low = core == 0
    place = jnp.stack([section.astype(jnp.int32), core])
    own_half = core.reshape(1)
    gate, up, down = gate_w[0], up_w[0], down_w[0]

    one_core = [[2 * chip + side for chip in range(experts)] for side in range(2)]
    siblings = [(device, device ^ 1) for device in range(devices)]

    def exchange(wire):
        blocks = wire.reshape(experts, PIECES * capacity, wire.shape[1])
        moved = lax.all_to_all(
            blocks, "ep", split_axis=0, concat_axis=0, tiled=True, axis_index_groups=one_core
        )
        return moved.reshape(wire.shape)

    def to_sibling(block):
        return lax.ppermute(block, "ep", siblings)

    def by_block(mine, theirs):
        return jnp.where(low, mine, theirs), jnp.where(low, theirs, mine)

    def by_moment(pair):
        return jnp.stack([jnp.where(section == m, pair[0], pair[1]) for m in range(sections)])

    target = slots(jnp.stack([routes_a[0], routes_b[0]]), experts, capacity)
    target = by_moment(target)
    affinity = by_moment(jnp.stack([affinity_a[0], affinity_b[0]]))
    target = jnp.stack(by_block(target, to_sibling(target)), axis=1)
    affinity = jnp.stack(by_block(affinity, to_sibling(affinity)), axis=1)
    shift = jnp.arange(PIECES, dtype=jnp.int32)[:, None, None] * (experts * capacity)
    flat = (sections, 2, PIECES * token_count, target.shape[-1])
    columns = (target[:, :, None] + shift).reshape(flat)
    weights = jnp.tile(affinity, (1, 1, PIECES, 1))
    lines = columns.swapaxes(2, 3)

    first = jnp.where(section == 0, tokens_a, tokens_b)
    lower, upper = first[:, :half_width], first[:, half_width:]
    chunks = list(
        by_block(jnp.where(low, lower, upper), to_sibling(jnp.where(low, upper, lower)))
    )

    def leave(i, moment, after=()):
        return dispatch(chunks[i], lines, moment, i, experts, capacity, after)

    def experts_of(wire):
        middle = wire.shape[0] // 2
        others = [to_sibling(wire[:middle]), to_sibling(wire[middle:])]
        hidden = hidden_units(own_half, wire, others, gate, up, capacity)
        return down_rows(own_half, hidden, to_sibling(hidden), down, other_down, capacity)

    states = ()
    first_leaving = leave(0, 0)
    first_wire = exchange(first_leaving)
    other_down = [to_sibling(block) for block in other_half(own_half, down, first_leaving, 4)]
    second_leaving, first_wire, *other_down = tie(leave(1, 0), first_wire, *other_down)
    for moment in range(sections):
        last = sections - 1 - moment
        hop = [(moment, moment + 1), (last, last - 1)]

        def settle(i, back):
            y = combine(chunks[i], back, columns, weights, moment, i, experts, capacity)
            after = record(place, y, states, moment, i, sections)
            if moment + 1 == sections:
                return after, None
            chunks[i] = lax.ppermute(y, "pp", hop)
            return after, leave(i, moment + 1, after[2:])

        second_wire = exchange(second_leaving)
        first_rows = experts_of(first_wire)
        first_rows, second_wire = tie(first_rows, second_wire)
        first_back = exchange(first_rows)
        second_rows = experts_of(second_wire)
        second_rows, first_back = tie(second_rows, first_back)
        second_back = exchange(second_rows)
        states, first_leaving = settle(0, first_back)
        if moment + 1 < sections:
            first_leaving, second_back = tie(first_leaving, second_back)
            first_wire = exchange(first_leaving)
        states, second_leaving = settle(1, second_back)
        if moment + 1 < sections:
            second_leaving, first_wire = tie(second_leaving, first_wire)
    forward, reverse, sent = states
    forward, reverse = finish(place, (forward, reverse), to_sibling(sent))
    return (forward[None], reverse[None])


def solution(mesh):
    placed = (
        P("ep", None),
        P("ep", None),
        P("pp", "ep", None),
        P("pp", "ep", None),
        P("pp", "ep", None),
        P("pp", "ep", None),
        P("pp", None, "ep"),
        P("pp", None, "ep"),
        P("pp", "ep", None),
    )
    return jax.shard_map(
        shards,
        mesh=mesh,
        in_specs=placed,
        out_specs=(P("pp", "ep", None), P("pp", "ep", None)),
        check_vma=False,
    )
```

```python
import jax
import jax.numpy as jnp
from jax import lax
from jax.experimental import pallas as pl
from jax.experimental.pallas import tpu as pltpu
from jax.sharding import PartitionSpec as P

MIB = 1 << 20
PIECES = 4
GROUP = 8


def vmem():
    return pl.BlockSpec(memory_space=pltpu.VMEM)


def smem():
    return pl.BlockSpec(memory_space=pltpu.SMEM)


def anywhere():
    return pl.BlockSpec(memory_space=pl.ANY)


def whole(array):
    return pl.BlockSpec(array.shape, lambda step: (0,) * len(array.shape))


def in_hbm(block):
    return pltpu.with_memory_space_constraint(block, pltpu.HBM)


def in_vmem(block):
    return pltpu.with_memory_space_constraint(block, pltpu.VMEM)


def params(mib):
    return pltpu.CompilerParams(vmem_limit_bytes=mib * MIB)


def small_cost():
    return pl.CostEstimate(flops=MIB, bytes_accessed=MIB, transcendentals=0)


def spans(width, step=256):
    return [slice(start, min(start + step, width)) for start in range(0, width, step)]


def split(index, size, count):
    factor = -(-(1 << 16) // size)
    assert all((n * factor) >> 16 == n // size for n in range(size * count))
    high = (index * factor) >> 16
    return high, index - high * size


def wire_codes(shape, axis, experts, capacity):
    index = lax.broadcasted_iota(jnp.int32, shape, axis)
    expert, rest = split(index, PIECES * capacity, experts)
    piece, slot = split(rest, capacity, PIECES)
    return (piece * experts + expert) * capacity + slot


def group_order(axis, capacity):
    size = GROUP * PIECES * capacity
    shape = (1, size) if axis == 1 else (size, 1)
    index = lax.broadcasted_iota(jnp.int32, shape, axis)
    chip, rest = split(index, PIECES * capacity, GROUP)
    piece, slot = split(rest, capacity, PIECES)
    place = (piece * GROUP + chip) * capacity + slot
    other = lax.broadcasted_iota(jnp.int32, (size, size), 1 - axis)
    return jnp.where(other == place, 1.0, 0.0).astype(jnp.bfloat16)


def tie_kernel(*refs):
    del refs


def tie(*blocks):
    return pl.pallas_call(
        tie_kernel,
        out_shape=tuple(pltpu.HBM(x.shape, x.dtype) for x in blocks),
        in_specs=[anywhere()] * len(blocks),
        out_specs=(anywhere(),) * len(blocks),
        input_output_aliases={n: n for n in range(len(blocks))},
        cost_estimate=pl.CostEstimate(flops=0, bytes_accessed=0, transcendentals=0),
        name="tie",
    )(*[in_hbm(x) for x in blocks])


def dispatch(x, lines, moment, block, experts, capacity, after=()):
    tokens, width = x.shape
    part = width // PIECES
    wire = experts * PIECES * capacity
    count = PIECES * tokens

    groups = 4
    lines_each = wire // groups

    def kernel(x_ref, line_ref, *rest):
        out_ref, stacked, ready, sems = rest[-4:]
        for piece in range(PIECES):
            stacked[piece * tokens : (piece + 1) * tokens, :] = x_ref[
                :, piece * part : (piece + 1) * part
            ]
        lines = line_ref[0, 0]

        def write(group):
            where = pl.ds(pl.multiple_of(group * lines_each, lines_each), lines_each)
            return pltpu.make_async_copy(ready.at[where], out_ref.at[where], sems.at[group])

        def work(group, _):
            rows = wire_codes((lines_each, 1), 0, experts, capacity)
            rows += group * (experts // groups * capacity)
            hit = (rows == lines[0:1, :]) | (rows == lines[1:2, :])
            select = jnp.where(hit, 1.0, 0.0).astype(jnp.bfloat16)
            place = pl.ds(pl.multiple_of(group * lines_each, lines_each), lines_each)
            for columns in spans(part):
                ready[place, columns] = jnp.dot(
                    select, stacked[:, columns], preferred_element_type=jnp.float32
                ).astype(jnp.bfloat16)
            write(group).start()
            return _

        lax.fori_loop(0, groups, work, 0)
        for group in range(groups):
            write(group).wait()

    return pl.pallas_call(
        kernel,
        out_shape=pltpu.HBM((wire, part), jnp.bfloat16),
        grid=(1,),
        in_specs=[
            whole(x),
            pl.BlockSpec((1, 1) + lines.shape[2:], lambda step: (moment, block, 0, 0)),
        ]
        + [anywhere()] * len(after),
        out_specs=anywhere(),
        scratch_shapes=[
            pltpu.VMEM((count, part), jnp.bfloat16),
            pltpu.VMEM((wire, part), jnp.bfloat16),
            pltpu.SemaphoreType.DMA((groups,)),
        ],
        compiler_params=params(24),
        cost_estimate=small_cost(),
        name="dispatch",
    )(x, in_hbm(lines), *[in_hbm(block) for block in after])


def half_units(half, wires, gate, up, sums, capacity):
    wire_rows = sum(wire.shape[0] for wire in wires)
    part = wires[0].shape[1]
    rows_count = wire_rows // PIECES
    units = gate.shape[1]
    width = 2 * PIECES * part
    height = GROUP * capacity
    span = PIECES * height
    groups = rows_count // height
    last = sums is not None
    count = len(wires)

    def kernel(half_ref, *refs):
        wire_refs, (gate_ref, up_ref), refs = refs[:count], refs[count : count + 2], refs[count + 2 :]
        if last:
            before, (out_ref, gate_sum, up_sum, squares), refs = refs[:3], refs[3:7], refs[7:]
        else:
            (gate_sum, up_sum, squares), refs = refs[:3], refs[3:]
        held, rows, gate_blocks, up_blocks, wire_sems, gate_sems, up_sems = refs
        half = half_ref[0]
        wire_copies = []
        at = 0
        for number, ref in enumerate(wire_refs):
            lines = pl.ds(at, ref.shape[0])
            wire_copies.append(pltpu.make_async_copy(ref, held.at[lines], wire_sems.at[number]))
            at += ref.shape[0]

        def loads(piece):
            lines = pl.ds(pl.multiple_of((half * PIECES + piece) * part, part), part)
            return (
                pltpu.make_async_copy(gate_ref.at[lines], gate_blocks.at[piece], gate_sems.at[piece]),
                pltpu.make_async_copy(up_ref.at[lines], up_blocks.at[piece], up_sems.at[piece]),
            )

        for copy in wire_copies:
            copy.start()
        for piece in range(PIECES):
            for copy in loads(piece):
                copy.start()
        if last:
            gate_sum[...], up_sum[...], squares[...] = (ref[...] for ref in before)
        else:
            gate_sum[...] = jnp.zeros_like(gate_sum)
            up_sum[...] = jnp.zeros_like(up_sum)
            squares[...] = jnp.zeros_like(squares)
        order = group_order(1, capacity)
        for copy in wire_copies:
            copy.wait()

        def reorder(group, _):
            lines = pl.ds(pl.multiple_of(group * span, span), span)
            target = pl.ds(pl.multiple_of(group * height, height), height)
            for columns in spans(part):
                ordered = jnp.dot(
                    order, held[lines, columns], preferred_element_type=jnp.float32
                ).astype(jnp.bfloat16)
                for piece in range(PIECES):
                    rows[piece, target, columns] = ordered[piece * height : (piece + 1) * height]
            return _

        lax.fori_loop(0, groups, reorder, 0)

        def work(piece, _):
            for copy in loads(piece):
                copy.wait()
            values = rows[piece]
            gate_sum[...] += jnp.dot(values, gate_blocks[piece], preferred_element_type=jnp.float32)
            up_sum[...] += jnp.dot(values, up_blocks[piece], preferred_element_type=jnp.float32)
            total = squares[...]
            for columns in spans(part, 128):
                few = values[:, columns].astype(jnp.float32)
                total += few * few
            squares[...] = total
            return _

        lax.fori_loop(0, PIECES, work, 0)
        if last:
            mean = jnp.sum(squares[...], axis=-1, keepdims=True) / width
            scale = lax.rsqrt(mean + 1e-06)
            out_ref[...] = (jax.nn.silu(gate_sum[...] * scale) * (up_sum[...] * scale)).astype(
                jnp.bfloat16
            )

    totals = (
        jax.ShapeDtypeStruct((rows_count, units), jnp.float32),
        jax.ShapeDtypeStruct((rows_count, units), jnp.float32),
        jax.ShapeDtypeStruct((rows_count, 128), jnp.float32),
    )
    scratch = [
        pltpu.VMEM((wire_rows, part), jnp.bfloat16),
        pltpu.VMEM((PIECES, rows_count, part), jnp.bfloat16),
        pltpu.VMEM((PIECES, part, units), jnp.bfloat16),
        pltpu.VMEM((PIECES, part, units), jnp.bfloat16),
        pltpu.SemaphoreType.DMA((count,)),
        pltpu.SemaphoreType.DMA((PIECES,)),
        pltpu.SemaphoreType.DMA((PIECES,)),
    ]
    if last:
        scratch = [pltpu.VMEM(total.shape, total.dtype) for total in totals] + scratch
    return pl.pallas_call(
        kernel,
        out_shape=jax.ShapeDtypeStruct((rows_count, units), jnp.bfloat16) if last else totals,
        in_specs=[smem()] + [anywhere()] * (count + 2) + [vmem()] * (3 if last else 0),
        out_specs=vmem() if last else (vmem(),) * 3,
        scratch_shapes=scratch,
        compiler_params=params(32),
        cost_estimate=small_cost(),
        name="hidden_units" if last else "own_half_sums",
    )(half, *wires, in_hbm(gate), in_hbm(up), *(sums or ()))


def down_rows(core, hidden, other_hidden, down, other_down, capacity):
    rows, units = hidden.shape
    lines_each, half_width = other_down[0].shape
    blocks_count = len(other_down)
    part = half_width // PIECES
    height = GROUP * capacity
    span = PIECES * height
    groups = rows // height

    def kernel(
        core_ref, hidden_ref, other_ref, down_ref, *rest
    ):
        other_down_refs, rest = rest[:blocks_count], rest[blocks_count:]
        out_ref, blocks, other_blocks, stacked, ready, sems, other_sems, out_sems = rest
        core = core_ref[0]

        def loads(piece):
            place = pl.ds(pl.multiple_of((core * PIECES + piece) * part, part), part)
            columns = pl.ds(pl.multiple_of(piece * part, part), part)
            return [
                pltpu.make_async_copy(down_ref.at[:, place], blocks.at[piece], sems.at[piece])
            ] + [
                pltpu.make_async_copy(
                    ref.at[:, columns],
                    other_blocks.at[piece, pl.ds(number * lines_each, lines_each)],
                    other_sems.at[piece, number],
                )
                for number, ref in enumerate(other_down_refs)
            ]

        for piece in range(PIECES):
            for copy in loads(piece):
                copy.start()
        order = group_order(0, capacity)

        def work(piece, _):
            for copy in loads(piece):
                copy.wait()
            total = jnp.dot(hidden_ref[...], blocks[piece], preferred_element_type=jnp.float32)
            total += jnp.dot(
                other_ref[...], other_blocks[piece], preferred_element_type=jnp.float32
            )
            total = total.astype(jnp.bfloat16)
            for group in range(groups):
                at = pl.ds(pl.multiple_of(group * span + piece * height, height), height)
                stacked[at, :] = total[group * height : (group + 1) * height]
            return _

        lax.fori_loop(0, PIECES, work, 0)

        def write(group):
            where = pl.ds(pl.multiple_of(group * span, span), span)
            return pltpu.make_async_copy(ready.at[where], out_ref.at[where], out_sems.at[group])

        def arrange(group, _):
            lines = pl.ds(pl.multiple_of(group * span, span), span)
            for columns in spans(part):
                ready[lines, columns] = jnp.dot(
                    order, stacked[lines, columns], preferred_element_type=jnp.float32
                ).astype(jnp.bfloat16)
            write(group).start()
            return _

        lax.fori_loop(0, groups, arrange, 0)
        copies = [write(group) for group in range(groups)]
        for copy in copies:
            copy.wait()

    return pl.pallas_call(
        kernel,
        out_shape=pltpu.HBM((rows * PIECES, part), jnp.bfloat16),
        in_specs=[smem(), vmem(), vmem()] + [anywhere()] * (1 + blocks_count),
        out_specs=anywhere(),
        scratch_shapes=[
            pltpu.VMEM((PIECES, units, part), jnp.bfloat16),
            pltpu.VMEM((PIECES, units, part), jnp.bfloat16),
            pltpu.VMEM((rows * PIECES, part), jnp.bfloat16),
            pltpu.VMEM((rows * PIECES, part), jnp.bfloat16),
            pltpu.SemaphoreType.DMA((PIECES,)),
            pltpu.SemaphoreType.DMA((PIECES, blocks_count)),
            pltpu.SemaphoreType.DMA((groups,)),
        ],
        compiler_params=params(40),
        cost_estimate=small_cost(),
        name="down_rows",
    )(core, hidden, other_hidden, in_hbm(down), *[in_hbm(block) for block in other_down])


def other_half(core, down, after, count):
    units, width = down.shape
    half_width = width // 2
    height = units // count

    def kernel(core_ref, down_ref, after_ref, *rest):
        del after_ref
        outs, sems = rest[:-1], rest[-1]
        place = pl.ds(pl.multiple_of((1 - core_ref[0]) * half_width, half_width), half_width)
        copies = [
            pltpu.make_async_copy(
                down_ref.at[pl.ds(number * height, height), place], out, sems.at[number]
            )
            for number, out in enumerate(outs)
        ]
        for copy in copies:
            copy.start()
        for copy in copies:
            copy.wait()

    return pl.pallas_call(
        kernel,
        out_shape=(jax.ShapeDtypeStruct((height, half_width), down.dtype),) * count,
        in_specs=[smem()] + [anywhere()] * 2,
        out_specs=(vmem(),) * count,
        scratch_shapes=[pltpu.SemaphoreType.DMA((count,))],
        compiler_params=params(24),
        cost_estimate=small_cost(),
        name="other_half",
    )(core, in_hbm(down), in_hbm(after))


def combine(x, wire, columns, weights, moment, block, experts, capacity):
    tokens, width = x.shape
    part = width // PIECES
    count = PIECES * tokens
    wire_rows = wire.shape[0]

    def kernel(x_ref, wire_ref, column_ref, weight_ref, y_ref, factors):
        rows = wire_codes((1, wire_rows), 1, experts, capacity)
        codes, shares = column_ref[0, 0], weight_ref[0, 0]
        table = jnp.where(rows == codes[:, 0:1], shares[:, 0:1], 0.0)
        table += jnp.where(rows == codes[:, 1:2], shares[:, 1:2], 0.0)
        high = table.astype(jnp.bfloat16)
        factors[:count, :] = high
        factors[count:, :] = (table - high.astype(jnp.float32)).astype(jnp.bfloat16)
        for lanes in spans(part):
            both = jnp.dot(factors[...], wire_ref[:, lanes], preferred_element_type=jnp.float32)
            total = both[:count, :] + both[count:, :]
            for piece in range(PIECES):
                target = slice(piece * part + lanes.start, piece * part + lanes.stop)
                y_ref[:, target] = (
                    x_ref[:, target].astype(jnp.float32) + total[piece * tokens : (piece + 1) * tokens]
                ).astype(jnp.bfloat16)

    per_block = lambda array: pl.BlockSpec(
        (1, 1) + array.shape[2:], lambda step: (moment, block, 0, 0)
    )
    return pl.pallas_call(
        kernel,
        out_shape=jax.ShapeDtypeStruct((tokens, width), x.dtype),
        grid=(1,),
        in_specs=[whole(x), whole(wire), per_block(columns), per_block(weights)],
        out_specs=pl.BlockSpec((tokens, width), lambda step: (0, 0)),
        scratch_shapes=[pltpu.VMEM((2 * count, wire_rows), jnp.bfloat16)],
        compiler_params=params(24),
        cost_estimate=small_cost(),
        name="combine",
    )(in_hbm(x), in_hbm(wire), in_hbm(columns), in_hbm(weights))


def record(place, y, states, moment, block, sections):
    tokens, width = y.shape

    def kernel(place_ref, y_ref, *rest):
        forward_ref, reverse_ref, sent_ref, sems = rest[-4:]
        section, core = place_ref[0], place_ref[1]
        for number, (state_ref, turn) in enumerate(
            ((forward_ref, moment), (reverse_ref, sections - 1 - moment))
        ):

            @pl.when((section == turn) & (core == block))
            def _():
                half = pl.ds(block * width, width)
                copy = pltpu.make_async_copy(y_ref, state_ref.at[:, half], sems.at[number])
                copy.start()
                copy.wait()

            @pl.when((section == turn) & (core != block))
            def _():
                copy = pltpu.make_async_copy(y_ref, sent_ref.at[number], sems.at[number])
                copy.start()
                copy.wait()

    result = pltpu.HBM((tokens, 2 * width), y.dtype)
    return pl.pallas_call(
        kernel,
        out_shape=(result, result, pltpu.HBM((2, tokens, width), y.dtype)),
        in_specs=[smem()] + [anywhere()] * (1 + len(states)),
        out_specs=(anywhere(),) * 3,
        input_output_aliases={2 + n: n for n in range(len(states))},
        scratch_shapes=[pltpu.SemaphoreType.DMA((2,))],
        cost_estimate=small_cost(),
        name="record",
    )(place, in_vmem(y), *[in_hbm(state) for state in states])


def finish(place, states, arrived):
    tokens, width = arrived.shape[1:]

    def kernel(place_ref, forward_in, reverse_in, arrived_ref, forward_ref, reverse_ref, sems):
        del forward_in, reverse_in
        half = pl.ds(pl.multiple_of((1 - place_ref[1]) * width, width), width)
        copies = [
            pltpu.make_async_copy(arrived_ref.at[n], ref.at[:, half], sems.at[n])
            for n, ref in enumerate((forward_ref, reverse_ref))
        ]
        for copy in copies:
            copy.start()
        for copy in copies:
            copy.wait()

    return pl.pallas_call(
        kernel,
        out_shape=tuple(pltpu.HBM(state.shape, state.dtype) for state in states),
        in_specs=[smem()] + [anywhere()] * 3,
        out_specs=(anywhere(),) * 2,
        input_output_aliases={1: 0, 2: 1},
        scratch_shapes=[pltpu.SemaphoreType.DMA((2,))],
        name="finish",
    )(place, *[in_hbm(state) for state in states], in_vmem(arrived))


def slots(routes, experts, capacity):
    flat = routes.reshape(routes.shape[:-2] + (-1,))
    order = jnp.arange(flat.shape[-1], dtype=jnp.int32)
    earlier = (flat[..., :, None] == flat[..., None, :]) & (order[None, :] < order[:, None])
    slot = flat * capacity + jnp.sum(earlier.astype(jnp.int32), axis=-1)
    return slot.reshape(routes.shape)


def shards(tokens_a, tokens_b, routes_a, routes_b, affinity_a, affinity_b, gate_w, up_w, down_w):
    sections = lax.axis_size("pp")
    devices = lax.axis_size("ep")
    experts = devices // 2
    token_count, width = tokens_a.shape
    half_width = width // 2
    capacity = 2 * (token_count * routes_a.shape[2] // devices) + 2
    section = lax.axis_index("pp")
    core = (lax.axis_index("ep") % 2).astype(jnp.int32)
    low = core == 0
    place = jnp.stack([section.astype(jnp.int32), core])
    own_half = core.reshape(1)
    gate, up, down = gate_w[0], up_w[0], down_w[0]

    one_core = [[2 * chip + side for chip in range(experts)] for side in range(2)]
    siblings = [(device, device ^ 1) for device in range(devices)]

    def exchange(wire):
        blocks = wire.reshape(experts, PIECES * capacity, wire.shape[1])
        moved = lax.all_to_all(
            blocks, "ep", split_axis=0, concat_axis=0, tiled=True, axis_index_groups=one_core
        )
        return moved.reshape(wire.shape)

    def to_sibling(block):
        return lax.ppermute(block, "ep", siblings)

    def by_block(mine, theirs):
        return jnp.where(low, mine, theirs), jnp.where(low, theirs, mine)

    def by_moment(pair):
        return jnp.stack([jnp.where(section == m, pair[0], pair[1]) for m in range(sections)])

    target = slots(jnp.stack([routes_a[0], routes_b[0]]), experts, capacity)
    target = by_moment(target)
    affinity = by_moment(jnp.stack([affinity_a[0], affinity_b[0]]))
    target = jnp.stack(by_block(target, to_sibling(target)), axis=1)
    affinity = jnp.stack(by_block(affinity, to_sibling(affinity)), axis=1)
    shift = jnp.arange(PIECES, dtype=jnp.int32)[:, None, None] * (experts * capacity)
    flat = (sections, 2, PIECES * token_count, target.shape[-1])
    columns = (target[:, :, None] + shift).reshape(flat)
    weights = jnp.tile(affinity, (1, 1, PIECES, 1))
    lines = columns.swapaxes(2, 3)

    first = jnp.where(section == 0, tokens_a, tokens_b)
    lower, upper = first[:, :half_width], first[:, half_width:]
    chunks = list(
        by_block(jnp.where(low, lower, upper), to_sibling(jnp.where(low, upper, lower)))
    )

    def leave(i, moment, after=()):
        return dispatch(chunks[i], lines, moment, i, experts, capacity, after)

    def experts_of(wire):
        middle = wire.shape[0] // 2
        others = [to_sibling(wire[:middle]), to_sibling(wire[middle:])]
        sums = half_units(own_half, [in_hbm(wire)], gate, up, None, capacity)
        hidden = half_units(1 - own_half, others, gate, up, sums, capacity)
        return down_rows(own_half, hidden, to_sibling(hidden), down, other_down, capacity)

    states = ()
    first_leaving = leave(0, 0)
    first_wire = exchange(first_leaving)
    other_down = [to_sibling(block) for block in other_half(own_half, down, first_leaving, 4)]
    second_leaving, first_wire, columns, weights, *other_down = tie(
        leave(1, 0), first_wire, columns, weights, *other_down
    )
    for moment in range(sections):
        last = sections - 1 - moment
        hop = [(moment, moment + 1), (last, last - 1)]

        def settle(i, back):
            y = combine(chunks[i], back, columns, weights, moment, i, experts, capacity)
            after = record(place, y, states, moment, i, sections)
            if moment + 1 == sections:
                return after, None
            chunks[i] = lax.ppermute(y, "pp", hop)
            return after, leave(i, moment + 1, after[2:])

        second_wire = exchange(second_leaving)
        first_rows = experts_of(first_wire)
        first_rows, second_wire = tie(first_rows, second_wire)
        first_back = exchange(first_rows)
        second_rows = experts_of(second_wire)
        second_rows, first_back = tie(second_rows, first_back)
        second_back = exchange(second_rows)
        states, first_leaving = settle(0, first_back)
        if moment + 1 < sections:
            first_leaving, second_back = tie(first_leaving, second_back)
            first_wire = exchange(first_leaving)
        states, second_leaving = settle(1, second_back)
        if moment + 1 < sections:
            second_leaving, first_wire = tie(second_leaving, first_wire)
    forward, reverse, sent = states
    forward, reverse = finish(place, (forward, reverse), to_sibling(sent))
    return (forward[None], reverse[None])


def solution(mesh):
    placed = (
        P("ep", None),
        P("ep", None),
        P("pp", "ep", None),
        P("pp", "ep", None),
        P("pp", "ep", None),
        P("pp", "ep", None),
        P("pp", None, "ep"),
        P("pp", None, "ep"),
        P("pp", "ep", None),
    )
    return jax.shard_map(
        shards,
        mesh=mesh,
        in_specs=placed,
        out_specs=(P("pp", "ep", None), P("pp", "ep", None)),
        check_vma=False,
    )
```

```python
import jax
import jax.numpy as jnp
from jax import lax
from jax.experimental import pallas as pl
from jax.experimental.pallas import tpu as pltpu
from jax.sharding import PartitionSpec as P

MIB = 1 << 20
PIECES = 4
GROUP = 8


def vmem():
    return pl.BlockSpec(memory_space=pltpu.VMEM)


def smem():
    return pl.BlockSpec(memory_space=pltpu.SMEM)


def anywhere():
    return pl.BlockSpec(memory_space=pl.ANY)


def whole(array):
    return pl.BlockSpec(array.shape, lambda step: (0,) * len(array.shape))


def in_hbm(block):
    return pltpu.with_memory_space_constraint(block, pltpu.HBM)


def in_vmem(block):
    return pltpu.with_memory_space_constraint(block, pltpu.VMEM)


def params(mib):
    return pltpu.CompilerParams(vmem_limit_bytes=mib * MIB)


def small_cost():
    return pl.CostEstimate(flops=MIB, bytes_accessed=MIB, transcendentals=0)


def spans(width, step=256):
    return [slice(start, min(start + step, width)) for start in range(0, width, step)]


def split(index, size, count):
    factor = -(-(1 << 16) // size)
    assert all((n * factor) >> 16 == n // size for n in range(size * count))
    high = (index * factor) >> 16
    return high, index - high * size


def wire_codes(shape, axis, experts, capacity):
    index = lax.broadcasted_iota(jnp.int32, shape, axis)
    expert, rest = split(index, PIECES * capacity, experts)
    piece, slot = split(rest, capacity, PIECES)
    return (piece * experts + expert) * capacity + slot


def group_order(axis, capacity):
    size = GROUP * PIECES * capacity
    shape = (1, size) if axis == 1 else (size, 1)
    index = lax.broadcasted_iota(jnp.int32, shape, axis)
    chip, rest = split(index, PIECES * capacity, GROUP)
    piece, slot = split(rest, capacity, PIECES)
    place = (piece * GROUP + chip) * capacity + slot
    other = lax.broadcasted_iota(jnp.int32, (size, size), 1 - axis)
    return jnp.where(other == place, 1.0, 0.0).astype(jnp.bfloat16)


def tie_kernel(*refs):
    del refs


def tie(blocks, after):
    return pl.pallas_call(
        tie_kernel,
        out_shape=tuple(pltpu.HBM(x.shape, x.dtype) for x in blocks),
        in_specs=[anywhere()] * (len(blocks) + 1),
        out_specs=(anywhere(),) * len(blocks),
        input_output_aliases={n: n for n in range(len(blocks))},
        cost_estimate=pl.CostEstimate(flops=0, bytes_accessed=0, transcendentals=0),
        name="tie",
    )(*[in_hbm(x) for x in blocks], after)


def dispatch(x, lines, moment, block, experts, capacity, after=()):
    tokens, width = x.shape
    part = width // PIECES
    wire = experts * PIECES * capacity
    count = PIECES * tokens

    groups = 4
    lines_each = wire // groups

    def kernel(x_ref, line_ref, *rest):
        out_ref, stacked, ready, sems = rest[-4:]
        for piece in range(PIECES):
            stacked[piece * tokens : (piece + 1) * tokens, :] = x_ref[
                :, piece * part : (piece + 1) * part
            ]
        lines = line_ref[0, 0]
        codes = wire_codes((wire, 1), 0, experts, capacity)
        copies = []
        for group in range(groups):
            place = slice(group * lines_each, (group + 1) * lines_each)
            rows = codes[place]
            hit = (rows == lines[0:1, :]) | (rows == lines[1:2, :])
            select = jnp.where(hit, 1.0, 0.0).astype(jnp.bfloat16)
            for columns in spans(part):
                ready[place, columns] = jnp.dot(
                    select, stacked[:, columns], preferred_element_type=jnp.float32
                ).astype(jnp.bfloat16)
            where = pl.ds(group * lines_each, lines_each)
            copies.append(
                pltpu.make_async_copy(ready.at[where], out_ref.at[where], sems.at[group])
            )
            copies[-1].start()
        for copy in copies:
            copy.wait()

    return pl.pallas_call(
        kernel,
        out_shape=pltpu.HBM((wire, part), jnp.bfloat16),
        grid=(1,),
        in_specs=[
            whole(x),
            pl.BlockSpec((1, 1) + lines.shape[2:], lambda step: (moment, block, 0, 0)),
        ]
        + [anywhere()] * len(after),
        out_specs=anywhere(),
        scratch_shapes=[
            pltpu.VMEM((count, part), jnp.bfloat16),
            pltpu.VMEM((wire, part), jnp.bfloat16),
            pltpu.SemaphoreType.DMA((groups,)),
        ],
        compiler_params=params(24),
        cost_estimate=small_cost(),
        name="dispatch",
    )(x, in_hbm(lines), *[in_hbm(block) for block in after])


def load_half(core, gate, up, after, part):
    units = gate.shape[1]

    def kernel(core_ref, gate_ref, up_ref, after_ref, gate_out, up_out, sems):
        del after_ref
        copies = []
        for piece in range(PIECES):
            lines = pl.ds(pl.multiple_of((core_ref[0] * PIECES + piece) * part, part), part)
            for number, (ref, out) in enumerate(((gate_ref, gate_out), (up_ref, up_out))):
                copies.append(
                    pltpu.make_async_copy(ref.at[lines], out.at[piece], sems.at[number, piece])
                )
        for copy in copies:
            copy.start()
        for copy in copies:
            copy.wait()

    return pl.pallas_call(
        kernel,
        out_shape=(jax.ShapeDtypeStruct((PIECES, part, units), gate.dtype),) * 2,
        in_specs=[smem()] + [anywhere()] * 3,
        out_specs=(vmem(),) * 2,
        scratch_shapes=[pltpu.SemaphoreType.DMA((2, PIECES))],
        compiler_params=params(16),
        cost_estimate=small_cost(),
        name="load_half",
    )(core, in_hbm(gate), in_hbm(up), in_hbm(after))


def hidden_units(core, own, others, own_gate, own_up, gate, up, down, other_down, capacity):
    wire_rows, part = own.shape
    rows_count = wire_rows // PIECES
    units = gate.shape[1]
    half_width = PIECES * part
    height = GROUP * capacity
    span = PIECES * height
    groups = rows_count // height

    def kernel(
        core_ref, own_ref, low_ref, high_ref, own_gate_ref, own_up_ref, gate_ref, up_ref,
        down_ref, other_down_ref, out_ref, down_out, other_down_out,
        wires, rows, gate_blocks, up_blocks, gate_sum, up_sum,
        wire_sems, gate_sems, up_sems, down_sems,
    ):
        core = core_ref[0]
        middle = wire_rows // 2
        wire_copies = [
            pltpu.make_async_copy(own_ref, wires.at[pl.ds(0, wire_rows)], wire_sems.at[0]),
            pltpu.make_async_copy(low_ref, wires.at[pl.ds(wire_rows, middle)], wire_sems.at[1]),
            pltpu.make_async_copy(
                high_ref, wires.at[pl.ds(wire_rows + middle, middle)], wire_sems.at[2]
            ),
        ]
        loads = []
        down_loads = []
        for piece in range(PIECES):
            lines = pl.ds(pl.multiple_of(((1 - core) * PIECES + piece) * part, part), part)
            loads += [
                pltpu.make_async_copy(gate_ref.at[lines], gate_blocks.at[piece], gate_sems.at[piece]),
                pltpu.make_async_copy(up_ref.at[lines], up_blocks.at[piece], up_sems.at[piece]),
            ]
            place = pl.ds(pl.multiple_of((core * PIECES + piece) * part, part), part)
            down_loads += [
                pltpu.make_async_copy(
                    down_ref.at[:, place], down_out.at[piece], down_sems.at[0, piece]
                ),
                pltpu.make_async_copy(
                    other_down_ref.at[:, pl.ds(piece * part, part)],
                    other_down_out.at[piece],
                    down_sems.at[1, piece],
                ),
            ]
        for copy in wire_copies + loads:
            copy.start()
        order = group_order(1, capacity)
        squares = 0.0
        for step in range(2 * PIECES):
            piece = step % PIECES
            mine = step < PIECES
            if piece == 0:
                base = 0 if mine else wire_rows
                for copy in wire_copies[:1] if mine else wire_copies[1:]:
                    copy.wait()
                for group in range(groups):
                    for columns in spans(part):
                        ordered = jnp.dot(
                            order,
                            wires[base + group * span : base + (group + 1) * span, columns],
                            preferred_element_type=jnp.float32,
                        ).astype(jnp.bfloat16)
                        for number in range(PIECES):
                            rows[
                                group * height : (group + 1) * height,
                                number * part + columns.start : number * part + columns.stop,
                            ] = ordered[number * height : (number + 1) * height]
            if mine:
                down_loads[2 * piece].start()
                down_loads[2 * piece + 1].start()
                gate_block, up_block = own_gate_ref[piece], own_up_ref[piece]
            else:
                loads[2 * piece].wait()
                loads[2 * piece + 1].wait()
                gate_block, up_block = gate_blocks[piece], up_blocks[piece]
            values = rows[:, piece * part : (piece + 1) * part]
            gate = jnp.dot(values, gate_block, preferred_element_type=jnp.float32)
            up = jnp.dot(values, up_block, preferred_element_type=jnp.float32)
            if step == 0:
                gate_sum[...], up_sum[...] = gate, up
            else:
                gate_sum[...] += gate
                up_sum[...] += up
            for columns in spans(part, 128):
                few = values[:, columns].astype(jnp.float32)
                squares += few * few
        mean = jnp.sum(squares, axis=-1, keepdims=True) / (2 * half_width)
        scale = lax.rsqrt(mean + 1e-06)
        out_ref[...] = (jax.nn.silu(gate_sum[...] * scale) * (up_sum[...] * scale)).astype(
            jnp.bfloat16
        )
        for copy in down_loads:
            copy.wait()

    blocks = jax.ShapeDtypeStruct((PIECES, units, part), down.dtype)
    return pl.pallas_call(
        kernel,
        out_shape=(jax.ShapeDtypeStruct((rows_count, units), jnp.bfloat16), blocks, blocks),
        in_specs=[smem()] + [anywhere()] * 3 + [vmem()] * 2 + [anywhere()] * 4,
        out_specs=(vmem(),) * 3,
        scratch_shapes=[
            pltpu.VMEM((2 * wire_rows, part), jnp.bfloat16),
            pltpu.VMEM((rows_count, half_width), jnp.bfloat16),
            pltpu.VMEM((PIECES, part, units), jnp.bfloat16),
            pltpu.VMEM((PIECES, part, units), jnp.bfloat16),
            pltpu.VMEM((rows_count, units), jnp.float32),
            pltpu.VMEM((rows_count, units), jnp.float32),
            pltpu.SemaphoreType.DMA((3,)),
            pltpu.SemaphoreType.DMA((PIECES,)),
            pltpu.SemaphoreType.DMA((PIECES,)),
            pltpu.SemaphoreType.DMA((2, PIECES)),
        ],
        compiler_params=params(32),
        cost_estimate=small_cost(),
        name="hidden_units",
    )(
        core, in_hbm(own), *others, own_gate, own_up,
        *[in_hbm(block) for block in (gate, up, down, other_down)],
    )


def down_rows(hidden, other_hidden, blocks, other_blocks, capacity):
    rows, units = hidden.shape
    part = blocks.shape[2]
    height = GROUP * capacity
    span = PIECES * height
    groups = rows // height

    def kernel(
        hidden_ref, other_ref, blocks_ref, other_blocks_ref, out_ref, stacked, ready, out_sems
    ):
        order = group_order(0, capacity)
        for piece in range(PIECES):
            total = jnp.dot(hidden_ref[...], blocks_ref[piece], preferred_element_type=jnp.float32)
            total += jnp.dot(
                other_ref[...], other_blocks_ref[piece], preferred_element_type=jnp.float32
            )
            total = total.astype(jnp.bfloat16)
            for group in range(groups):
                at = group * span + piece * height
                stacked[at : at + height, :] = total[group * height : (group + 1) * height]
        copies = []
        for group in range(groups):
            lines = slice(group * span, (group + 1) * span)
            for columns in spans(part):
                ready[lines, columns] = jnp.dot(
                    order, stacked[lines, columns], preferred_element_type=jnp.float32
                ).astype(jnp.bfloat16)
            where = pl.ds(group * span, span)
            copies.append(
                pltpu.make_async_copy(ready.at[where], out_ref.at[where], out_sems.at[group])
            )
            copies[-1].start()
        for copy in copies:
            copy.wait()

    return pl.pallas_call(
        kernel,
        out_shape=pltpu.HBM((rows * PIECES, part), jnp.bfloat16),
        in_specs=[vmem()] * 4,
        out_specs=anywhere(),
        scratch_shapes=[
            pltpu.VMEM((rows * PIECES, part), jnp.bfloat16),
            pltpu.VMEM((rows * PIECES, part), jnp.bfloat16),
            pltpu.SemaphoreType.DMA((groups,)),
        ],
        compiler_params=params(24),
        cost_estimate=small_cost(),
        name="down_rows",
    )(hidden, other_hidden, blocks, other_blocks)


def other_half(core, down, after, count):
    units, width = down.shape
    half_width = width // 2
    height = units // count

    def kernel(core_ref, down_ref, after_ref, *rest):
        del after_ref
        outs, sems = rest[:-1], rest[-1]
        place = pl.ds(pl.multiple_of((1 - core_ref[0]) * half_width, half_width), half_width)
        copies = [
            pltpu.make_async_copy(
                down_ref.at[pl.ds(number * height, height), place], out, sems.at[number]
            )
            for number, out in enumerate(outs)
        ]
        for copy in copies:
            copy.start()
        for copy in copies:
            copy.wait()

    return pl.pallas_call(
        kernel,
        out_shape=(jax.ShapeDtypeStruct((height, half_width), down.dtype),) * count,
        in_specs=[smem()] + [anywhere()] * 2,
        out_specs=(vmem(),) * count,
        scratch_shapes=[pltpu.SemaphoreType.DMA((count,))],
        compiler_params=params(24),
        cost_estimate=small_cost(),
        name="other_half",
    )(core, in_hbm(down), in_hbm(after))


def combine(x, wire, columns, weights, moment, block, experts, capacity):
    tokens, width = x.shape
    part = width // PIECES
    count = PIECES * tokens
    wire_rows = wire.shape[0]

    def kernel(x_ref, wire_ref, column_ref, weight_ref, y_ref, factors):
        rows = wire_codes((1, wire_rows), 1, experts, capacity)
        codes, shares = column_ref[0, 0], weight_ref[0, 0]
        table = jnp.where(rows == codes[:, 0:1], shares[:, 0:1], 0.0)
        table += jnp.where(rows == codes[:, 1:2], shares[:, 1:2], 0.0)
        high = table.astype(jnp.bfloat16)
        factors[:count, :] = high
        factors[count:, :] = (table - high.astype(jnp.float32)).astype(jnp.bfloat16)
        for lanes in spans(part):
            both = jnp.dot(factors[...], wire_ref[:, lanes], preferred_element_type=jnp.float32)
            total = both[:count, :] + both[count:, :]
            for piece in range(PIECES):
                target = slice(piece * part + lanes.start, piece * part + lanes.stop)
                y_ref[:, target] = (
                    x_ref[:, target].astype(jnp.float32) + total[piece * tokens : (piece + 1) * tokens]
                ).astype(jnp.bfloat16)

    per_block = lambda array: pl.BlockSpec(
        (1, 1) + array.shape[2:], lambda step: (moment, block, 0, 0)
    )
    return pl.pallas_call(
        kernel,
        out_shape=jax.ShapeDtypeStruct((tokens, width), x.dtype),
        grid=(1,),
        in_specs=[whole(x), whole(wire), per_block(columns), per_block(weights)],
        out_specs=pl.BlockSpec((tokens, width), lambda step: (0, 0)),
        scratch_shapes=[pltpu.VMEM((2 * count, wire_rows), jnp.bfloat16)],
        compiler_params=params(24),
        cost_estimate=small_cost(),
        name="combine",
    )(in_hbm(x), in_hbm(wire), in_hbm(columns), in_hbm(weights))


def record(place, y, states, moment, block, sections):
    tokens, width = y.shape

    def kernel(place_ref, y_ref, *rest):
        forward_ref, reverse_ref, sent_ref, sems = rest[-4:]
        section, core = place_ref[0], place_ref[1]
        for number, (state_ref, turn) in enumerate(
            ((forward_ref, moment), (reverse_ref, sections - 1 - moment))
        ):

            @pl.when((section == turn) & (core == block))
            def _():
                half = pl.ds(block * width, width)
                copy = pltpu.make_async_copy(y_ref, state_ref.at[:, half], sems.at[number])
                copy.start()
                copy.wait()

            @pl.when((section == turn) & (core != block))
            def _():
                copy = pltpu.make_async_copy(y_ref, sent_ref.at[number], sems.at[number])
                copy.start()
                copy.wait()

    result = pltpu.HBM((tokens, 2 * width), y.dtype)
    return pl.pallas_call(
        kernel,
        out_shape=(result, result, pltpu.HBM((2, tokens, width), y.dtype)),
        in_specs=[smem()] + [anywhere()] * (1 + len(states)),
        out_specs=(anywhere(),) * 3,
        input_output_aliases={2 + n: n for n in range(len(states))},
        scratch_shapes=[pltpu.SemaphoreType.DMA((2,))],
        cost_estimate=small_cost(),
        name="record",
    )(place, in_vmem(y), *[in_hbm(state) for state in states])


def finish(place, states, arrived):
    tokens, width = arrived.shape[1:]

    def kernel(place_ref, forward_in, reverse_in, arrived_ref, forward_ref, reverse_ref, sems):
        del forward_in, reverse_in
        half = pl.ds(pl.multiple_of((1 - place_ref[1]) * width, width), width)
        copies = [
            pltpu.make_async_copy(arrived_ref.at[n], ref.at[:, half], sems.at[n])
            for n, ref in enumerate((forward_ref, reverse_ref))
        ]
        for copy in copies:
            copy.start()
        for copy in copies:
            copy.wait()

    return pl.pallas_call(
        kernel,
        out_shape=tuple(pltpu.HBM(state.shape, state.dtype) for state in states),
        in_specs=[smem()] + [anywhere()] * 3,
        out_specs=(anywhere(),) * 2,
        input_output_aliases={1: 0, 2: 1},
        scratch_shapes=[pltpu.SemaphoreType.DMA((2,))],
        name="finish",
    )(place, *[in_hbm(state) for state in states], in_vmem(arrived))


def slots(routes, experts, capacity):
    flat = routes.reshape(routes.shape[:-2] + (-1,))
    order = jnp.arange(flat.shape[-1], dtype=jnp.int32)
    earlier = (flat[..., :, None] == flat[..., None, :]) & (order[None, :] < order[:, None])
    slot = flat * capacity + jnp.sum(earlier.astype(jnp.int32), axis=-1)
    return slot.reshape(routes.shape)


def shards(tokens_a, tokens_b, routes_a, routes_b, affinity_a, affinity_b, gate_w, up_w, down_w):
    sections = lax.axis_size("pp")
    devices = lax.axis_size("ep")
    experts = devices // 2
    token_count, width = tokens_a.shape
    half_width = width // 2
    capacity = 2 * (token_count * routes_a.shape[2] // devices) + 2
    section = lax.axis_index("pp")
    core = (lax.axis_index("ep") % 2).astype(jnp.int32)
    low = core == 0
    place = jnp.stack([section.astype(jnp.int32), core])
    own_half = core.reshape(1)
    gate, up, down = gate_w[0], up_w[0], down_w[0]

    one_core = [[2 * chip + side for chip in range(experts)] for side in range(2)]
    siblings = [(device, device ^ 1) for device in range(devices)]

    def exchange(wire):
        blocks = wire.reshape(experts, PIECES * capacity, wire.shape[1])
        moved = lax.all_to_all(
            blocks, "ep", split_axis=0, concat_axis=0, tiled=True, axis_index_groups=one_core
        )
        return moved.reshape(wire.shape)

    def to_sibling(block):
        return lax.ppermute(block, "ep", siblings)

    def by_block(mine, theirs):
        return jnp.where(low, mine, theirs), jnp.where(low, theirs, mine)

    def by_moment(pair):
        return jnp.stack([jnp.where(section == m, pair[0], pair[1]) for m in range(sections)])

    target = slots(jnp.stack([routes_a[0], routes_b[0]]), experts, capacity)
    target = by_moment(target)
    affinity = by_moment(jnp.stack([affinity_a[0], affinity_b[0]]))
    target = jnp.stack(by_block(target, to_sibling(target)), axis=1)
    affinity = jnp.stack(by_block(affinity, to_sibling(affinity)), axis=1)
    shift = jnp.arange(PIECES, dtype=jnp.int32)[:, None, None] * (experts * capacity)
    flat = (sections, 2, PIECES * token_count, target.shape[-1])
    columns = (target[:, :, None] + shift).reshape(flat)
    weights = jnp.tile(affinity, (1, 1, PIECES, 1))
    lines = columns.swapaxes(2, 3)

    first = jnp.where(section == 0, tokens_a, tokens_b)
    lower, upper = first[:, :half_width], first[:, half_width:]
    chunks = list(
        by_block(jnp.where(low, lower, upper), to_sibling(jnp.where(low, upper, lower)))
    )

    def leave(i, moment, after=()):
        return dispatch(chunks[i], lines, moment, i, experts, capacity, after)

    def experts_of(wire):
        middle = wire.shape[0] // 2
        others = [to_sibling(wire[:middle]), to_sibling(wire[middle:])]
        own_gate, own_up = load_half(own_half, gate, up, wire, wire.shape[1])
        hidden, *blocks = hidden_units(
            own_half, wire, others, own_gate, own_up, gate, up, down, other_down, capacity
        )
        return down_rows(hidden, to_sibling(hidden), *blocks, capacity)

    states = ()
    first_leaving = leave(0, 0)
    first_wire = exchange(first_leaving)
    other_down = [to_sibling(block) for block in other_half(own_half, down, first_leaving, 4)]
    second_leaving, columns, weights, other_down = tie(
        (leave(1, 0), columns, weights, jnp.concatenate(other_down)), first_wire
    )
    for moment in range(sections):
        last = sections - 1 - moment
        hop = [(moment, moment + 1), (last, last - 1)]

        def settle(i, back):
            y = combine(chunks[i], back, columns, weights, moment, i, experts, capacity)
            after = record(place, y, states, moment, i, sections)
            if moment + 1 == sections:
                return after, None
            chunks[i] = lax.ppermute(y, "pp", hop)
            return after, leave(i, moment + 1, after[2:])

        second_wire = exchange(second_leaving)
        first_rows = experts_of(first_wire)
        (first_rows,) = tie((first_rows,), second_wire)
        first_back = exchange(first_rows)
        second_rows = experts_of(second_wire)
        (second_rows,) = tie((second_rows,), first_back)
        second_back = exchange(second_rows)
        states, first_leaving = settle(0, first_back)
        if moment + 1 < sections:
            (first_leaving,) = tie((first_leaving,), second_back)
            first_wire = exchange(first_leaving)
        states, second_leaving = settle(1, second_back)
        if moment + 1 < sections:
            (second_leaving,) = tie((second_leaving,), first_wire)
    forward, reverse, sent = states
    forward, reverse = finish(place, (forward, reverse), to_sibling(sent))
    return (forward[None], reverse[None])


def solution(mesh):
    placed = (
        P("ep", None),
        P("ep", None),
        P("pp", "ep", None),
        P("pp", "ep", None),
        P("pp", "ep", None),
        P("pp", "ep", None),
        P("pp", None, "ep"),
        P("pp", None, "ep"),
        P("pp", "ep", None),
    )
    return jax.shard_map(
        shards,
        mesh=mesh,
        in_specs=placed,
        out_specs=(P("pp", "ep", None), P("pp", "ep", None)),
        check_vma=False,
    )
```

```python
import jax
import jax.numpy as jnp
from jax import lax
from jax.experimental import pallas as pl
from jax.experimental.pallas import tpu as pltpu
from jax.sharding import PartitionSpec as P

MIB = 1 << 20
PIECES = 4
GROUP = 8


def vmem():
    return pl.BlockSpec(memory_space=pltpu.VMEM)


def smem():
    return pl.BlockSpec(memory_space=pltpu.SMEM)


def anywhere():
    return pl.BlockSpec(memory_space=pl.ANY)


def whole(array):
    return pl.BlockSpec(array.shape, lambda step: (0,) * len(array.shape))


def in_hbm(block):
    return pltpu.with_memory_space_constraint(block, pltpu.HBM)


def in_vmem(block):
    return pltpu.with_memory_space_constraint(block, pltpu.VMEM)


def params(mib):
    return pltpu.CompilerParams(vmem_limit_bytes=mib * MIB)


def small_cost():
    return pl.CostEstimate(flops=MIB, bytes_accessed=MIB, transcendentals=0)


def spans(width, step=256):
    return [slice(start, min(start + step, width)) for start in range(0, width, step)]


def split(index, size, count):
    factor = -(-(1 << 16) // size)
    assert all((n * factor) >> 16 == n // size for n in range(size * count))
    high = (index * factor) >> 16
    return high, index - high * size


def wire_codes(shape, axis, experts, capacity):
    index = lax.broadcasted_iota(jnp.int32, shape, axis)
    expert, rest = split(index, PIECES * capacity, experts)
    piece, slot = split(rest, capacity, PIECES)
    return (piece * experts + expert) * capacity + slot


def group_order(axis, capacity):
    size = GROUP * PIECES * capacity
    shape = (1, size) if axis == 1 else (size, 1)
    index = lax.broadcasted_iota(jnp.int32, shape, axis)
    chip, rest = split(index, PIECES * capacity, GROUP)
    piece, slot = split(rest, capacity, PIECES)
    place = (piece * GROUP + chip) * capacity + slot
    other = lax.broadcasted_iota(jnp.int32, (size, size), 1 - axis)
    return jnp.where(other == place, 1.0, 0.0).astype(jnp.bfloat16)


def tie_kernel(*refs):
    del refs


def tie(blocks, after):
    return pl.pallas_call(
        tie_kernel,
        out_shape=tuple(pltpu.HBM(x.shape, x.dtype) for x in blocks),
        in_specs=[anywhere()] * (len(blocks) + 1),
        out_specs=(anywhere(),) * len(blocks),
        input_output_aliases={n: n for n in range(len(blocks))},
        cost_estimate=pl.CostEstimate(flops=0, bytes_accessed=0, transcendentals=0),
        name="tie",
    )(*[in_hbm(x) for x in blocks], after)


def parts_of(width):
    first = -(-width // 256) * 128
    return (slice(0, first), slice(first, width))


def dispatch_first(x, lines, width, moment, block, experts, capacity, after):
    count, first = x.shape
    wire = experts * PIECES * capacity
    groups = 4
    lines_each = wire // groups

    def kernel(x_ref, line_ref, *rest):
        out_ref, select_ref, ready, sems = rest[-4:]
        lines = line_ref[0, 0]
        rows = wire_codes((wire, 1), 0, experts, capacity)
        copies = []
        for group in range(groups):
            place = slice(group * lines_each, (group + 1) * lines_each)
            hit = (rows[place] == lines[0:1, :]) | (rows[place] == lines[1:2, :])
            select = jnp.where(hit, 1.0, 0.0).astype(jnp.bfloat16)
            select_ref[place, :] = select
            for columns in spans(first):
                ready[place, columns] = jnp.dot(
                    select, x_ref[:, columns], preferred_element_type=jnp.float32
                ).astype(jnp.bfloat16)
            where = pl.ds(group * lines_each, lines_each)
            copies.append(
                pltpu.make_async_copy(
                    ready.at[where], out_ref.at[where, pl.ds(0, first)], sems.at[group]
                )
            )
            copies[-1].start()
        for copy in copies:
            copy.wait()

    return pl.pallas_call(
        kernel,
        out_shape=(
            pltpu.HBM((wire, width), jnp.bfloat16),
            jax.ShapeDtypeStruct((wire, count), jnp.bfloat16),
        ),
        grid=(1,),
        in_specs=[
            whole(x),
            pl.BlockSpec((1, 1) + lines.shape[2:], lambda step: (moment, block, 0, 0)),
        ]
        + [anywhere()] * len(after),
        out_specs=(anywhere(), pl.BlockSpec((wire, count), lambda step: (0, 0))),
        scratch_shapes=[
            pltpu.VMEM((wire, first), jnp.bfloat16),
            pltpu.SemaphoreType.DMA((groups,)),
        ],
        compiler_params=params(24),
        cost_estimate=small_cost(),
        name="dispatch_first",
    )(x, in_hbm(lines), *[in_hbm(block) for block in after])


def dispatch_second(x, select, wire_rows):
    second = x.shape[1]
    wire, width = wire_rows.shape
    groups = 4
    lines_each = wire // groups

    def kernel(x_ref, select_ref, wire_ref, out_ref, ready, sems):
        del wire_ref
        copies = []
        for group in range(groups):
            place = slice(group * lines_each, (group + 1) * lines_each)
            for columns in spans(second):
                ready[place, columns] = jnp.dot(
                    select_ref[place, :], x_ref[:, columns], preferred_element_type=jnp.float32
                ).astype(jnp.bfloat16)
            where = pl.ds(group * lines_each, lines_each)
            copies.append(
                pltpu.make_async_copy(
                    ready.at[where], out_ref.at[where, pl.ds(width - second, second)], sems.at[group]
                )
            )
            copies[-1].start()
        for copy in copies:
            copy.wait()

    return pl.pallas_call(
        kernel,
        out_shape=pltpu.HBM((wire, width), jnp.bfloat16),
        in_specs=[vmem(), vmem(), anywhere()],
        out_specs=anywhere(),
        input_output_aliases={2: 0},
        scratch_shapes=[
            pltpu.VMEM((wire, second), jnp.bfloat16),
            pltpu.SemaphoreType.DMA((groups,)),
        ],
        compiler_params=params(24),
        cost_estimate=small_cost(),
        name="dispatch_second",
    )(x, select, in_hbm(wire_rows))


def load_half(core, gate, up, after, part):
    units = gate.shape[1]

    def kernel(core_ref, gate_ref, up_ref, after_ref, gate_out, up_out, sems):
        del after_ref
        copies = []
        for piece in range(PIECES):
            lines = pl.ds(pl.multiple_of((core_ref[0] * PIECES + piece) * part, part), part)
            for number, (ref, out) in enumerate(((gate_ref, gate_out), (up_ref, up_out))):
                copies.append(
                    pltpu.make_async_copy(ref.at[lines], out.at[piece], sems.at[number, piece])
                )
        for copy in copies:
            copy.start()
        for copy in copies:
            copy.wait()

    return pl.pallas_call(
        kernel,
        out_shape=(jax.ShapeDtypeStruct((PIECES, part, units), gate.dtype),) * 2,
        in_specs=[smem()] + [anywhere()] * 3,
        out_specs=(vmem(),) * 2,
        scratch_shapes=[pltpu.SemaphoreType.DMA((2, PIECES))],
        compiler_params=params(16),
        cost_estimate=small_cost(),
        name="load_half",
    )(core, in_hbm(gate), in_hbm(up), in_hbm(after))


def hidden_units(core, own, others, own_gate, own_up, gate, up, down, other_down, capacity):
    wire_rows, part = own.shape
    rows_count = wire_rows // PIECES
    units = gate.shape[1]
    half_width = PIECES * part
    height = GROUP * capacity
    span = PIECES * height
    groups = rows_count // height

    def kernel(
        core_ref, own_ref, low_ref, high_ref, own_gate_ref, own_up_ref, gate_ref, up_ref,
        down_ref, other_down_ref, out_ref, down_out, other_down_out,
        wires, rows, gate_blocks, up_blocks, gate_sum, up_sum,
        wire_sems, gate_sems, up_sems, down_sems,
    ):
        core = core_ref[0]
        middle = wire_rows // 2
        wire_copies = [
            pltpu.make_async_copy(own_ref, wires.at[pl.ds(0, wire_rows)], wire_sems.at[0]),
            pltpu.make_async_copy(low_ref, wires.at[pl.ds(wire_rows, middle)], wire_sems.at[1]),
            pltpu.make_async_copy(
                high_ref, wires.at[pl.ds(wire_rows + middle, middle)], wire_sems.at[2]
            ),
        ]
        loads = []
        down_loads = []
        for piece in range(PIECES):
            lines = pl.ds(pl.multiple_of(((1 - core) * PIECES + piece) * part, part), part)
            loads += [
                pltpu.make_async_copy(gate_ref.at[lines], gate_blocks.at[piece], gate_sems.at[piece]),
                pltpu.make_async_copy(up_ref.at[lines], up_blocks.at[piece], up_sems.at[piece]),
            ]
            place = pl.ds(pl.multiple_of((core * PIECES + piece) * part, part), part)
            down_loads += [
                pltpu.make_async_copy(
                    down_ref.at[:, place], down_out.at[piece], down_sems.at[0, piece]
                ),
                pltpu.make_async_copy(
                    other_down_ref.at[:, pl.ds(piece * part, part)],
                    other_down_out.at[piece],
                    down_sems.at[1, piece],
                ),
            ]
        for copy in wire_copies + loads:
            copy.start()
        order = group_order(1, capacity)
        squares = 0.0
        for step in range(2 * PIECES):
            piece = step % PIECES
            mine = step < PIECES
            if piece == 0:
                base = 0 if mine else wire_rows
                for copy in wire_copies[:1] if mine else wire_copies[1:]:
                    copy.wait()
                for group in range(groups):
                    for columns in spans(part):
                        ordered = jnp.dot(
                            order,
                            wires[base + group * span : base + (group + 1) * span, columns],
                            preferred_element_type=jnp.float32,
                        ).astype(jnp.bfloat16)
                        for number in range(PIECES):
                            rows[
                                group * height : (group + 1) * height,
                                number * part + columns.start : number * part + columns.stop,
                            ] = ordered[number * height : (number + 1) * height]
            if mine:
                down_loads[2 * piece].start()
                down_loads[2 * piece + 1].start()
                gate_block, up_block = own_gate_ref[piece], own_up_ref[piece]
            else:
                loads[2 * piece].wait()
                loads[2 * piece + 1].wait()
                gate_block, up_block = gate_blocks[piece], up_blocks[piece]
            values = rows[:, piece * part : (piece + 1) * part]
            gate = jnp.dot(values, gate_block, preferred_element_type=jnp.float32)
            up = jnp.dot(values, up_block, preferred_element_type=jnp.float32)
            if step == 0:
                gate_sum[...], up_sum[...] = gate, up
            else:
                gate_sum[...] += gate
                up_sum[...] += up
            for columns in spans(part, 128):
                few = values[:, columns].astype(jnp.float32)
                squares += few * few
        mean = jnp.sum(squares, axis=-1, keepdims=True) / (2 * half_width)
        scale = lax.rsqrt(mean + 1e-06)
        out_ref[...] = (jax.nn.silu(gate_sum[...] * scale) * (up_sum[...] * scale)).astype(
            jnp.bfloat16
        )
        for copy in down_loads:
            copy.wait()

    blocks = jax.ShapeDtypeStruct((PIECES, units, part), down.dtype)
    return pl.pallas_call(
        kernel,
        out_shape=(jax.ShapeDtypeStruct((rows_count, units), jnp.bfloat16), blocks, blocks),
        in_specs=[smem()] + [anywhere()] * 3 + [vmem()] * 2 + [anywhere()] * 4,
        out_specs=(vmem(),) * 3,
        scratch_shapes=[
            pltpu.VMEM((2 * wire_rows, part), jnp.bfloat16),
            pltpu.VMEM((rows_count, half_width), jnp.bfloat16),
            pltpu.VMEM((PIECES, part, units), jnp.bfloat16),
            pltpu.VMEM((PIECES, part, units), jnp.bfloat16),
            pltpu.VMEM((rows_count, units), jnp.float32),
            pltpu.VMEM((rows_count, units), jnp.float32),
            pltpu.SemaphoreType.DMA((3,)),
            pltpu.SemaphoreType.DMA((PIECES,)),
            pltpu.SemaphoreType.DMA((PIECES,)),
            pltpu.SemaphoreType.DMA((2, PIECES)),
        ],
        compiler_params=params(32),
        cost_estimate=small_cost(),
        name="hidden_units",
    )(
        core, in_hbm(own), *others, own_gate, own_up,
        *[in_hbm(block) for block in (gate, up, down, other_down)],
    )


def down_rows(hidden, other_hidden, blocks, other_blocks, capacity):
    rows, units = hidden.shape
    part = blocks.shape[2]
    height = GROUP * capacity
    span = PIECES * height
    groups = rows // height

    def kernel(
        hidden_ref, other_ref, blocks_ref, other_blocks_ref, out_ref, stacked, ready, out_sems
    ):
        order = group_order(0, capacity)
        for piece in range(PIECES):
            total = jnp.dot(hidden_ref[...], blocks_ref[piece], preferred_element_type=jnp.float32)
            total += jnp.dot(
                other_ref[...], other_blocks_ref[piece], preferred_element_type=jnp.float32
            )
            total = total.astype(jnp.bfloat16)
            for group in range(groups):
                at = group * span + piece * height
                stacked[at : at + height, :] = total[group * height : (group + 1) * height]
        copies = []
        for group in range(groups):
            lines = slice(group * span, (group + 1) * span)
            for columns in spans(part):
                ready[lines, columns] = jnp.dot(
                    order, stacked[lines, columns], preferred_element_type=jnp.float32
                ).astype(jnp.bfloat16)
            where = pl.ds(group * span, span)
            copies.append(
                pltpu.make_async_copy(ready.at[where], out_ref.at[where], out_sems.at[group])
            )
            copies[-1].start()
        for copy in copies:
            copy.wait()

    return pl.pallas_call(
        kernel,
        out_shape=pltpu.HBM((rows * PIECES, part), jnp.bfloat16),
        in_specs=[vmem()] * 4,
        out_specs=anywhere(),
        scratch_shapes=[
            pltpu.VMEM((rows * PIECES, part), jnp.bfloat16),
            pltpu.VMEM((rows * PIECES, part), jnp.bfloat16),
            pltpu.SemaphoreType.DMA((groups,)),
        ],
        compiler_params=params(24),
        cost_estimate=small_cost(),
        name="down_rows",
    )(hidden, other_hidden, blocks, other_blocks)


def other_half(core, down, after, count):
    units, width = down.shape
    half_width = width // 2
    height = units // count

    def kernel(core_ref, down_ref, after_ref, *rest):
        del after_ref
        outs, sems = rest[:-1], rest[-1]
        place = pl.ds(pl.multiple_of((1 - core_ref[0]) * half_width, half_width), half_width)
        copies = [
            pltpu.make_async_copy(
                down_ref.at[pl.ds(number * height, height), place], out, sems.at[number]
            )
            for number, out in enumerate(outs)
        ]
        for copy in copies:
            copy.start()
        for copy in copies:
            copy.wait()

    return pl.pallas_call(
        kernel,
        out_shape=(jax.ShapeDtypeStruct((height, half_width), down.dtype),) * count,
        in_specs=[smem()] + [anywhere()] * 2,
        out_specs=(vmem(),) * count,
        scratch_shapes=[pltpu.SemaphoreType.DMA((count,))],
        compiler_params=params(24),
        cost_estimate=small_cost(),
        name="other_half",
    )(core, in_hbm(down), in_hbm(after))


def combine_first(x, wire, columns, weights, moment, block, experts, capacity):
    count, first = x.shape
    wire_rows = wire.shape[0]

    def kernel(x_ref, wire_ref, column_ref, weight_ref, y_ref, factors, held, sem):
        copy = pltpu.make_async_copy(wire_ref.at[:, pl.ds(0, first)], held, sem.at[0])
        copy.start()
        rows = wire_codes((1, wire_rows), 1, experts, capacity)
        codes, shares = column_ref[0, 0], weight_ref[0, 0]
        codes = jnp.concatenate([codes + piece * (experts * capacity) for piece in range(PIECES)])
        shares = jnp.concatenate([shares] * PIECES)
        table = jnp.where(rows == codes[:, 0:1], shares[:, 0:1], 0.0)
        table += jnp.where(rows == codes[:, 1:2], shares[:, 1:2], 0.0)
        high = table.astype(jnp.bfloat16)
        factors[:count, :] = high
        factors[count:, :] = (table - high.astype(jnp.float32)).astype(jnp.bfloat16)
        copy.wait()
        for lanes in spans(first):
            both = jnp.dot(factors[...], held[:, lanes], preferred_element_type=jnp.float32)
            y_ref[:, lanes] = (
                x_ref[:, lanes].astype(jnp.float32) + both[:count, :] + both[count:, :]
            ).astype(jnp.bfloat16)

    per_block = lambda array: pl.BlockSpec(
        (1, 1) + array.shape[2:], lambda step: (moment, block, 0, 0)
    )
    return pl.pallas_call(
        kernel,
        out_shape=(
            jax.ShapeDtypeStruct((count, first), x.dtype),
            jax.ShapeDtypeStruct((2 * count, wire_rows), jnp.bfloat16),
        ),
        grid=(1,),
        in_specs=[whole(x), anywhere(), per_block(columns), per_block(weights)],
        out_specs=(
            pl.BlockSpec((count, first), lambda step: (0, 0)),
            pl.BlockSpec((2 * count, wire_rows), lambda step: (0, 0)),
        ),
        scratch_shapes=[
            pltpu.VMEM((wire_rows, first), jnp.bfloat16),
            pltpu.SemaphoreType.DMA((1,)),
        ],
        compiler_params=params(24),
        cost_estimate=small_cost(),
        name="combine_first",
    )(in_hbm(x), in_hbm(wire), in_hbm(columns), in_hbm(weights))


def combine_second(x, wire, factors):
    count, second = x.shape
    wire_rows, width = wire.shape

    def kernel(x_ref, wire_ref, factor_ref, y_ref, held, start, sems):
        copies = [
            pltpu.make_async_copy(
                wire_ref.at[:, pl.ds(width - second, second)], held, sems.at[0]
            ),
            pltpu.make_async_copy(x_ref, start, sems.at[1]),
        ]
        for copy in copies:
            copy.start()
        for copy in copies:
            copy.wait()
        for lanes in spans(second):
            both = jnp.dot(factor_ref[...], held[:, lanes], preferred_element_type=jnp.float32)
            y_ref[:, lanes] = (
                start[:, lanes].astype(jnp.float32) + both[:count, :] + both[count:, :]
            ).astype(jnp.bfloat16)

    return pl.pallas_call(
        kernel,
        out_shape=jax.ShapeDtypeStruct((count, second), x.dtype),
        in_specs=[anywhere(), anywhere(), vmem()],
        out_specs=vmem(),
        scratch_shapes=[
            pltpu.VMEM((wire_rows, second), jnp.bfloat16),
            pltpu.VMEM((count, second), x.dtype),
            pltpu.SemaphoreType.DMA((2,)),
        ],
        compiler_params=params(24),
        cost_estimate=small_cost(),
        name="combine_second",
    )(in_hbm(x), in_hbm(wire), factors)


def record(place, ys, states, moment, block, sections):
    count = ys[0].shape[0]
    tokens = count // PIECES
    widths = [y.shape[1] for y in ys]
    part = sum(widths)
    starts = (0, widths[0])

    def kernel(place_ref, first_ref, second_ref, *rest):
        forward_ref, reverse_ref, sent_ref, sems = rest[-4:]
        section, core = place_ref[0], place_ref[1]
        for number, (state_ref, turn) in enumerate(
            ((forward_ref, moment), (reverse_ref, sections - 1 - moment))
        ):

            @pl.when((section == turn) & (core == block))
            def _():
                copies = []
                for which, y_ref in enumerate((first_ref, second_ref)):
                    for piece in range(PIECES):
                        at = (block * PIECES + piece) * part + starts[which]
                        copies.append(
                            pltpu.make_async_copy(
                                y_ref.at[pl.ds(piece * tokens, tokens)],
                                state_ref.at[:, pl.ds(at, widths[which])],
                                sems.at[number, which * PIECES + piece],
                            )
                        )
                for copy in copies:
                    copy.start()
                for copy in copies:
                    copy.wait()

            @pl.when((section == turn) & (core != block))
            def _():
                copies = [
                    pltpu.make_async_copy(
                        y_ref,
                        sent_ref.at[number, :, pl.ds(starts[which], widths[which])],
                        sems.at[number, which],
                    )
                    for which, y_ref in enumerate((first_ref, second_ref))
                ]
                for copy in copies:
                    copy.start()
                for copy in copies:
                    copy.wait()

    result = pltpu.HBM((tokens, 2 * PIECES * part), ys[0].dtype)
    return pl.pallas_call(
        kernel,
        out_shape=(result, result, pltpu.HBM((2, count, part), ys[0].dtype)),
        in_specs=[smem()] + [anywhere()] * (2 + len(states)),
        out_specs=(anywhere(),) * 3,
        input_output_aliases={3 + n: n for n in range(len(states))},
        scratch_shapes=[pltpu.SemaphoreType.DMA((2, 2 * PIECES))],
        cost_estimate=small_cost(),
        name="record",
    )(place, *[in_vmem(y) for y in ys], *[in_hbm(state) for state in states])


def finish(place, states, arrived):
    count, part = arrived.shape[1:]
    tokens = count // PIECES

    def kernel(place_ref, forward_in, reverse_in, arrived_ref, forward_ref, reverse_ref, sems):
        del forward_in, reverse_in
        half = 1 - place_ref[1]
        copies = []
        for number, ref in enumerate((forward_ref, reverse_ref)):
            for piece in range(PIECES):
                at = pl.multiple_of((half * PIECES + piece) * part, part)
                copies.append(
                    pltpu.make_async_copy(
                        arrived_ref.at[number, pl.ds(piece * tokens, tokens)],
                        ref.at[:, pl.ds(at, part)],
                        sems.at[number, piece],
                    )
                )
        for copy in copies:
            copy.start()
        for copy in copies:
            copy.wait()

    return pl.pallas_call(
        kernel,
        out_shape=tuple(pltpu.HBM(state.shape, state.dtype) for state in states),
        in_specs=[smem()] + [anywhere()] * 3,
        out_specs=(anywhere(),) * 2,
        input_output_aliases={1: 0, 2: 1},
        scratch_shapes=[pltpu.SemaphoreType.DMA((2, PIECES))],
        name="finish",
    )(place, *[in_hbm(state) for state in states], in_vmem(arrived))


def slots(routes, experts, capacity):
    flat = routes.reshape(routes.shape[:-2] + (-1,))
    order = jnp.arange(flat.shape[-1], dtype=jnp.int32)
    earlier = (flat[..., :, None] == flat[..., None, :]) & (order[None, :] < order[:, None])
    slot = flat * capacity + jnp.sum(earlier.astype(jnp.int32), axis=-1)
    return slot.reshape(routes.shape)


def shards(tokens_a, tokens_b, routes_a, routes_b, affinity_a, affinity_b, gate_w, up_w, down_w):
    sections = lax.axis_size("pp")
    devices = lax.axis_size("ep")
    experts = devices // 2
    token_count, width = tokens_a.shape
    half_width = width // 2
    capacity = 2 * (token_count * routes_a.shape[2] // devices) + 2
    section = lax.axis_index("pp")
    core = (lax.axis_index("ep") % 2).astype(jnp.int32)
    low = core == 0
    place = jnp.stack([section.astype(jnp.int32), core])
    own_half = core.reshape(1)
    gate, up, down = gate_w[0], up_w[0], down_w[0]

    one_core = [[2 * chip + side for chip in range(experts)] for side in range(2)]
    siblings = [(device, device ^ 1) for device in range(devices)]

    def exchange(wire):
        blocks = wire.reshape(experts, PIECES * capacity, wire.shape[1])
        moved = lax.all_to_all(
            blocks, "ep", split_axis=0, concat_axis=0, tiled=True, axis_index_groups=one_core
        )
        return moved.reshape(wire.shape)

    def to_sibling(block):
        return lax.ppermute(block, "ep", siblings)

    def by_block(mine, theirs):
        return jnp.where(low, mine, theirs), jnp.where(low, theirs, mine)

    def by_moment(pair):
        return jnp.stack([jnp.where(section == m, pair[0], pair[1]) for m in range(sections)])

    target = slots(jnp.stack([routes_a[0], routes_b[0]]), experts, capacity)
    target = by_moment(target)
    affinity = by_moment(jnp.stack([affinity_a[0], affinity_b[0]]))
    target = jnp.stack(by_block(target, to_sibling(target)), axis=1)
    affinity = jnp.stack(by_block(affinity, to_sibling(affinity)), axis=1)
    shift = jnp.arange(PIECES, dtype=jnp.int32)[:, None] * (experts * capacity)
    lines = target.swapaxes(2, 3)
    lines = (lines[:, :, :, None] + shift).reshape(lines.shape[:3] + (PIECES * token_count,))

    first = jnp.where(section == 0, tokens_a, tokens_b)
    lower, upper = first[:, :half_width], first[:, half_width:]
    chunks = by_block(jnp.where(low, lower, upper), to_sibling(jnp.where(low, upper, lower)))
    part = half_width // PIECES
    stacked = [jnp.concatenate(jnp.split(chunk, PIECES, axis=1)) for chunk in chunks]
    chunks = [[chunk[:, columns] for columns in parts_of(part)] for chunk in stacked]

    def leave(i, moment, after=()):
        first, select = dispatch_first(
            chunks[i][0], lines, part, moment, i, experts, capacity, after
        )
        return dispatch_second(chunks[i][1], select, first)

    def experts_of(wire):
        middle = wire.shape[0] // 2
        others = [to_sibling(wire[:middle]), to_sibling(wire[middle:])]
        own_gate, own_up = load_half(own_half, gate, up, wire, wire.shape[1])
        hidden, *blocks = hidden_units(
            own_half, wire, others, own_gate, own_up, gate, up, down, other_down, capacity
        )
        return down_rows(hidden, to_sibling(hidden), *blocks, capacity)

    states = ()
    first_leaving = leave(0, 0)
    first_wire = exchange(first_leaving)
    other_down = [to_sibling(block) for block in other_half(own_half, down, first_leaving, 8)]
    second_leaving, target, affinity, other_down = tie(
        (leave(1, 0), target, affinity, jnp.concatenate(other_down)), first_wire
    )
    for moment in range(sections):
        last = sections - 1 - moment
        hop = [(moment, moment + 1), (last, last - 1)]

        def settle(i, back):
            y, factors = combine_first(
                chunks[i][0], back, target, affinity, moment, i, experts, capacity
            )
            ys = [y, combine_second(chunks[i][1], back, factors)]
            after = record(place, ys, states, moment, i, sections)
            if moment + 1 == sections:
                return after, None
            chunks[i] = [lax.ppermute(y, "pp", hop) for y in ys]
            return after, leave(i, moment + 1, after[2:])

        second_wire = exchange(second_leaving)
        first_rows = experts_of(first_wire)
        (first_rows,) = tie((first_rows,), second_wire)
        first_back = exchange(first_rows)
        second_rows = experts_of(second_wire)
        (second_rows,) = tie((second_rows,), first_back)
        second_back = exchange(second_rows)
        states, first_leaving = settle(0, first_back)
        if moment + 1 < sections:
            (first_leaving,) = tie((first_leaving,), second_back)
            first_wire = exchange(first_leaving)
        states, second_leaving = settle(1, second_back)
        if moment + 1 < sections:
            (second_leaving,) = tie((second_leaving,), first_wire)
    forward, reverse, sent = states
    forward, reverse = finish(place, (forward, reverse), to_sibling(sent))
    return (forward[None], reverse[None])


def solution(mesh):
    placed = (
        P("ep", None),
        P("ep", None),
        P("pp", "ep", None),
        P("pp", "ep", None),
        P("pp", "ep", None),
        P("pp", "ep", None),
        P("pp", None, "ep"),
        P("pp", None, "ep"),
        P("pp", "ep", None),
    )
    return jax.shard_map(
        shards,
        mesh=mesh,
        in_specs=placed,
        out_specs=(P("pp", "ep", None), P("pp", "ep", None)),
        check_vma=False,
    )
```

```python
import jax
import jax.numpy as jnp
from jax import lax
from jax.experimental import pallas as pl
from jax.experimental.pallas import tpu as pltpu
from jax.sharding import PartitionSpec as P

MIB = 1 << 20
PIECES = 4
GROUP = 8


def vmem():
    return pl.BlockSpec(memory_space=pltpu.VMEM)


def smem():
    return pl.BlockSpec(memory_space=pltpu.SMEM)


def anywhere():
    return pl.BlockSpec(memory_space=pl.ANY)


def whole(array):
    return pl.BlockSpec(array.shape, lambda step: (0,) * len(array.shape))


def in_hbm(block):
    return pltpu.with_memory_space_constraint(block, pltpu.HBM)


def in_vmem(block):
    return pltpu.with_memory_space_constraint(block, pltpu.VMEM)


def params(mib):
    return pltpu.CompilerParams(vmem_limit_bytes=mib * MIB)


def small_cost():
    return pl.CostEstimate(flops=MIB, bytes_accessed=MIB, transcendentals=0)


def spans(width, step=256):
    return [slice(start, min(start + step, width)) for start in range(0, width, step)]


def split(index, size, count):
    factor = -(-(1 << 16) // size)
    assert all((n * factor) >> 16 == n // size for n in range(size * count))
    high = (index * factor) >> 16
    return high, index - high * size


def wire_codes(shape, axis, experts, capacity):
    index = lax.broadcasted_iota(jnp.int32, shape, axis)
    expert, rest = split(index, PIECES * capacity, experts)
    piece, slot = split(rest, capacity, PIECES)
    return (piece * experts + expert) * capacity + slot


def group_order(axis, capacity):
    size = GROUP * PIECES * capacity
    shape = (1, size) if axis == 1 else (size, 1)
    index = lax.broadcasted_iota(jnp.int32, shape, axis)
    chip, rest = split(index, PIECES * capacity, GROUP)
    piece, slot = split(rest, capacity, PIECES)
    place = (piece * GROUP + chip) * capacity + slot
    other = lax.broadcasted_iota(jnp.int32, (size, size), 1 - axis)
    return jnp.where(other == place, 1.0, 0.0).astype(jnp.bfloat16)


def tie_kernel(*refs):
    del refs


def tie(blocks, after):
    return pl.pallas_call(
        tie_kernel,
        out_shape=tuple(pltpu.HBM(x.shape, x.dtype) for x in blocks),
        in_specs=[anywhere()] * (len(blocks) + 1),
        out_specs=(anywhere(),) * len(blocks),
        input_output_aliases={n: n for n in range(len(blocks))},
        cost_estimate=pl.CostEstimate(flops=0, bytes_accessed=0, transcendentals=0),
        name="tie",
    )(*[in_hbm(x) for x in blocks], after)


def parts_of(width):
    first = -(-width // 256) * 128
    return (slice(0, first), slice(first, width))


def dispatch_first(x, lines, width, moment, block, experts, capacity, after):
    count, first = x.shape
    wire = experts * PIECES * capacity
    groups = 4
    lines_each = wire // groups

    def kernel(x_ref, line_ref, *rest):
        out_ref, select_ref, ready, sems = rest[-4:]
        lines = line_ref[0, 0]
        rows = wire_codes((wire, 1), 0, experts, capacity)
        copies = []
        for group in range(groups):
            place = slice(group * lines_each, (group + 1) * lines_each)
            hit = (rows[place] == lines[0:1, :]) | (rows[place] == lines[1:2, :])
            select = jnp.where(hit, 1.0, 0.0).astype(jnp.bfloat16)
            select_ref[place, :] = select
            for columns in spans(first):
                ready[place, columns] = jnp.dot(
                    select, x_ref[:, columns], preferred_element_type=jnp.float32
                ).astype(jnp.bfloat16)
            where = pl.ds(group * lines_each, lines_each)
            copies.append(
                pltpu.make_async_copy(
                    ready.at[where], out_ref.at[where, pl.ds(0, first)], sems.at[group]
                )
            )
            copies[-1].start()
        for copy in copies:
            copy.wait()

    return pl.pallas_call(
        kernel,
        out_shape=(
            pltpu.HBM((wire, width), jnp.bfloat16),
            jax.ShapeDtypeStruct((wire, count), jnp.bfloat16),
        ),
        grid=(1,),
        in_specs=[
            whole(x),
            pl.BlockSpec((1, 1) + lines.shape[2:], lambda step: (moment, block, 0, 0)),
        ]
        + [anywhere()] * len(after),
        out_specs=(anywhere(), pl.BlockSpec((wire, count), lambda step: (0, 0))),
        scratch_shapes=[
            pltpu.VMEM((wire, first), jnp.bfloat16),
            pltpu.SemaphoreType.DMA((groups,)),
        ],
        compiler_params=params(24),
        cost_estimate=small_cost(),
        name="dispatch_first",
    )(x, in_hbm(lines), *[in_hbm(block) for block in after])


def dispatch_second(x, select, wire_rows):
    second = x.shape[1]
    wire, width = wire_rows.shape
    groups = 4
    lines_each = wire // groups

    def kernel(x_ref, select_ref, wire_ref, out_ref, ready, sems):
        del wire_ref
        copies = []
        for group in range(groups):
            place = slice(group * lines_each, (group + 1) * lines_each)
            for columns in spans(second):
                ready[place, columns] = jnp.dot(
                    select_ref[place, :], x_ref[:, columns], preferred_element_type=jnp.float32
                ).astype(jnp.bfloat16)
            where = pl.ds(group * lines_each, lines_each)
            copies.append(
                pltpu.make_async_copy(
                    ready.at[where], out_ref.at[where, pl.ds(width - second, second)], sems.at[group]
                )
            )
            copies[-1].start()
        for copy in copies:
            copy.wait()

    return pl.pallas_call(
        kernel,
        out_shape=pltpu.HBM((wire, width), jnp.bfloat16),
        in_specs=[vmem(), vmem(), anywhere()],
        out_specs=anywhere(),
        input_output_aliases={2: 0},
        scratch_shapes=[
            pltpu.VMEM((wire, second), jnp.bfloat16),
            pltpu.SemaphoreType.DMA((groups,)),
        ],
        compiler_params=params(24),
        cost_estimate=small_cost(),
        name="dispatch_second",
    )(x, select, in_hbm(wire_rows))


def load_half(core, gate, up, after, part):
    units = gate.shape[1]

    def kernel(core_ref, gate_ref, up_ref, after_ref, gate_out, up_out, sems):
        del after_ref
        copies = []
        for piece in range(PIECES):
            lines = pl.ds(pl.multiple_of((core_ref[0] * PIECES + piece) * part, part), part)
            for number, (ref, out) in enumerate(((gate_ref, gate_out), (up_ref, up_out))):
                copies.append(
                    pltpu.make_async_copy(ref.at[lines], out.at[piece], sems.at[number, piece])
                )
        for copy in copies:
            copy.start()
        for copy in copies:
            copy.wait()

    return pl.pallas_call(
        kernel,
        out_shape=(jax.ShapeDtypeStruct((PIECES, part, units), gate.dtype),) * 2,
        in_specs=[smem()] + [anywhere()] * 3,
        out_specs=(vmem(),) * 2,
        scratch_shapes=[pltpu.SemaphoreType.DMA((2, PIECES))],
        compiler_params=params(16),
        cost_estimate=small_cost(),
        name="load_half",
    )(core, in_hbm(gate), in_hbm(up), in_hbm(after))


def hidden_units(core, own, others, own_gate, own_up, gate, up, down, other_down, capacity):
    wire_rows, part = own.shape
    rows_count = wire_rows // PIECES
    units = gate.shape[1]
    half_width = PIECES * part
    height = GROUP * capacity
    span = PIECES * height
    groups = rows_count // height

    def kernel(
        core_ref, own_ref, low_ref, high_ref, own_gate_ref, own_up_ref, gate_ref, up_ref,
        down_ref, other_down_ref, out_ref, down_out, other_down_out,
        wires, rows, gate_blocks, up_blocks, gate_sum, up_sum,
        wire_sems, gate_sems, up_sems, down_sems,
    ):
        core = core_ref[0]
        middle = wire_rows // 2
        wire_copies = [
            pltpu.make_async_copy(own_ref, wires.at[pl.ds(0, wire_rows)], wire_sems.at[0]),
            pltpu.make_async_copy(low_ref, wires.at[pl.ds(wire_rows, middle)], wire_sems.at[1]),
            pltpu.make_async_copy(
                high_ref, wires.at[pl.ds(wire_rows + middle, middle)], wire_sems.at[2]
            ),
        ]
        loads = []
        down_loads = []
        for piece in range(PIECES):
            lines = pl.ds(pl.multiple_of(((1 - core) * PIECES + piece) * part, part), part)
            loads += [
                pltpu.make_async_copy(gate_ref.at[lines], gate_blocks.at[piece], gate_sems.at[piece]),
                pltpu.make_async_copy(up_ref.at[lines], up_blocks.at[piece], up_sems.at[piece]),
            ]
            place = pl.ds(pl.multiple_of((core * PIECES + piece) * part, part), part)
            down_loads += [
                pltpu.make_async_copy(
                    down_ref.at[:, place], down_out.at[piece], down_sems.at[0, piece]
                ),
                pltpu.make_async_copy(
                    other_down_ref.at[:, pl.ds(piece * part, part)],
                    other_down_out.at[piece],
                    down_sems.at[1, piece],
                ),
            ]
        for copy in wire_copies + loads:
            copy.start()
        order = group_order(1, capacity)
        squares = 0.0
        for step in range(2 * PIECES):
            piece = step % PIECES
            mine = step < PIECES
            if piece == 0:
                base = 0 if mine else wire_rows
                for copy in wire_copies[:1] if mine else wire_copies[1:]:
                    copy.wait()
                for group in range(groups):
                    for columns in spans(part):
                        ordered = jnp.dot(
                            order,
                            wires[base + group * span : base + (group + 1) * span, columns],
                            preferred_element_type=jnp.float32,
                        ).astype(jnp.bfloat16)
                        for number in range(PIECES):
                            rows[
                                group * height : (group + 1) * height,
                                number * part + columns.start : number * part + columns.stop,
                            ] = ordered[number * height : (number + 1) * height]
            if mine:
                down_loads[2 * piece].start()
                down_loads[2 * piece + 1].start()
                gate_block, up_block = own_gate_ref[piece], own_up_ref[piece]
            else:
                loads[2 * piece].wait()
                loads[2 * piece + 1].wait()
                gate_block, up_block = gate_blocks[piece], up_blocks[piece]
            values = rows[:, piece * part : (piece + 1) * part]
            gate = jnp.dot(values, gate_block, preferred_element_type=jnp.float32)
            up = jnp.dot(values, up_block, preferred_element_type=jnp.float32)
            if step == 0:
                gate_sum[...], up_sum[...] = gate, up
            else:
                gate_sum[...] += gate
                up_sum[...] += up
            for columns in spans(part, 128):
                few = values[:, columns].astype(jnp.float32)
                squares += few * few
        mean = jnp.sum(squares, axis=-1, keepdims=True) / (2 * half_width)
        scale = lax.rsqrt(mean + 1e-06)
        out_ref[...] = (jax.nn.silu(gate_sum[...] * scale) * (up_sum[...] * scale)).astype(
            jnp.bfloat16
        )
        for copy in down_loads:
            copy.wait()

    blocks = jax.ShapeDtypeStruct((PIECES, units, part), down.dtype)
    return pl.pallas_call(
        kernel,
        out_shape=(jax.ShapeDtypeStruct((rows_count, units), jnp.bfloat16), blocks, blocks),
        in_specs=[smem()] + [anywhere()] * 3 + [vmem()] * 2 + [anywhere()] * 4,
        out_specs=(vmem(),) * 3,
        scratch_shapes=[
            pltpu.VMEM((2 * wire_rows, part), jnp.bfloat16),
            pltpu.VMEM((rows_count, half_width), jnp.bfloat16),
            pltpu.VMEM((PIECES, part, units), jnp.bfloat16),
            pltpu.VMEM((PIECES, part, units), jnp.bfloat16),
            pltpu.VMEM((rows_count, units), jnp.float32),
            pltpu.VMEM((rows_count, units), jnp.float32),
            pltpu.SemaphoreType.DMA((3,)),
            pltpu.SemaphoreType.DMA((PIECES,)),
            pltpu.SemaphoreType.DMA((PIECES,)),
            pltpu.SemaphoreType.DMA((2, PIECES)),
        ],
        compiler_params=params(32),
        cost_estimate=small_cost(),
        name="hidden_units",
    )(
        core, in_hbm(own), *others, own_gate, own_up,
        *[in_hbm(block) for block in (gate, up, down, other_down)],
    )


def down_rows(hidden, other_hidden, blocks, other_blocks, capacity):
    rows, units = hidden.shape
    part = blocks.shape[2]
    height = GROUP * capacity
    span = PIECES * height
    groups = rows // height

    def kernel(
        hidden_ref, other_ref, blocks_ref, other_blocks_ref, out_ref, stacked, ready, out_sems
    ):
        order = group_order(0, capacity)
        for piece in range(PIECES):
            total = jnp.dot(hidden_ref[...], blocks_ref[piece], preferred_element_type=jnp.float32)
            total += jnp.dot(
                other_ref[...], other_blocks_ref[piece], preferred_element_type=jnp.float32
            )
            total = total.astype(jnp.bfloat16)
            for group in range(groups):
                at = group * span + piece * height
                stacked[at : at + height, :] = total[group * height : (group + 1) * height]
        copies = []
        for group in range(groups):
            lines = slice(group * span, (group + 1) * span)
            for columns in spans(part):
                ready[lines, columns] = jnp.dot(
                    order, stacked[lines, columns], preferred_element_type=jnp.float32
                ).astype(jnp.bfloat16)
            where = pl.ds(group * span, span)
            copies.append(
                pltpu.make_async_copy(ready.at[where], out_ref.at[where], out_sems.at[group])
            )
            copies[-1].start()
        for copy in copies:
            copy.wait()

    return pl.pallas_call(
        kernel,
        out_shape=pltpu.HBM((rows * PIECES, part), jnp.bfloat16),
        in_specs=[vmem()] * 4,
        out_specs=anywhere(),
        scratch_shapes=[
            pltpu.VMEM((rows * PIECES, part), jnp.bfloat16),
            pltpu.VMEM((rows * PIECES, part), jnp.bfloat16),
            pltpu.SemaphoreType.DMA((groups,)),
        ],
        compiler_params=params(24),
        cost_estimate=small_cost(),
        name="down_rows",
    )(hidden, other_hidden, blocks, other_blocks)


def other_half(core, down, after, count):
    units, width = down.shape
    half_width = width // 2
    height = units // count

    def kernel(core_ref, down_ref, after_ref, *rest):
        del after_ref
        outs, sems = rest[:-1], rest[-1]
        place = pl.ds(pl.multiple_of((1 - core_ref[0]) * half_width, half_width), half_width)
        copies = [
            pltpu.make_async_copy(
                down_ref.at[pl.ds(number * height, height), place], out, sems.at[number]
            )
            for number, out in enumerate(outs)
        ]
        for copy in copies:
            copy.start()
        for copy in copies:
            copy.wait()

    return pl.pallas_call(
        kernel,
        out_shape=(jax.ShapeDtypeStruct((height, half_width), down.dtype),) * count,
        in_specs=[smem()] + [anywhere()] * 2,
        out_specs=(vmem(),) * count,
        scratch_shapes=[pltpu.SemaphoreType.DMA((count,))],
        compiler_params=params(24),
        cost_estimate=small_cost(),
        name="other_half",
    )(core, in_hbm(down), in_hbm(after))


def combine_first(x, wire, columns, weights, moment, block, experts, capacity):
    count, first = x.shape
    wire_rows = wire.shape[0]

    def kernel(x_ref, wire_ref, column_ref, weight_ref, y_ref, factors, held, sem):
        copy = pltpu.make_async_copy(wire_ref.at[:, pl.ds(0, first)], held, sem.at[0])
        copy.start()
        rows = wire_codes((1, wire_rows), 1, experts, capacity)
        codes, shares = column_ref[0, 0], weight_ref[0, 0]
        codes = jnp.concatenate([codes + piece * (experts * capacity) for piece in range(PIECES)])
        shares = jnp.concatenate([shares] * PIECES)
        table = jnp.where(rows == codes[:, 0:1], shares[:, 0:1], 0.0)
        table += jnp.where(rows == codes[:, 1:2], shares[:, 1:2], 0.0)
        high = table.astype(jnp.bfloat16)
        factors[:count, :] = high
        factors[count:, :] = (table - high.astype(jnp.float32)).astype(jnp.bfloat16)
        copy.wait()
        for lanes in spans(first):
            both = jnp.dot(factors[...], held[:, lanes], preferred_element_type=jnp.float32)
            y_ref[:, lanes] = (
                x_ref[:, lanes].astype(jnp.float32) + both[:count, :] + both[count:, :]
            ).astype(jnp.bfloat16)

    per_block = lambda array: pl.BlockSpec(
        (1, 1) + array.shape[2:], lambda step: (moment, block, 0, 0)
    )
    return pl.pallas_call(
        kernel,
        out_shape=(
            jax.ShapeDtypeStruct((count, first), x.dtype),
            jax.ShapeDtypeStruct((2 * count, wire_rows), jnp.bfloat16),
        ),
        grid=(1,),
        in_specs=[whole(x), anywhere(), per_block(columns), per_block(weights)],
        out_specs=(
            pl.BlockSpec((count, first), lambda step: (0, 0)),
            pl.BlockSpec((2 * count, wire_rows), lambda step: (0, 0)),
        ),
        scratch_shapes=[
            pltpu.VMEM((wire_rows, first), jnp.bfloat16),
            pltpu.SemaphoreType.DMA((1,)),
        ],
        compiler_params=params(24),
        cost_estimate=small_cost(),
        name="combine_first",
    )(in_hbm(x), in_hbm(wire), in_hbm(columns), in_hbm(weights))


def combine_second(x, wire, factors):
    count, second = x.shape
    wire_rows, width = wire.shape

    def kernel(x_ref, wire_ref, factor_ref, y_ref, held, start, sems):
        copies = [
            pltpu.make_async_copy(
                wire_ref.at[:, pl.ds(width - second, second)], held, sems.at[0]
            ),
            pltpu.make_async_copy(x_ref, start, sems.at[1]),
        ]
        for copy in copies:
            copy.start()
        for copy in copies:
            copy.wait()
        for lanes in spans(second):
            both = jnp.dot(factor_ref[...], held[:, lanes], preferred_element_type=jnp.float32)
            y_ref[:, lanes] = (
                start[:, lanes].astype(jnp.float32) + both[:count, :] + both[count:, :]
            ).astype(jnp.bfloat16)

    return pl.pallas_call(
        kernel,
        out_shape=jax.ShapeDtypeStruct((count, second), x.dtype),
        in_specs=[anywhere(), anywhere(), vmem()],
        out_specs=vmem(),
        scratch_shapes=[
            pltpu.VMEM((wire_rows, second), jnp.bfloat16),
            pltpu.VMEM((count, second), x.dtype),
            pltpu.SemaphoreType.DMA((2,)),
        ],
        compiler_params=params(24),
        cost_estimate=small_cost(),
        name="combine_second",
    )(in_hbm(x), in_hbm(wire), factors)


def record(place, ys, states, moment, block, sections):
    count = ys[0].shape[0]
    tokens = count // PIECES
    widths = [y.shape[1] for y in ys]
    part = sum(widths)
    starts = (0, widths[0])

    def kernel(place_ref, first_ref, second_ref, *rest):
        forward_ref, reverse_ref, sent_ref, sems = rest[-4:]
        section, core = place_ref[0], place_ref[1]
        for number, (state_ref, turn) in enumerate(
            ((forward_ref, moment), (reverse_ref, sections - 1 - moment))
        ):

            @pl.when((section == turn) & (core == block))
            def _():
                copies = []
                for which, y_ref in enumerate((first_ref, second_ref)):
                    for piece in range(PIECES):
                        at = (block * PIECES + piece) * part + starts[which]
                        copies.append(
                            pltpu.make_async_copy(
                                y_ref.at[pl.ds(piece * tokens, tokens)],
                                state_ref.at[:, pl.ds(at, widths[which])],
                                sems.at[number, which * PIECES + piece],
                            )
                        )
                for copy in copies:
                    copy.start()
                for copy in copies:
                    copy.wait()

            @pl.when((section == turn) & (core != block))
            def _():
                copies = [
                    pltpu.make_async_copy(
                        y_ref,
                        sent_ref.at[number, :, pl.ds(starts[which], widths[which])],
                        sems.at[number, which],
                    )
                    for which, y_ref in enumerate((first_ref, second_ref))
                ]
                for copy in copies:
                    copy.start()
                for copy in copies:
                    copy.wait()

    result = pltpu.HBM((tokens, 2 * PIECES * part), ys[0].dtype)
    return pl.pallas_call(
        kernel,
        out_shape=(result, result, pltpu.HBM((2, count, part), ys[0].dtype)),
        in_specs=[smem()] + [anywhere()] * (2 + len(states)),
        out_specs=(anywhere(),) * 3,
        input_output_aliases={3 + n: n for n in range(len(states))},
        scratch_shapes=[pltpu.SemaphoreType.DMA((2, 2 * PIECES))],
        cost_estimate=small_cost(),
        name="record",
    )(place, *[in_vmem(y) for y in ys], *[in_hbm(state) for state in states])


def finish(place, states, arrived):
    count, part = arrived.shape[1:]
    tokens = count // PIECES

    def kernel(place_ref, forward_in, reverse_in, arrived_ref, forward_ref, reverse_ref, sems):
        del forward_in, reverse_in
        half = 1 - place_ref[1]
        copies = []
        for number, ref in enumerate((forward_ref, reverse_ref)):
            for piece in range(PIECES):
                at = pl.multiple_of((half * PIECES + piece) * part, part)
                copies.append(
                    pltpu.make_async_copy(
                        arrived_ref.at[number, pl.ds(piece * tokens, tokens)],
                        ref.at[:, pl.ds(at, part)],
                        sems.at[number, piece],
                    )
                )
        for copy in copies:
            copy.start()
        for copy in copies:
            copy.wait()

    return pl.pallas_call(
        kernel,
        out_shape=tuple(pltpu.HBM(state.shape, state.dtype) for state in states),
        in_specs=[smem()] + [anywhere()] * 3,
        out_specs=(anywhere(),) * 2,
        input_output_aliases={1: 0, 2: 1},
        scratch_shapes=[pltpu.SemaphoreType.DMA((2, PIECES))],
        name="finish",
    )(place, *[in_hbm(state) for state in states], in_vmem(arrived))


def split_tokens(place, tokens_a, tokens_b):
    tokens, width = tokens_a.shape
    part = width // 2 // PIECES
    count = PIECES * tokens

    def kernel(place_ref, a_ref, b_ref, kept_ref, leaving_ref, sems):
        section, core = place_ref[0], place_ref[1]

        def move(ref):
            copies = []
            for which, (half, out) in enumerate(((core, kept_ref), (1 - core, leaving_ref))):
                for piece in range(PIECES):
                    at = pl.multiple_of((half * PIECES + piece) * part, part)
                    copies.append(
                        pltpu.make_async_copy(
                            ref.at[:, pl.ds(at, part)],
                            out.at[pl.ds(piece * tokens, tokens)],
                            sems.at[which, piece],
                        )
                    )
            for copy in copies:
                copy.start()
            for copy in copies:
                copy.wait()

        @pl.when(section == 0)
        def _():
            move(a_ref)

        @pl.when(section != 0)
        def _():
            move(b_ref)

    return pl.pallas_call(
        kernel,
        out_shape=(jax.ShapeDtypeStruct((count, part), tokens_a.dtype),) * 2,
        in_specs=[smem(), anywhere(), anywhere()],
        out_specs=(vmem(), vmem()),
        scratch_shapes=[pltpu.SemaphoreType.DMA((2, PIECES))],
        compiler_params=params(16),
        cost_estimate=small_cost(),
        name="split_tokens",
    )(place, in_hbm(tokens_a), in_hbm(tokens_b))


def order_blocks(place, kept, arrived):
    count, part = kept.shape
    columns = parts_of(part)

    def kernel(place_ref, kept_ref, arrived_ref, *outs):
        def put(first_ref, second_ref):
            for block, ref in enumerate((first_ref, second_ref)):
                for number, lanes in enumerate(columns):
                    outs[2 * block + number][...] = ref[:, lanes]

        @pl.when(place_ref[1] == 0)
        def _():
            put(kept_ref, arrived_ref)

        @pl.when(place_ref[1] != 0)
        def _():
            put(arrived_ref, kept_ref)

    shapes = tuple(
        jax.ShapeDtypeStruct((count, lanes.stop - lanes.start), kept.dtype) for lanes in columns
    )
    outs = pl.pallas_call(
        kernel,
        out_shape=shapes * 2,
        in_specs=[smem(), vmem(), vmem()],
        out_specs=(vmem(),) * 4,
        compiler_params=params(16),
        cost_estimate=small_cost(),
        name="order_blocks",
    )(place, kept, arrived)
    return [list(outs[:2]), list(outs[2:])]


def join_rows(blocks):
    height, width = blocks[0].shape

    def kernel(*refs):
        sources, (out_ref, sems) = refs[:-2], refs[-2:]
        copies = [
            pltpu.make_async_copy(ref, out_ref.at[pl.ds(number * height, height)], sems.at[number])
            for number, ref in enumerate(sources)
        ]
        for copy in copies:
            copy.start()
        for copy in copies:
            copy.wait()

    return pl.pallas_call(
        kernel,
        out_shape=pltpu.HBM((height * len(blocks), width), blocks[0].dtype),
        in_specs=[anywhere()] * len(blocks),
        out_specs=anywhere(),
        scratch_shapes=[pltpu.SemaphoreType.DMA((len(blocks),))],
        compiler_params=params(16),
        cost_estimate=small_cost(),
        name="join_rows",
    )(*[in_vmem(block) for block in blocks])


def slots(routes, experts, capacity):
    flat = routes.reshape(routes.shape[:-2] + (-1,))
    order = jnp.arange(flat.shape[-1], dtype=jnp.int32)
    earlier = (flat[..., :, None] == flat[..., None, :]) & (order[None, :] < order[:, None])
    slot = flat * capacity + jnp.sum(earlier.astype(jnp.int32), axis=-1)
    return slot.reshape(routes.shape)


def shards(tokens_a, tokens_b, routes_a, routes_b, affinity_a, affinity_b, gate_w, up_w, down_w):
    sections = lax.axis_size("pp")
    devices = lax.axis_size("ep")
    experts = devices // 2
    token_count, width = tokens_a.shape
    half_width = width // 2
    capacity = 2 * (token_count * routes_a.shape[2] // devices) + 2
    section = lax.axis_index("pp")
    core = (lax.axis_index("ep") % 2).astype(jnp.int32)
    low = core == 0
    place = jnp.stack([section.astype(jnp.int32), core])
    own_half = core.reshape(1)
    gate, up, down = gate_w[0], up_w[0], down_w[0]

    one_core = [[2 * chip + side for chip in range(experts)] for side in range(2)]
    siblings = [(device, device ^ 1) for device in range(devices)]

    def exchange(wire):
        blocks = wire.reshape(experts, PIECES * capacity, wire.shape[1])
        moved = lax.all_to_all(
            blocks, "ep", split_axis=0, concat_axis=0, tiled=True, axis_index_groups=one_core
        )
        return moved.reshape(wire.shape)

    def to_sibling(block):
        return lax.ppermute(block, "ep", siblings)

    def by_block(mine, theirs):
        return jnp.where(low, mine, theirs), jnp.where(low, theirs, mine)

    def by_moment(pair):
        return jnp.stack([jnp.where(section == m, pair[0], pair[1]) for m in range(sections)])

    target = slots(jnp.stack([routes_a[0], routes_b[0]]), experts, capacity)
    target = by_moment(target)
    affinity = by_moment(jnp.stack([affinity_a[0], affinity_b[0]]))
    target = jnp.stack(by_block(target, to_sibling(target)), axis=1)
    affinity = jnp.stack(by_block(affinity, to_sibling(affinity)), axis=1)
    shift = jnp.arange(PIECES, dtype=jnp.int32)[:, None] * (experts * capacity)
    lines = target.swapaxes(2, 3)
    lines = (lines[:, :, :, None] + shift).reshape(lines.shape[:3] + (PIECES * token_count,))

    kept, leaving = split_tokens(place, tokens_a, tokens_b)
    part = kept.shape[1]
    chunks = order_blocks(place, kept, to_sibling(leaving))

    def leave(i, moment, after=()):
        first, select = dispatch_first(
            chunks[i][0], lines, part, moment, i, experts, capacity, after
        )
        return dispatch_second(chunks[i][1], select, first)

    def experts_of(wire):
        middle = wire.shape[0] // 2
        others = [to_sibling(wire[:middle]), to_sibling(wire[middle:])]
        own_gate, own_up = load_half(own_half, gate, up, wire, wire.shape[1])
        hidden, *blocks = hidden_units(
            own_half, wire, others, own_gate, own_up, gate, up, down, other_down, capacity
        )
        return down_rows(hidden, to_sibling(hidden), *blocks, capacity)

    states = ()
    first_leaving = leave(0, 0)
    first_wire = exchange(first_leaving)
    other_down = [to_sibling(block) for block in other_half(own_half, down, first_leaving, 8)]
    second_leaving, target, affinity, other_down = tie(
        (leave(1, 0), target, affinity, join_rows(other_down)), first_wire
    )
    for moment in range(sections):
        last = sections - 1 - moment
        hop = [(moment, moment + 1), (last, last - 1)]

        def settle(i, back):
            y, factors = combine_first(
                chunks[i][0], back, target, affinity, moment, i, experts, capacity
            )
            ys = [y, combine_second(chunks[i][1], back, factors)]
            after = record(place, ys, states, moment, i, sections)
            if moment + 1 == sections:
                return after, None
            chunks[i] = [lax.ppermute(y, "pp", hop) for y in ys]
            return after, leave(i, moment + 1, after[2:])

        second_wire = exchange(second_leaving)
        first_rows = experts_of(first_wire)
        (first_rows,) = tie((first_rows,), second_wire)
        first_back = exchange(first_rows)
        second_rows = experts_of(second_wire)
        (second_rows,) = tie((second_rows,), first_back)
        second_back = exchange(second_rows)
        states, first_leaving = settle(0, first_back)
        if moment + 1 < sections:
            (first_leaving,) = tie((first_leaving,), second_back)
            first_wire = exchange(first_leaving)
        states, second_leaving = settle(1, second_back)
        if moment + 1 < sections:
            (second_leaving,) = tie((second_leaving,), first_wire)
    forward, reverse, sent = states
    forward, reverse = finish(place, (forward, reverse), to_sibling(sent))
    return (forward[None], reverse[None])


def solution(mesh):
    placed = (
        P("ep", None),
        P("ep", None),
        P("pp", "ep", None),
        P("pp", "ep", None),
        P("pp", "ep", None),
        P("pp", "ep", None),
        P("pp", None, "ep"),
        P("pp", None, "ep"),
        P("pp", "ep", None),
    )
    return jax.shard_map(
        shards,
        mesh=mesh,
        in_specs=placed,
        out_specs=(P("pp", "ep", None), P("pp", "ep", None)),
        check_vma=False,
    )
```

```python
import jax
import jax.numpy as jnp
from jax import lax
from jax.experimental import pallas as pl
from jax.experimental.pallas import tpu as pltpu
from jax.sharding import PartitionSpec as P

MIB = 1 << 20
PIECES = 4
GROUP = 8


def vmem():
    return pl.BlockSpec(memory_space=pltpu.VMEM)


def smem():
    return pl.BlockSpec(memory_space=pltpu.SMEM)


def anywhere():
    return pl.BlockSpec(memory_space=pl.ANY)


def whole(array):
    return pl.BlockSpec(array.shape, lambda step: (0,) * len(array.shape))


def in_hbm(block):
    return pltpu.with_memory_space_constraint(block, pltpu.HBM)


def in_vmem(block):
    return pltpu.with_memory_space_constraint(block, pltpu.VMEM)


def params(mib):
    return pltpu.CompilerParams(vmem_limit_bytes=mib * MIB)


def small_cost():
    return pl.CostEstimate(flops=MIB, bytes_accessed=MIB, transcendentals=0)


def spans(width, step=256):
    return [slice(start, min(start + step, width)) for start in range(0, width, step)]


def split(index, size, count):
    factor = -(-(1 << 16) // size)
    assert all((n * factor) >> 16 == n // size for n in range(size * count))
    high = (index * factor) >> 16
    return high, index - high * size


def wire_codes(shape, axis, experts, capacity):
    index = lax.broadcasted_iota(jnp.int32, shape, axis)
    expert, rest = split(index, PIECES * capacity, experts)
    piece, slot = split(rest, capacity, PIECES)
    return (piece * experts + expert) * capacity + slot


def group_order(axis, capacity):
    size = GROUP * PIECES * capacity
    shape = (1, size) if axis == 1 else (size, 1)
    index = lax.broadcasted_iota(jnp.int32, shape, axis)
    chip, rest = split(index, PIECES * capacity, GROUP)
    piece, slot = split(rest, capacity, PIECES)
    place = (piece * GROUP + chip) * capacity + slot
    other = lax.broadcasted_iota(jnp.int32, (size, size), 1 - axis)
    return jnp.where(other == place, 1.0, 0.0).astype(jnp.bfloat16)


def tie_kernel(*refs):
    del refs


def tie(blocks, after):
    return pl.pallas_call(
        tie_kernel,
        out_shape=tuple(pltpu.HBM(x.shape, x.dtype) for x in blocks),
        in_specs=[anywhere()] * (len(blocks) + 1),
        out_specs=(anywhere(),) * len(blocks),
        input_output_aliases={n: n for n in range(len(blocks))},
        cost_estimate=pl.CostEstimate(flops=0, bytes_accessed=0, transcendentals=0),
        name="tie",
    )(*[in_hbm(x) for x in blocks], after)


def parts_of(width):
    first = -(-width // 256) * 128
    return (slice(0, first), slice(first, width))


def dispatch_first(x, lines, width, moment, block, experts, capacity, after):
    count, first = x.shape
    wire = experts * PIECES * capacity
    groups = 4
    lines_each = wire // groups

    def kernel(x_ref, line_ref, *rest):
        out_ref, select_ref, ready, sems = rest[-4:]
        lines = line_ref[0, 0]
        rows = wire_codes((wire, 1), 0, experts, capacity)
        copies = []
        for group in range(groups):
            place = slice(group * lines_each, (group + 1) * lines_each)
            hit = (rows[place] == lines[0:1, :]) | (rows[place] == lines[1:2, :])
            select = jnp.where(hit, 1.0, 0.0).astype(jnp.bfloat16)
            select_ref[place, :] = select
            for columns in spans(first):
                ready[place, columns] = jnp.dot(
                    select, x_ref[:, columns], preferred_element_type=jnp.float32
                ).astype(jnp.bfloat16)
            where = pl.ds(group * lines_each, lines_each)
            copies.append(
                pltpu.make_async_copy(
                    ready.at[where], out_ref.at[where, pl.ds(0, first)], sems.at[group]
                )
            )
            copies[-1].start()
        for copy in copies:
            copy.wait()

    return pl.pallas_call(
        kernel,
        out_shape=(
            pltpu.HBM((wire, width), jnp.bfloat16),
            jax.ShapeDtypeStruct((wire, count), jnp.bfloat16),
        ),
        grid=(1,),
        in_specs=[
            whole(x),
            pl.BlockSpec((1, 1) + lines.shape[2:], lambda step: (moment, block, 0, 0)),
        ]
        + [anywhere()] * len(after),
        out_specs=(anywhere(), pl.BlockSpec((wire, count), lambda step: (0, 0))),
        scratch_shapes=[
            pltpu.VMEM((wire, first), jnp.bfloat16),
            pltpu.SemaphoreType.DMA((groups,)),
        ],
        compiler_params=params(24),
        cost_estimate=small_cost(),
        name="dispatch_first",
    )(x, in_hbm(lines), *[in_hbm(block) for block in after])


def dispatch_second(x, select, wire_rows):
    second = x.shape[1]
    wire, width = wire_rows.shape
    groups = 4
    lines_each = wire // groups

    def kernel(x_ref, select_ref, wire_ref, out_ref, ready, sems):
        del wire_ref
        copies = []
        for group in range(groups):
            place = slice(group * lines_each, (group + 1) * lines_each)
            for columns in spans(second):
                ready[place, columns] = jnp.dot(
                    select_ref[place, :], x_ref[:, columns], preferred_element_type=jnp.float32
                ).astype(jnp.bfloat16)
            where = pl.ds(group * lines_each, lines_each)
            copies.append(
                pltpu.make_async_copy(
                    ready.at[where], out_ref.at[where, pl.ds(width - second, second)], sems.at[group]
                )
            )
            copies[-1].start()
        for copy in copies:
            copy.wait()

    return pl.pallas_call(
        kernel,
        out_shape=pltpu.HBM((wire, width), jnp.bfloat16),
        in_specs=[vmem(), vmem(), anywhere()],
        out_specs=anywhere(),
        input_output_aliases={2: 0},
        scratch_shapes=[
            pltpu.VMEM((wire, second), jnp.bfloat16),
            pltpu.SemaphoreType.DMA((groups,)),
        ],
        compiler_params=params(24),
        cost_estimate=small_cost(),
        name="dispatch_second",
    )(x, select, in_hbm(wire_rows))


def load_half(core, gate, up, after, part):
    units = gate.shape[1]

    def kernel(core_ref, gate_ref, up_ref, after_ref, gate_out, up_out, sems):
        del after_ref
        copies = []
        for piece in range(PIECES):
            lines = pl.ds(pl.multiple_of((core_ref[0] * PIECES + piece) * part, part), part)
            for number, (ref, out) in enumerate(((gate_ref, gate_out), (up_ref, up_out))):
                copies.append(
                    pltpu.make_async_copy(ref.at[lines], out.at[piece], sems.at[number, piece])
                )
        for copy in copies:
            copy.start()
        for copy in copies:
            copy.wait()

    return pl.pallas_call(
        kernel,
        out_shape=(jax.ShapeDtypeStruct((PIECES, part, units), gate.dtype),) * 2,
        in_specs=[smem()] + [anywhere()] * 3,
        out_specs=(vmem(),) * 2,
        scratch_shapes=[pltpu.SemaphoreType.DMA((2, PIECES))],
        compiler_params=params(16),
        cost_estimate=small_cost(),
        name="load_half",
    )(core, in_hbm(gate), in_hbm(up), in_hbm(after))


def hidden_units(core, own, others, own_gate, own_up, gate, up, down, other_down, capacity):
    wire_rows, part = own.shape
    rows_count = wire_rows // PIECES
    units = gate.shape[1]
    half_width = PIECES * part
    height = GROUP * capacity
    span = PIECES * height
    groups = rows_count // height

    def kernel(
        core_ref, own_ref, low_ref, high_ref, own_gate_ref, own_up_ref, gate_ref, up_ref,
        down_ref, other_down_ref, out_ref, down_out, other_down_out,
        wires, rows, gate_blocks, up_blocks, gate_sum, up_sum,
        wire_sems, gate_sems, up_sems, down_sems,
    ):
        core = core_ref[0]
        middle = wire_rows // 2
        wire_copies = [
            pltpu.make_async_copy(own_ref, wires.at[pl.ds(0, wire_rows)], wire_sems.at[0]),
            pltpu.make_async_copy(low_ref, wires.at[pl.ds(wire_rows, middle)], wire_sems.at[1]),
            pltpu.make_async_copy(
                high_ref, wires.at[pl.ds(wire_rows + middle, middle)], wire_sems.at[2]
            ),
        ]
        loads = []
        down_loads = []
        for piece in range(PIECES):
            lines = pl.ds(pl.multiple_of(((1 - core) * PIECES + piece) * part, part), part)
            loads += [
                pltpu.make_async_copy(gate_ref.at[lines], gate_blocks.at[piece], gate_sems.at[piece]),
                pltpu.make_async_copy(up_ref.at[lines], up_blocks.at[piece], up_sems.at[piece]),
            ]
            place = pl.ds(pl.multiple_of((core * PIECES + piece) * part, part), part)
            down_loads += [
                pltpu.make_async_copy(
                    down_ref.at[:, place], down_out.at[piece], down_sems.at[0, piece]
                ),
                pltpu.make_async_copy(
                    other_down_ref.at[:, pl.ds(piece * part, part)],
                    other_down_out.at[piece],
                    down_sems.at[1, piece],
                ),
            ]
        for copy in wire_copies + loads:
            copy.start()
        order = group_order(1, capacity)
        squares = 0.0
        for step in range(2 * PIECES):
            piece = step % PIECES
            mine = step < PIECES
            if piece == 0:
                base = 0 if mine else wire_rows
                for copy in wire_copies[:1] if mine else wire_copies[1:]:
                    copy.wait()
                for group in range(groups):
                    for columns in spans(part):
                        ordered = jnp.dot(
                            order,
                            wires[base + group * span : base + (group + 1) * span, columns],
                            preferred_element_type=jnp.float32,
                        ).astype(jnp.bfloat16)
                        for number in range(PIECES):
                            rows[
                                group * height : (group + 1) * height,
                                number * part + columns.start : number * part + columns.stop,
                            ] = ordered[number * height : (number + 1) * height]
            if mine:
                down_loads[2 * piece].start()
                down_loads[2 * piece + 1].start()
                gate_block, up_block = own_gate_ref[piece], own_up_ref[piece]
            else:
                loads[2 * piece].wait()
                loads[2 * piece + 1].wait()
                gate_block, up_block = gate_blocks[piece], up_blocks[piece]
            values = rows[:, piece * part : (piece + 1) * part]
            gate = jnp.dot(values, gate_block, preferred_element_type=jnp.float32)
            up = jnp.dot(values, up_block, preferred_element_type=jnp.float32)
            if step == 0:
                gate_sum[...], up_sum[...] = gate, up
            else:
                gate_sum[...] += gate
                up_sum[...] += up
            for columns in spans(part, 128):
                few = values[:, columns].astype(jnp.float32)
                squares += few * few
        mean = jnp.sum(squares, axis=-1, keepdims=True) / (2 * half_width)
        scale = lax.rsqrt(mean + 1e-06)
        out_ref[...] = (jax.nn.silu(gate_sum[...] * scale) * (up_sum[...] * scale)).astype(
            jnp.bfloat16
        )
        for copy in down_loads:
            copy.wait()

    blocks = jax.ShapeDtypeStruct((PIECES, units, part), down.dtype)
    return pl.pallas_call(
        kernel,
        out_shape=(jax.ShapeDtypeStruct((rows_count, units), jnp.bfloat16), blocks, blocks),
        in_specs=[smem()] + [anywhere()] * 3 + [vmem()] * 2 + [anywhere()] * 4,
        out_specs=(vmem(),) * 3,
        scratch_shapes=[
            pltpu.VMEM((2 * wire_rows, part), jnp.bfloat16),
            pltpu.VMEM((rows_count, half_width), jnp.bfloat16),
            pltpu.VMEM((PIECES, part, units), jnp.bfloat16),
            pltpu.VMEM((PIECES, part, units), jnp.bfloat16),
            pltpu.VMEM((rows_count, units), jnp.float32),
            pltpu.VMEM((rows_count, units), jnp.float32),
            pltpu.SemaphoreType.DMA((3,)),
            pltpu.SemaphoreType.DMA((PIECES,)),
            pltpu.SemaphoreType.DMA((PIECES,)),
            pltpu.SemaphoreType.DMA((2, PIECES)),
        ],
        compiler_params=params(32),
        cost_estimate=small_cost(),
        name="hidden_units",
    )(
        core, in_hbm(own), *others, own_gate, own_up,
        *[in_hbm(block) for block in (gate, up, down, other_down)],
    )


def down_rows(hidden, other_hidden, blocks, other_blocks, capacity):
    rows, units = hidden.shape
    part = blocks.shape[2]
    height = GROUP * capacity
    span = PIECES * height
    groups = rows // height

    def kernel(
        hidden_ref, other_ref, blocks_ref, other_blocks_ref, out_ref, stacked, ready, out_sems
    ):
        order = group_order(0, capacity)
        for piece in range(PIECES):
            total = jnp.dot(hidden_ref[...], blocks_ref[piece], preferred_element_type=jnp.float32)
            total += jnp.dot(
                other_ref[...], other_blocks_ref[piece], preferred_element_type=jnp.float32
            )
            total = total.astype(jnp.bfloat16)
            for group in range(groups):
                at = group * span + piece * height
                stacked[at : at + height, :] = total[group * height : (group + 1) * height]
        copies = []
        for group in range(groups):
            lines = slice(group * span, (group + 1) * span)
            for columns in spans(part):
                ready[lines, columns] = jnp.dot(
                    order, stacked[lines, columns], preferred_element_type=jnp.float32
                ).astype(jnp.bfloat16)
            where = pl.ds(group * span, span)
            copies.append(
                pltpu.make_async_copy(ready.at[where], out_ref.at[where], out_sems.at[group])
            )
            copies[-1].start()
        for copy in copies:
            copy.wait()

    return pl.pallas_call(
        kernel,
        out_shape=pltpu.HBM((rows * PIECES, part), jnp.bfloat16),
        in_specs=[vmem()] * 4,
        out_specs=anywhere(),
        scratch_shapes=[
            pltpu.VMEM((rows * PIECES, part), jnp.bfloat16),
            pltpu.VMEM((rows * PIECES, part), jnp.bfloat16),
            pltpu.SemaphoreType.DMA((groups,)),
        ],
        compiler_params=params(24),
        cost_estimate=small_cost(),
        name="down_rows",
    )(hidden, other_hidden, blocks, other_blocks)


def other_half(core, down, after, count):
    units, width = down.shape
    half_width = width // 2
    height = units // count

    def kernel(core_ref, down_ref, after_ref, *rest):
        del after_ref
        outs, sems = rest[:-1], rest[-1]
        place = pl.ds(pl.multiple_of((1 - core_ref[0]) * half_width, half_width), half_width)
        copies = [
            pltpu.make_async_copy(
                down_ref.at[pl.ds(number * height, height), place], out, sems.at[number]
            )
            for number, out in enumerate(outs)
        ]
        for copy in copies:
            copy.start()
        for copy in copies:
            copy.wait()

    return pl.pallas_call(
        kernel,
        out_shape=(jax.ShapeDtypeStruct((height, half_width), down.dtype),) * count,
        in_specs=[smem()] + [anywhere()] * 2,
        out_specs=(vmem(),) * count,
        scratch_shapes=[pltpu.SemaphoreType.DMA((count,))],
        compiler_params=params(24),
        cost_estimate=small_cost(),
        name="other_half",
    )(core, in_hbm(down), in_hbm(after))


def combine_first(x, wire, columns, weights, moment, block, experts, capacity):
    count, first = x.shape
    wire_rows = wire.shape[0]

    def kernel(x_ref, wire_ref, column_ref, weight_ref, y_ref, factors, held, sem):
        copy = pltpu.make_async_copy(wire_ref.at[:, pl.ds(0, first)], held, sem.at[0])
        copy.start()
        rows = wire_codes((1, wire_rows), 1, experts, capacity)
        codes, shares = column_ref[0, 0], weight_ref[0, 0]
        codes = jnp.concatenate([codes + piece * (experts * capacity) for piece in range(PIECES)])
        shares = jnp.concatenate([shares] * PIECES)
        table = jnp.where(rows == codes[:, 0:1], shares[:, 0:1], 0.0)
        table += jnp.where(rows == codes[:, 1:2], shares[:, 1:2], 0.0)
        high = table.astype(jnp.bfloat16)
        factors[:count, :] = high
        factors[count:, :] = (table - high.astype(jnp.float32)).astype(jnp.bfloat16)
        copy.wait()
        for lanes in spans(first):
            both = jnp.dot(factors[...], held[:, lanes], preferred_element_type=jnp.float32)
            y_ref[:, lanes] = (
                x_ref[:, lanes].astype(jnp.float32) + both[:count, :] + both[count:, :]
            ).astype(jnp.bfloat16)

    per_block = lambda array: pl.BlockSpec(
        (1, 1) + array.shape[2:], lambda step: (moment, block, 0, 0)
    )
    return pl.pallas_call(
        kernel,
        out_shape=(
            jax.ShapeDtypeStruct((count, first), x.dtype),
            jax.ShapeDtypeStruct((2 * count, wire_rows), jnp.bfloat16),
        ),
        grid=(1,),
        in_specs=[whole(x), anywhere(), per_block(columns), per_block(weights)],
        out_specs=(
            pl.BlockSpec((count, first), lambda step: (0, 0)),
            pl.BlockSpec((2 * count, wire_rows), lambda step: (0, 0)),
        ),
        scratch_shapes=[
            pltpu.VMEM((wire_rows, first), jnp.bfloat16),
            pltpu.SemaphoreType.DMA((1,)),
        ],
        compiler_params=params(24),
        cost_estimate=small_cost(),
        name="combine_first",
    )(in_hbm(x), in_hbm(wire), in_hbm(columns), in_hbm(weights))


def combine_second(x, wire, factors):
    count, second = x.shape
    wire_rows, width = wire.shape

    def kernel(x_ref, wire_ref, factor_ref, y_ref, held, start, sems):
        copies = [
            pltpu.make_async_copy(
                wire_ref.at[:, pl.ds(width - second, second)], held, sems.at[0]
            ),
            pltpu.make_async_copy(x_ref, start, sems.at[1]),
        ]
        for copy in copies:
            copy.start()
        for copy in copies:
            copy.wait()
        for lanes in spans(second):
            both = jnp.dot(factor_ref[...], held[:, lanes], preferred_element_type=jnp.float32)
            y_ref[:, lanes] = (
                start[:, lanes].astype(jnp.float32) + both[:count, :] + both[count:, :]
            ).astype(jnp.bfloat16)

    return pl.pallas_call(
        kernel,
        out_shape=jax.ShapeDtypeStruct((count, second), x.dtype),
        in_specs=[anywhere(), anywhere(), vmem()],
        out_specs=vmem(),
        scratch_shapes=[
            pltpu.VMEM((wire_rows, second), jnp.bfloat16),
            pltpu.VMEM((count, second), x.dtype),
            pltpu.SemaphoreType.DMA((2,)),
        ],
        compiler_params=params(24),
        cost_estimate=small_cost(),
        name="combine_second",
    )(in_hbm(x), in_hbm(wire), factors)


def record(place, ys, states, moment, block, sections):
    count = ys[0].shape[0]
    tokens = count // PIECES
    widths = [y.shape[1] for y in ys]
    part = sum(widths)
    starts = (0, widths[0])

    def kernel(place_ref, first_ref, second_ref, *rest):
        forward_ref, reverse_ref, sent_ref, sems = rest[-4:]
        section, core = place_ref[0], place_ref[1]
        for number, (state_ref, turn) in enumerate(
            ((forward_ref, moment), (reverse_ref, sections - 1 - moment))
        ):

            @pl.when((section == turn) & (core == block))
            def _():
                copies = []
                for which, y_ref in enumerate((first_ref, second_ref)):
                    for piece in range(PIECES):
                        at = (block * PIECES + piece) * part + starts[which]
                        copies.append(
                            pltpu.make_async_copy(
                                y_ref.at[pl.ds(piece * tokens, tokens)],
                                state_ref.at[:, pl.ds(at, widths[which])],
                                sems.at[number, which * PIECES + piece],
                            )
                        )
                for copy in copies:
                    copy.start()
                for copy in copies:
                    copy.wait()

            @pl.when((section == turn) & (core != block))
            def _():
                copies = [
                    pltpu.make_async_copy(
                        y_ref,
                        sent_ref.at[number, :, pl.ds(starts[which], widths[which])],
                        sems.at[number, which],
                    )
                    for which, y_ref in enumerate((first_ref, second_ref))
                ]
                for copy in copies:
                    copy.start()
                for copy in copies:
                    copy.wait()

    result = pltpu.HBM((tokens, 2 * PIECES * part), ys[0].dtype)
    return pl.pallas_call(
        kernel,
        out_shape=(result, result, pltpu.HBM((2, count, part), ys[0].dtype)),
        in_specs=[smem()] + [anywhere()] * (2 + len(states)),
        out_specs=(anywhere(),) * 3,
        input_output_aliases={3 + n: n for n in range(len(states))},
        scratch_shapes=[pltpu.SemaphoreType.DMA((2, 2 * PIECES))],
        cost_estimate=small_cost(),
        name="record",
    )(place, *[in_vmem(y) for y in ys], *[in_hbm(state) for state in states])


def finish(place, states, arrived):
    count, part = arrived.shape[1:]
    tokens = count // PIECES

    def kernel(place_ref, forward_in, reverse_in, arrived_ref, forward_ref, reverse_ref, sems):
        del forward_in, reverse_in
        half = 1 - place_ref[1]
        copies = []
        for number, ref in enumerate((forward_ref, reverse_ref)):
            for piece in range(PIECES):
                at = pl.multiple_of((half * PIECES + piece) * part, part)
                copies.append(
                    pltpu.make_async_copy(
                        arrived_ref.at[number, pl.ds(piece * tokens, tokens)],
                        ref.at[:, pl.ds(at, part)],
                        sems.at[number, piece],
                    )
                )
        for copy in copies:
            copy.start()
        for copy in copies:
            copy.wait()

    return pl.pallas_call(
        kernel,
        out_shape=tuple(pltpu.HBM(state.shape, state.dtype) for state in states),
        in_specs=[smem()] + [anywhere()] * 3,
        out_specs=(anywhere(),) * 2,
        input_output_aliases={1: 0, 2: 1},
        scratch_shapes=[pltpu.SemaphoreType.DMA((2, PIECES))],
        name="finish",
    )(place, *[in_hbm(state) for state in states], in_vmem(arrived))


def split_tokens(place, tokens_a, tokens_b):
    tokens, width = tokens_a.shape
    part = width // 2 // PIECES
    count = PIECES * tokens

    def kernel(place_ref, a_ref, b_ref, kept_ref, leaving_ref, sems):
        section, core = place_ref[0], place_ref[1]

        def move(ref):
            copies = []
            for which, (half, out) in enumerate(((core, kept_ref), (1 - core, leaving_ref))):
                for piece in range(PIECES):
                    at = pl.multiple_of((half * PIECES + piece) * part, part)
                    copies.append(
                        pltpu.make_async_copy(
                            ref.at[:, pl.ds(at, part)],
                            out.at[pl.ds(piece * tokens, tokens)],
                            sems.at[which, piece],
                        )
                    )
            for copy in copies:
                copy.start()
            for copy in copies:
                copy.wait()

        @pl.when(section == 0)
        def _():
            move(a_ref)

        @pl.when(section != 0)
        def _():
            move(b_ref)

    return pl.pallas_call(
        kernel,
        out_shape=(jax.ShapeDtypeStruct((count, part), tokens_a.dtype),) * 2,
        in_specs=[smem(), anywhere(), anywhere()],
        out_specs=(vmem(), vmem()),
        scratch_shapes=[pltpu.SemaphoreType.DMA((2, PIECES))],
        compiler_params=params(16),
        cost_estimate=small_cost(),
        name="split_tokens",
    )(place, in_hbm(tokens_a), in_hbm(tokens_b))


def order_blocks(place, kept, arrived):
    count, part = kept.shape
    columns = parts_of(part)

    def kernel(place_ref, kept_ref, arrived_ref, *outs):
        def put(first_ref, second_ref):
            for block, ref in enumerate((first_ref, second_ref)):
                for number, lanes in enumerate(columns):
                    outs[2 * block + number][...] = ref[:, lanes]

        @pl.when(place_ref[1] == 0)
        def _():
            put(kept_ref, arrived_ref)

        @pl.when(place_ref[1] != 0)
        def _():
            put(arrived_ref, kept_ref)

    shapes = tuple(
        jax.ShapeDtypeStruct((count, lanes.stop - lanes.start), kept.dtype) for lanes in columns
    )
    outs = pl.pallas_call(
        kernel,
        out_shape=shapes * 2,
        in_specs=[smem(), vmem(), vmem()],
        out_specs=(vmem(),) * 4,
        compiler_params=params(16),
        cost_estimate=small_cost(),
        name="order_blocks",
    )(place, kept, arrived)
    return [list(outs[:2]), list(outs[2:])]


def join_rows(blocks):
    height, width = blocks[0].shape
    count = len(blocks)

    def kernel(*refs):
        sources, (out_ref, held, in_sems, out_sems) = refs[:count], refs[count:]
        arriving, leaving = [], []
        for number, ref in enumerate(sources):
            lines = pl.ds(number * height, height)
            arriving.append(pltpu.make_async_copy(ref, held.at[lines], in_sems.at[number]))
            leaving.append(
                pltpu.make_async_copy(held.at[lines], out_ref.at[lines], out_sems.at[number])
            )
        for copy in arriving:
            copy.start()
        for first, second in zip(arriving, leaving):
            first.wait()
            second.start()
        for copy in leaving:
            copy.wait()

    return pl.pallas_call(
        kernel,
        out_shape=pltpu.HBM((height * count, width), blocks[0].dtype),
        in_specs=[anywhere()] * count,
        out_specs=anywhere(),
        scratch_shapes=[
            pltpu.VMEM((height * count, width), blocks[0].dtype),
            pltpu.SemaphoreType.DMA((count,)),
            pltpu.SemaphoreType.DMA((count,)),
        ],
        compiler_params=params(16),
        cost_estimate=small_cost(),
        name="join_rows",
    )(*blocks)


def slots(routes, experts, capacity):
    flat = routes.reshape(routes.shape[:-2] + (-1,))
    order = jnp.arange(flat.shape[-1], dtype=jnp.int32)
    earlier = (flat[..., :, None] == flat[..., None, :]) & (order[None, :] < order[:, None])
    slot = flat * capacity + jnp.sum(earlier.astype(jnp.int32), axis=-1)
    return slot.reshape(routes.shape)


def shards(tokens_a, tokens_b, routes_a, routes_b, affinity_a, affinity_b, gate_w, up_w, down_w):
    sections = lax.axis_size("pp")
    devices = lax.axis_size("ep")
    experts = devices // 2
    token_count, width = tokens_a.shape
    half_width = width // 2
    capacity = 2 * (token_count * routes_a.shape[2] // devices) + 2
    section = lax.axis_index("pp")
    core = (lax.axis_index("ep") % 2).astype(jnp.int32)
    low = core == 0
    place = jnp.stack([section.astype(jnp.int32), core])
    own_half = core.reshape(1)
    gate, up, down = gate_w[0], up_w[0], down_w[0]

    one_core = [[2 * chip + side for chip in range(experts)] for side in range(2)]
    siblings = [(device, device ^ 1) for device in range(devices)]

    def exchange(wire):
        blocks = wire.reshape(experts, PIECES * capacity, wire.shape[1])
        moved = lax.all_to_all(
            blocks, "ep", split_axis=0, concat_axis=0, tiled=True, axis_index_groups=one_core
        )
        return moved.reshape(wire.shape)

    def to_sibling(block):
        return lax.ppermute(block, "ep", siblings)

    def by_block(mine, theirs):
        return jnp.where(low, mine, theirs), jnp.where(low, theirs, mine)

    def by_moment(pair):
        return jnp.stack([jnp.where(section == m, pair[0], pair[1]) for m in range(sections)])

    target = slots(jnp.stack([routes_a[0], routes_b[0]]), experts, capacity)
    target = by_moment(target)
    affinity = by_moment(jnp.stack([affinity_a[0], affinity_b[0]]))
    target = jnp.stack(by_block(target, to_sibling(target)), axis=1)
    affinity = jnp.stack(by_block(affinity, to_sibling(affinity)), axis=1)
    shift = jnp.arange(PIECES, dtype=jnp.int32)[:, None] * (experts * capacity)
    lines = target.swapaxes(2, 3)
    lines = (lines[:, :, :, None] + shift).reshape(lines.shape[:3] + (PIECES * token_count,))

    kept, leaving = split_tokens(place, tokens_a, tokens_b)
    part = kept.shape[1]
    chunks = order_blocks(place, kept, to_sibling(leaving))

    def leave(i, moment, after=()):
        first, select = dispatch_first(
            chunks[i][0], lines, part, moment, i, experts, capacity, after
        )
        return dispatch_second(chunks[i][1], select, first)

    def experts_of(wire):
        middle = wire.shape[0] // 2
        others = [to_sibling(wire[:middle]), to_sibling(wire[middle:])]
        own_gate, own_up = load_half(own_half, gate, up, wire, wire.shape[1])
        hidden, *blocks = hidden_units(
            own_half, wire, others, own_gate, own_up, gate, up, down, other_down, capacity
        )
        return down_rows(hidden, to_sibling(hidden), *blocks, capacity)

    states = ()
    first_leaving = leave(0, 0)
    first_wire = exchange(first_leaving)
    other_down = [to_sibling(block) for block in other_half(own_half, down, first_leaving, 8)]
    second_leaving, target, affinity, other_down = tie(
        (leave(1, 0), target, affinity, join_rows(other_down)), first_wire
    )
    for moment in range(sections):
        last = sections - 1 - moment
        hop = [(moment, moment + 1), (last, last - 1)]

        def settle(i, back):
            y, factors = combine_first(
                chunks[i][0], back, target, affinity, moment, i, experts, capacity
            )
            ys = [y, combine_second(chunks[i][1], back, factors)]
            after = record(place, ys, states, moment, i, sections)
            if moment + 1 == sections:
                return after, None
            chunks[i] = [lax.ppermute(y, "pp", hop) for y in ys]
            return after, leave(i, moment + 1, after[2:])

        second_wire = exchange(second_leaving)
        first_rows = experts_of(first_wire)
        (first_rows,) = tie((first_rows,), second_wire)
        first_back = exchange(first_rows)
        second_rows = experts_of(second_wire)
        (second_rows,) = tie((second_rows,), first_back)
        second_back = exchange(second_rows)
        states, first_leaving = settle(0, first_back)
        if moment + 1 < sections:
            (first_leaving,) = tie((first_leaving,), second_back)
            first_wire = exchange(first_leaving)
        states, second_leaving = settle(1, second_back)
        if moment + 1 < sections:
            (second_leaving,) = tie((second_leaving,), first_wire)
    forward, reverse, sent = states
    forward, reverse = finish(place, (forward, reverse), to_sibling(sent))
    return (forward[None], reverse[None])


def solution(mesh):
    placed = (
        P("ep", None),
        P("ep", None),
        P("pp", "ep", None),
        P("pp", "ep", None),
        P("pp", "ep", None),
        P("pp", "ep", None),
        P("pp", None, "ep"),
        P("pp", None, "ep"),
        P("pp", "ep", None),
    )
    return jax.shard_map(
        shards,
        mesh=mesh,
        in_specs=placed,
        out_specs=(P("pp", "ep", None), P("pp", "ep", None)),
        check_vma=False,
    )
```

```python
import jax
import jax.numpy as jnp
from jax import lax
from jax.experimental import pallas as pl
from jax.experimental.pallas import tpu as pltpu
from jax.sharding import PartitionSpec as P

MIB = 1 << 20
PIECES = 4
GROUP = 8


def vmem():
    return pl.BlockSpec(memory_space=pltpu.VMEM)


def smem():
    return pl.BlockSpec(memory_space=pltpu.SMEM)


def anywhere():
    return pl.BlockSpec(memory_space=pl.ANY)


def whole(array):
    return pl.BlockSpec(array.shape, lambda step: (0,) * len(array.shape))


def in_hbm(block):
    return pltpu.with_memory_space_constraint(block, pltpu.HBM)


def in_vmem(block):
    return pltpu.with_memory_space_constraint(block, pltpu.VMEM)


def params(mib):
    return pltpu.CompilerParams(vmem_limit_bytes=mib * MIB)


def small_cost():
    return pl.CostEstimate(flops=MIB, bytes_accessed=MIB, transcendentals=0)


def spans(width, step=256):
    return [slice(start, min(start + step, width)) for start in range(0, width, step)]


def split(index, size, count):
    factor = -(-(1 << 16) // size)
    assert all((n * factor) >> 16 == n // size for n in range(size * count))
    high = (index * factor) >> 16
    return high, index - high * size


def wire_codes(shape, axis, experts, capacity):
    index = lax.broadcasted_iota(jnp.int32, shape, axis)
    expert, rest = split(index, PIECES * capacity, experts)
    piece, slot = split(rest, capacity, PIECES)
    return (piece * experts + expert) * capacity + slot


def group_order(axis, capacity):
    size = GROUP * PIECES * capacity
    shape = (1, size) if axis == 1 else (size, 1)
    index = lax.broadcasted_iota(jnp.int32, shape, axis)
    chip, rest = split(index, PIECES * capacity, GROUP)
    piece, slot = split(rest, capacity, PIECES)
    place = (piece * GROUP + chip) * capacity + slot
    other = lax.broadcasted_iota(jnp.int32, (size, size), 1 - axis)
    return jnp.where(other == place, 1.0, 0.0).astype(jnp.bfloat16)


def tie_kernel(*refs):
    del refs


def tie(blocks, after):
    return pl.pallas_call(
        tie_kernel,
        out_shape=tuple(pltpu.HBM(x.shape, x.dtype) for x in blocks),
        in_specs=[anywhere()] * (len(blocks) + 1),
        out_specs=(anywhere(),) * len(blocks),
        input_output_aliases={n: n for n in range(len(blocks))},
        cost_estimate=pl.CostEstimate(flops=0, bytes_accessed=0, transcendentals=0),
        name="tie",
    )(*[in_hbm(x) for x in blocks], after)


def parts_of(width):
    first = -(-width // 256) * 128
    return (slice(0, first), slice(first, width))


def dispatch_first(x, lines, width, moment, block, experts, capacity, after):
    count, first = x.shape
    wire = experts * PIECES * capacity
    groups = 4
    lines_each = wire // groups

    def kernel(x_ref, line_ref, *rest):
        out_ref, select_ref, ready, sems = rest[-4:]
        lines = line_ref[0, 0]
        rows = wire_codes((wire, 1), 0, experts, capacity)
        copies = []
        for group in range(groups):
            place = slice(group * lines_each, (group + 1) * lines_each)
            hit = (rows[place] == lines[0:1, :]) | (rows[place] == lines[1:2, :])
            select = jnp.where(hit, 1.0, 0.0).astype(jnp.bfloat16)
            select_ref[place, :] = select
            for columns in spans(first):
                ready[place, columns] = jnp.dot(
                    select, x_ref[:, columns], preferred_element_type=jnp.float32
                ).astype(jnp.bfloat16)
            where = pl.ds(group * lines_each, lines_each)
            copies.append(
                pltpu.make_async_copy(
                    ready.at[where], out_ref.at[where, pl.ds(0, first)], sems.at[group]
                )
            )
            copies[-1].start()
        for copy in copies:
            copy.wait()

    return pl.pallas_call(
        kernel,
        out_shape=(
            pltpu.HBM((wire, width), jnp.bfloat16),
            jax.ShapeDtypeStruct((wire, count), jnp.bfloat16),
        ),
        grid=(1,),
        in_specs=[
            whole(x),
            pl.BlockSpec((1, 1) + lines.shape[2:], lambda step: (moment, block, 0, 0)),
        ]
        + [anywhere()] * len(after),
        out_specs=(anywhere(), pl.BlockSpec((wire, count), lambda step: (0, 0))),
        scratch_shapes=[
            pltpu.VMEM((wire, first), jnp.bfloat16),
            pltpu.SemaphoreType.DMA((groups,)),
        ],
        compiler_params=params(24),
        cost_estimate=small_cost(),
        name="dispatch_first",
    )(x, in_hbm(lines), *[in_hbm(block) for block in after])


def dispatch_second(x, select, wire_rows):
    second = x.shape[1]
    wire, width = wire_rows.shape
    groups = 4
    lines_each = wire // groups

    def kernel(x_ref, select_ref, wire_ref, out_ref, ready, sems):
        del wire_ref
        copies = []
        for group in range(groups):
            place = slice(group * lines_each, (group + 1) * lines_each)
            for columns in spans(second):
                ready[place, columns] = jnp.dot(
                    select_ref[place, :], x_ref[:, columns], preferred_element_type=jnp.float32
                ).astype(jnp.bfloat16)
            where = pl.ds(group * lines_each, lines_each)
            copies.append(
                pltpu.make_async_copy(
                    ready.at[where], out_ref.at[where, pl.ds(width - second, second)], sems.at[group]
                )
            )
            copies[-1].start()
        for copy in copies:
            copy.wait()

    return pl.pallas_call(
        kernel,
        out_shape=pltpu.HBM((wire, width), jnp.bfloat16),
        in_specs=[vmem(), vmem(), anywhere()],
        out_specs=anywhere(),
        input_output_aliases={2: 0},
        scratch_shapes=[
            pltpu.VMEM((wire, second), jnp.bfloat16),
            pltpu.SemaphoreType.DMA((groups,)),
        ],
        compiler_params=params(24),
        cost_estimate=small_cost(),
        name="dispatch_second",
    )(x, select, in_hbm(wire_rows))


def load_half(core, gate, up, after, part):
    units = gate.shape[1]

    def kernel(core_ref, gate_ref, up_ref, after_ref, gate_out, up_out, sems):
        del after_ref
        copies = []
        for piece in range(PIECES):
            lines = pl.ds(pl.multiple_of((core_ref[0] * PIECES + piece) * part, part), part)
            for number, (ref, out) in enumerate(((gate_ref, gate_out), (up_ref, up_out))):
                copies.append(
                    pltpu.make_async_copy(ref.at[lines], out.at[piece], sems.at[number, piece])
                )
        for copy in copies:
            copy.start()
        for copy in copies:
            copy.wait()

    return pl.pallas_call(
        kernel,
        out_shape=(jax.ShapeDtypeStruct((PIECES, part, units), gate.dtype),) * 2,
        in_specs=[smem()] + [anywhere()] * 3,
        out_specs=(vmem(),) * 2,
        scratch_shapes=[pltpu.SemaphoreType.DMA((2, PIECES))],
        compiler_params=params(16),
        cost_estimate=small_cost(),
        name="load_half",
    )(core, in_hbm(gate), in_hbm(up), in_hbm(after))


def hidden_units(core, own, others, own_gate, own_up, gate, up, down, other_down, capacity):
    wire_rows, part = own.shape
    rows_count = wire_rows // PIECES
    units = gate.shape[1]
    half_width = PIECES * part
    height = GROUP * capacity
    span = PIECES * height
    groups = rows_count // height

    def kernel(
        core_ref, own_ref, low_ref, high_ref, own_gate_ref, own_up_ref, gate_ref, up_ref,
        down_ref, other_down_ref, out_ref, down_out, other_down_out,
        wires, rows, gate_blocks, up_blocks, gate_sum, up_sum,
        wire_sems, gate_sems, up_sems, down_sems,
    ):
        core = core_ref[0]
        middle = wire_rows // 2
        wire_copies = [
            pltpu.make_async_copy(own_ref, wires.at[pl.ds(0, wire_rows)], wire_sems.at[0]),
            pltpu.make_async_copy(low_ref, wires.at[pl.ds(wire_rows, middle)], wire_sems.at[1]),
            pltpu.make_async_copy(
                high_ref, wires.at[pl.ds(wire_rows + middle, middle)], wire_sems.at[2]
            ),
        ]
        loads = []
        down_loads = []
        for piece in range(PIECES):
            lines = pl.ds(pl.multiple_of(((1 - core) * PIECES + piece) * part, part), part)
            loads += [
                pltpu.make_async_copy(gate_ref.at[lines], gate_blocks.at[piece], gate_sems.at[piece]),
                pltpu.make_async_copy(up_ref.at[lines], up_blocks.at[piece], up_sems.at[piece]),
            ]
            place = pl.ds(pl.multiple_of((core * PIECES + piece) * part, part), part)
            down_loads += [
                pltpu.make_async_copy(
                    down_ref.at[:, place], down_out.at[piece], down_sems.at[0, piece]
                ),
                pltpu.make_async_copy(
                    other_down_ref.at[:, pl.ds(piece * part, part)],
                    other_down_out.at[piece],
                    down_sems.at[1, piece],
                ),
            ]
        for copy in wire_copies + loads:
            copy.start()
        order = group_order(1, capacity)
        squares = 0.0
        for step in range(2 * PIECES):
            piece = step % PIECES
            mine = step < PIECES
            if piece == 0:
                base = 0 if mine else wire_rows
                for copy in wire_copies[:1] if mine else wire_copies[1:]:
                    copy.wait()
                for group in range(groups):
                    for columns in spans(part):
                        ordered = jnp.dot(
                            order,
                            wires[base + group * span : base + (group + 1) * span, columns],
                            preferred_element_type=jnp.float32,
                        ).astype(jnp.bfloat16)
                        for number in range(PIECES):
                            rows[
                                group * height : (group + 1) * height,
                                number * part + columns.start : number * part + columns.stop,
                            ] = ordered[number * height : (number + 1) * height]
            if mine:
                down_loads[2 * piece].start()
                down_loads[2 * piece + 1].start()
                gate_block, up_block = own_gate_ref[piece], own_up_ref[piece]
            else:
                loads[2 * piece].wait()
                loads[2 * piece + 1].wait()
                gate_block, up_block = gate_blocks[piece], up_blocks[piece]
            values = rows[:, piece * part : (piece + 1) * part]
            gate = jnp.dot(values, gate_block, preferred_element_type=jnp.float32)
            up = jnp.dot(values, up_block, preferred_element_type=jnp.float32)
            if step == 0:
                gate_sum[...], up_sum[...] = gate, up
            else:
                gate_sum[...] += gate
                up_sum[...] += up
            for columns in spans(part, 128):
                few = values[:, columns].astype(jnp.float32)
                squares += few * few
        mean = jnp.sum(squares, axis=-1, keepdims=True) / (2 * half_width)
        scale = lax.rsqrt(mean + 1e-06)
        out_ref[...] = (jax.nn.silu(gate_sum[...] * scale) * (up_sum[...] * scale)).astype(
            jnp.bfloat16
        )
        for copy in down_loads:
            copy.wait()

    blocks = jax.ShapeDtypeStruct((PIECES, units, part), down.dtype)
    return pl.pallas_call(
        kernel,
        out_shape=(jax.ShapeDtypeStruct((rows_count, units), jnp.bfloat16), blocks, blocks),
        in_specs=[smem()] + [anywhere()] * 3 + [vmem()] * 2 + [anywhere()] * 4,
        out_specs=(vmem(),) * 3,
        scratch_shapes=[
            pltpu.VMEM((2 * wire_rows, part), jnp.bfloat16),
            pltpu.VMEM((rows_count, half_width), jnp.bfloat16),
            pltpu.VMEM((PIECES, part, units), jnp.bfloat16),
            pltpu.VMEM((PIECES, part, units), jnp.bfloat16),
            pltpu.VMEM((rows_count, units), jnp.float32),
            pltpu.VMEM((rows_count, units), jnp.float32),
            pltpu.SemaphoreType.DMA((3,)),
            pltpu.SemaphoreType.DMA((PIECES,)),
            pltpu.SemaphoreType.DMA((PIECES,)),
            pltpu.SemaphoreType.DMA((2, PIECES)),
        ],
        compiler_params=params(32),
        cost_estimate=small_cost(),
        name="hidden_units",
    )(
        core, in_hbm(own), *others, own_gate, own_up,
        *[in_hbm(block) for block in (gate, up, down, other_down)],
    )


def down_rows(hidden, other_hidden, blocks, other_blocks, capacity):
    rows, units = hidden.shape
    part = blocks.shape[2]
    height = GROUP * capacity
    span = PIECES * height
    groups = rows // height

    def kernel(
        hidden_ref, other_ref, blocks_ref, other_blocks_ref, out_ref, stacked, ready, out_sems
    ):
        order = group_order(0, capacity)
        for piece in range(PIECES):
            total = jnp.dot(hidden_ref[...], blocks_ref[piece], preferred_element_type=jnp.float32)
            total += jnp.dot(
                other_ref[...], other_blocks_ref[piece], preferred_element_type=jnp.float32
            )
            total = total.astype(jnp.bfloat16)
            for group in range(groups):
                at = group * span + piece * height
                stacked[at : at + height, :] = total[group * height : (group + 1) * height]
        copies = []
        for group in range(groups):
            lines = slice(group * span, (group + 1) * span)
            where = pl.ds(group * span, span)
            for number, columns in enumerate(spans(part)):
                ready[lines, columns] = jnp.dot(
                    order, stacked[lines, columns], preferred_element_type=jnp.float32
                ).astype(jnp.bfloat16)
                lanes = pl.ds(columns.start, columns.stop - columns.start)
                copies.append(
                    pltpu.make_async_copy(
                        ready.at[where, lanes], out_ref.at[where, lanes], out_sems.at[group, number]
                    )
                )
                copies[-1].start()
        for copy in copies:
            copy.wait()

    return pl.pallas_call(
        kernel,
        out_shape=pltpu.HBM((rows * PIECES, part), jnp.bfloat16),
        in_specs=[vmem()] * 4,
        out_specs=anywhere(),
        scratch_shapes=[
            pltpu.VMEM((rows * PIECES, part), jnp.bfloat16),
            pltpu.VMEM((rows * PIECES, part), jnp.bfloat16),
            pltpu.SemaphoreType.DMA((groups, len(spans(part)))),
        ],
        compiler_params=params(24),
        cost_estimate=small_cost(),
        name="down_rows",
    )(hidden, other_hidden, blocks, other_blocks)


def other_half(core, down, after, count):
    units, width = down.shape
    half_width = width // 2
    height = units // count

    def kernel(core_ref, down_ref, after_ref, *rest):
        del after_ref
        outs, sems = rest[:-1], rest[-1]
        place = pl.ds(pl.multiple_of((1 - core_ref[0]) * half_width, half_width), half_width)
        copies = [
            pltpu.make_async_copy(
                down_ref.at[pl.ds(number * height, height), place], out, sems.at[number]
            )
            for number, out in enumerate(outs)
        ]
        for copy in copies:
            copy.start()
        for copy in copies:
            copy.wait()

    return pl.pallas_call(
        kernel,
        out_shape=(jax.ShapeDtypeStruct((height, half_width), down.dtype),) * count,
        in_specs=[smem()] + [anywhere()] * 2,
        out_specs=(vmem(),) * count,
        scratch_shapes=[pltpu.SemaphoreType.DMA((count,))],
        compiler_params=params(24),
        cost_estimate=small_cost(),
        name="other_half",
    )(core, in_hbm(down), in_hbm(after))


def combine_first(x, wire, columns, weights, moment, block, experts, capacity):
    count, first = x.shape
    wire_rows = wire.shape[0]

    def kernel(x_ref, wire_ref, column_ref, weight_ref, y_ref, factors, held, sem):
        copy = pltpu.make_async_copy(wire_ref.at[:, pl.ds(0, first)], held, sem.at[0])
        copy.start()
        rows = wire_codes((1, wire_rows), 1, experts, capacity)
        codes, shares = column_ref[0, 0], weight_ref[0, 0]
        codes = jnp.concatenate([codes + piece * (experts * capacity) for piece in range(PIECES)])
        shares = jnp.concatenate([shares] * PIECES)
        table = jnp.where(rows == codes[:, 0:1], shares[:, 0:1], 0.0)
        table += jnp.where(rows == codes[:, 1:2], shares[:, 1:2], 0.0)
        high = table.astype(jnp.bfloat16)
        factors[:count, :] = high
        factors[count:, :] = (table - high.astype(jnp.float32)).astype(jnp.bfloat16)
        copy.wait()
        for lanes in spans(first):
            both = jnp.dot(factors[...], held[:, lanes], preferred_element_type=jnp.float32)
            y_ref[:, lanes] = (
                x_ref[:, lanes].astype(jnp.float32) + both[:count, :] + both[count:, :]
            ).astype(jnp.bfloat16)

    per_block = lambda array: pl.BlockSpec(
        (1, 1) + array.shape[2:], lambda step: (moment, block, 0, 0)
    )
    return pl.pallas_call(
        kernel,
        out_shape=(
            jax.ShapeDtypeStruct((count, first), x.dtype),
            jax.ShapeDtypeStruct((2 * count, wire_rows), jnp.bfloat16),
        ),
        grid=(1,),
        in_specs=[whole(x), anywhere(), per_block(columns), per_block(weights)],
        out_specs=(
            pl.BlockSpec((count, first), lambda step: (0, 0)),
            pl.BlockSpec((2 * count, wire_rows), lambda step: (0, 0)),
        ),
        scratch_shapes=[
            pltpu.VMEM((wire_rows, first), jnp.bfloat16),
            pltpu.SemaphoreType.DMA((1,)),
        ],
        compiler_params=params(24),
        cost_estimate=small_cost(),
        name="combine_first",
    )(in_hbm(x), in_hbm(wire), in_hbm(columns), in_hbm(weights))


def combine_second(x, wire, factors):
    count, second = x.shape
    wire_rows, width = wire.shape

    def kernel(x_ref, wire_ref, factor_ref, y_ref, held, start, sems):
        copies = [
            pltpu.make_async_copy(
                wire_ref.at[:, pl.ds(width - second, second)], held, sems.at[0]
            ),
            pltpu.make_async_copy(x_ref, start, sems.at[1]),
        ]
        for copy in copies:
            copy.start()
        for copy in copies:
            copy.wait()
        for lanes in spans(second):
            both = jnp.dot(factor_ref[...], held[:, lanes], preferred_element_type=jnp.float32)
            y_ref[:, lanes] = (
                start[:, lanes].astype(jnp.float32) + both[:count, :] + both[count:, :]
            ).astype(jnp.bfloat16)

    return pl.pallas_call(
        kernel,
        out_shape=jax.ShapeDtypeStruct((count, second), x.dtype),
        in_specs=[anywhere(), anywhere(), vmem()],
        out_specs=vmem(),
        scratch_shapes=[
            pltpu.VMEM((wire_rows, second), jnp.bfloat16),
            pltpu.VMEM((count, second), x.dtype),
            pltpu.SemaphoreType.DMA((2,)),
        ],
        compiler_params=params(24),
        cost_estimate=small_cost(),
        name="combine_second",
    )(in_hbm(x), in_hbm(wire), factors)


def record(place, ys, states, moment, block, sections):
    count = ys[0].shape[0]
    tokens = count // PIECES
    widths = [y.shape[1] for y in ys]
    part = sum(widths)
    starts = (0, widths[0])

    def kernel(place_ref, first_ref, second_ref, *rest):
        forward_ref, reverse_ref, sent_ref, sems = rest[-4:]
        section, core = place_ref[0], place_ref[1]
        for number, (state_ref, turn) in enumerate(
            ((forward_ref, moment), (reverse_ref, sections - 1 - moment))
        ):

            @pl.when((section == turn) & (core == block))
            def _():
                copies = []
                for which, y_ref in enumerate((first_ref, second_ref)):
                    for piece in range(PIECES):
                        at = (block * PIECES + piece) * part + starts[which]
                        copies.append(
                            pltpu.make_async_copy(
                                y_ref.at[pl.ds(piece * tokens, tokens)],
                                state_ref.at[:, pl.ds(at, widths[which])],
                                sems.at[number, which * PIECES + piece],
                            )
                        )
                for copy in copies:
                    copy.start()
                for copy in copies:
                    copy.wait()

            @pl.when((section == turn) & (core != block))
            def _():
                copies = [
                    pltpu.make_async_copy(
                        y_ref,
                        sent_ref.at[number, :, pl.ds(starts[which], widths[which])],
                        sems.at[number, which],
                    )
                    for which, y_ref in enumerate((first_ref, second_ref))
                ]
                for copy in copies:
                    copy.start()
                for copy in copies:
                    copy.wait()

    result = pltpu.HBM((tokens, 2 * PIECES * part), ys[0].dtype)
    return pl.pallas_call(
        kernel,
        out_shape=(result, result, pltpu.HBM((2, count, part), ys[0].dtype)),
        in_specs=[smem()] + [anywhere()] * (2 + len(states)),
        out_specs=(anywhere(),) * 3,
        input_output_aliases={3 + n: n for n in range(len(states))},
        scratch_shapes=[pltpu.SemaphoreType.DMA((2, 2 * PIECES))],
        cost_estimate=small_cost(),
        name="record",
    )(place, *[in_vmem(y) for y in ys], *[in_hbm(state) for state in states])


def finish(place, states, arrived):
    count, part = arrived.shape[1:]
    tokens = count // PIECES

    def kernel(place_ref, forward_in, reverse_in, arrived_ref, forward_ref, reverse_ref, sems):
        del forward_in, reverse_in
        half = 1 - place_ref[1]
        copies = []
        for number, ref in enumerate((forward_ref, reverse_ref)):
            for piece in range(PIECES):
                at = pl.multiple_of((half * PIECES + piece) * part, part)
                copies.append(
                    pltpu.make_async_copy(
                        arrived_ref.at[number, pl.ds(piece * tokens, tokens)],
                        ref.at[:, pl.ds(at, part)],
                        sems.at[number, piece],
                    )
                )
        for copy in copies:
            copy.start()
        for copy in copies:
            copy.wait()

    return pl.pallas_call(
        kernel,
        out_shape=tuple(pltpu.HBM(state.shape, state.dtype) for state in states),
        in_specs=[smem()] + [anywhere()] * 3,
        out_specs=(anywhere(),) * 2,
        input_output_aliases={1: 0, 2: 1},
        scratch_shapes=[pltpu.SemaphoreType.DMA((2, PIECES))],
        name="finish",
    )(place, *[in_hbm(state) for state in states], in_vmem(arrived))


def split_tokens(place, tokens_a, tokens_b):
    tokens, width = tokens_a.shape
    part = width // 2 // PIECES
    count = PIECES * tokens

    def kernel(place_ref, a_ref, b_ref, kept_ref, leaving_ref, sems):
        section, core = place_ref[0], place_ref[1]

        def move(ref):
            copies = []
            for which, (half, out) in enumerate(((core, kept_ref), (1 - core, leaving_ref))):
                for piece in range(PIECES):
                    at = pl.multiple_of((half * PIECES + piece) * part, part)
                    copies.append(
                        pltpu.make_async_copy(
                            ref.at[:, pl.ds(at, part)],
                            out.at[pl.ds(piece * tokens, tokens)],
                            sems.at[which, piece],
                        )
                    )
            for copy in copies:
                copy.start()
            for copy in copies:
                copy.wait()

        @pl.when(section == 0)
        def _():
            move(a_ref)

        @pl.when(section != 0)
        def _():
            move(b_ref)

    return pl.pallas_call(
        kernel,
        out_shape=(jax.ShapeDtypeStruct((count, part), tokens_a.dtype),) * 2,
        in_specs=[smem(), anywhere(), anywhere()],
        out_specs=(vmem(), vmem()),
        scratch_shapes=[pltpu.SemaphoreType.DMA((2, PIECES))],
        compiler_params=params(16),
        cost_estimate=small_cost(),
        name="split_tokens",
    )(place, in_hbm(tokens_a), in_hbm(tokens_b))


def order_blocks(place, kept, arrived):
    count, part = kept.shape
    columns = parts_of(part)

    def kernel(place_ref, kept_ref, arrived_ref, *outs):
        def put(first_ref, second_ref):
            for block, ref in enumerate((first_ref, second_ref)):
                for number, lanes in enumerate(columns):
                    outs[2 * block + number][...] = ref[:, lanes]

        @pl.when(place_ref[1] == 0)
        def _():
            put(kept_ref, arrived_ref)

        @pl.when(place_ref[1] != 0)
        def _():
            put(arrived_ref, kept_ref)

    shapes = tuple(
        jax.ShapeDtypeStruct((count, lanes.stop - lanes.start), kept.dtype) for lanes in columns
    )
    outs = pl.pallas_call(
        kernel,
        out_shape=shapes * 2,
        in_specs=[smem(), vmem(), vmem()],
        out_specs=(vmem(),) * 4,
        compiler_params=params(16),
        cost_estimate=small_cost(),
        name="order_blocks",
    )(place, kept, arrived)
    return [list(outs[:2]), list(outs[2:])]


def join_rows(blocks):
    height, width = blocks[0].shape
    count = len(blocks)

    def kernel(*refs):
        sources, (out_ref, held, in_sems, out_sems) = refs[:count], refs[count:]
        arriving, leaving = [], []
        for number, ref in enumerate(sources):
            lines = pl.ds(number * height, height)
            arriving.append(pltpu.make_async_copy(ref, held.at[lines], in_sems.at[number]))
            leaving.append(
                pltpu.make_async_copy(held.at[lines], out_ref.at[lines], out_sems.at[number])
            )
        for copy in arriving:
            copy.start()
        for first, second in zip(arriving, leaving):
            first.wait()
            second.start()
        for copy in leaving:
            copy.wait()

    return pl.pallas_call(
        kernel,
        out_shape=pltpu.HBM((height * count, width), blocks[0].dtype),
        in_specs=[anywhere()] * count,
        out_specs=anywhere(),
        scratch_shapes=[
            pltpu.VMEM((height * count, width), blocks[0].dtype),
            pltpu.SemaphoreType.DMA((count,)),
            pltpu.SemaphoreType.DMA((count,)),
        ],
        compiler_params=params(16),
        cost_estimate=small_cost(),
        name="join_rows",
    )(*blocks)


def slots(routes, experts, capacity):
    flat = routes.reshape(routes.shape[:-2] + (-1,))
    order = jnp.arange(flat.shape[-1], dtype=jnp.int32)
    earlier = (flat[..., :, None] == flat[..., None, :]) & (order[None, :] < order[:, None])
    slot = flat * capacity + jnp.sum(earlier.astype(jnp.int32), axis=-1)
    return slot.reshape(routes.shape)


def shards(tokens_a, tokens_b, routes_a, routes_b, affinity_a, affinity_b, gate_w, up_w, down_w):
    sections = lax.axis_size("pp")
    devices = lax.axis_size("ep")
    experts = devices // 2
    token_count, width = tokens_a.shape
    half_width = width // 2
    capacity = 2 * (token_count * routes_a.shape[2] // devices) + 2
    section = lax.axis_index("pp")
    core = (lax.axis_index("ep") % 2).astype(jnp.int32)
    low = core == 0
    place = jnp.stack([section.astype(jnp.int32), core])
    own_half = core.reshape(1)
    gate, up, down = gate_w[0], up_w[0], down_w[0]

    one_core = [[2 * chip + side for chip in range(experts)] for side in range(2)]
    siblings = [(device, device ^ 1) for device in range(devices)]

    def exchange(wire):
        blocks = wire.reshape(experts, PIECES * capacity, wire.shape[1])
        moved = lax.all_to_all(
            blocks, "ep", split_axis=0, concat_axis=0, tiled=True, axis_index_groups=one_core
        )
        return moved.reshape(wire.shape)

    def to_sibling(block):
        return lax.ppermute(block, "ep", siblings)

    def by_block(mine, theirs):
        return jnp.where(low, mine, theirs), jnp.where(low, theirs, mine)

    def by_moment(pair):
        return jnp.stack([jnp.where(section == m, pair[0], pair[1]) for m in range(sections)])

    target = slots(jnp.stack([routes_a[0], routes_b[0]]), experts, capacity)
    target = by_moment(target)
    affinity = by_moment(jnp.stack([affinity_a[0], affinity_b[0]]))
    target = jnp.stack(by_block(target, to_sibling(target)), axis=1)
    affinity = jnp.stack(by_block(affinity, to_sibling(affinity)), axis=1)
    shift = jnp.arange(PIECES, dtype=jnp.int32)[:, None] * (experts * capacity)
    lines = target.swapaxes(2, 3)
    lines = (lines[:, :, :, None] + shift).reshape(lines.shape[:3] + (PIECES * token_count,))

    kept, leaving = split_tokens(place, tokens_a, tokens_b)
    part = kept.shape[1]
    chunks = order_blocks(place, kept, to_sibling(leaving))

    def leave(i, moment, after=()):
        first, select = dispatch_first(
            chunks[i][0], lines, part, moment, i, experts, capacity, after
        )
        return dispatch_second(chunks[i][1], select, first)

    def experts_of(wire):
        middle = wire.shape[0] // 2
        others = [to_sibling(wire[:middle]), to_sibling(wire[middle:])]
        own_gate, own_up = load_half(own_half, gate, up, wire, wire.shape[1])
        hidden, *blocks = hidden_units(
            own_half, wire, others, own_gate, own_up, gate, up, down, other_down, capacity
        )
        return down_rows(hidden, to_sibling(hidden), *blocks, capacity)

    states = ()
    first_leaving = leave(0, 0)
    first_wire = exchange(first_leaving)
    other_down = [to_sibling(block) for block in other_half(own_half, down, first_leaving, 8)]
    second_leaving, target, affinity, other_down = tie(
        (leave(1, 0), target, affinity, join_rows(other_down)), first_wire
    )
    for moment in range(sections):
        last = sections - 1 - moment
        hop = [(moment, moment + 1), (last, last - 1)]

        def settle(i, back):
            y, factors = combine_first(
                chunks[i][0], back, target, affinity, moment, i, experts, capacity
            )
            ys = [y, combine_second(chunks[i][1], back, factors)]
            after = record(place, ys, states, moment, i, sections)
            if moment + 1 == sections:
                return after, None
            chunks[i] = [lax.ppermute(y, "pp", hop) for y in ys]
            return after, leave(i, moment + 1, after[2:])

        second_wire = exchange(second_leaving)
        first_rows = experts_of(first_wire)
        (first_rows,) = tie((first_rows,), second_wire)
        first_back = exchange(first_rows)
        second_rows = experts_of(second_wire)
        (second_rows,) = tie((second_rows,), first_back)
        second_back = exchange(second_rows)
        states, first_leaving = settle(0, first_back)
        if moment + 1 < sections:
            (first_leaving,) = tie((first_leaving,), second_back)
            first_wire = exchange(first_leaving)
        states, second_leaving = settle(1, second_back)
        if moment + 1 < sections:
            (second_leaving,) = tie((second_leaving,), first_wire)
    forward, reverse, sent = states
    forward, reverse = finish(place, (forward, reverse), to_sibling(sent))
    return (forward[None], reverse[None])


def solution(mesh):
    placed = (
        P("ep", None),
        P("ep", None),
        P("pp", "ep", None),
        P("pp", "ep", None),
        P("pp", "ep", None),
        P("pp", "ep", None),
        P("pp", None, "ep"),
        P("pp", None, "ep"),
        P("pp", "ep", None),
    )
    return jax.shard_map(
        shards,
        mesh=mesh,
        in_specs=placed,
        out_specs=(P("pp", "ep", None), P("pp", "ep", None)),
        check_vma=False,
    )
```
